32 devices in a mesh: section: 2 (over y), dp: 16 (over z, x, core).
Axes of the slice: x: 2, y: 2, z: 4, core: 2. Of those that a mesh axis runs over, the one named last changes fastest.
Arguments:
- tokens: bfloat16 [64, 64, 768], P('dp'), may hold values from -6 to 6
- images: bfloat16 [64, 256, 768], P('dp', 'section'), may hold values from -6 to 6
- lengths: int32 [64], P('dp'), may hold values from 5 to 64, as said below
- cotangent: bfloat16 [2, 64, 64, 768], P('section', 'dp'), may hold values from -6 to 6
- attend_gain: float32 [2, 768], P('section'), may hold values from 0.5 to 1.5
- attend_shift: float32 [2, 768], P('section'), may hold values from -2 to 2
- projections: bfloat16 [2, 768, 2304], P('section'), may hold values from -0.21875 to 0.21875
- query_bias: float32 [2, 768], P('section'), may hold values from -3 to 3
- value_bias: float32 [2, 768], P('section'), may hold values from -2 to 2
- output_weight: bfloat16 [2, 768, 768], P('section'), may hold values from -0.625 to 0.625
- output_bias: float32 [2, 768], P('section'), may hold values from -2 to 2
- feed_gain: float32 [2, 768], P('section'), may hold values from 0.5 to 1.5
- feed_shift: float32 [2, 768], P('section'), may hold values from -2 to 2
- expand_weight: bfloat16 [2, 768, 3072], P('section'), may hold values from -0.21875 to 0.21875
- expand_bias: float32 [2, 3072], P('section'), may hold values from -3 to 3
- reduce_weight: bfloat16 [2, 3072, 768], P('section'), may hold values from -0.21875 to 0.21875
- reduce_bias: float32 [2, 768], P('section'), may hold values from -2 to 2
- cross_gain: float32 [768], replicated, may hold values from 0.5 to 1.5
- cross_shift: float32 [768], replicated, may hold values from -2 to 2
- cross_query: bfloat16 [768, 768], replicated, may hold values from -0.21875 to 0.21875
- cross_query_bias: float32 [768], replicated, may hold values from -3 to 3
- cross_key: bfloat16 [768, 768], replicated, may hold values from -0.21875 to 0.21875
- cross_value: bfloat16 [768, 768], replicated, may hold values from -0.21875 to 0.21875
- cross_value_bias: float32 [768], replicated, may hold values from -2 to 2
- cross_out: bfloat16 [768, 768], replicated, may hold values from -1.25 to 1.25
- cross_out_bias: float32 [768], replicated, may hold values from -2 to 2
Outputs:
- layer_outputs: bfloat16 [2, 64, 64, 768], P('section', 'dp')
- input_gradient: float32 [2, 64, 64, 768], P('section', 'dp')
- image_gradient: float32 [64, 256, 768], P('dp', 'section')
- attend_gain_gradient: float32 [2, 768], P('section', 'dp')
- attend_shift_gradient: float32 [2, 768], P('section', 'dp')
- projections_gradient: float32 [2, 768, 2304], P('section', 'dp')
- query_bias_gradient: float32 [2, 768], P('section', 'dp')
- value_bias_gradient: float32 [2, 768], P('section', 'dp')
- output_weight_gradient: float32 [2, 768, 768], P('section', 'dp')
- output_bias_gradient: float32 [2, 768], P('section', 'dp')
- feed_gain_gradient: float32 [2, 768], P('section', 'dp')
- feed_shift_gradient: float32 [2, 768], P('section', 'dp')
- expand_weight_gradient: float32 [2, 768, 3072], P('section', 'dp')
- expand_bias_gradient: float32 [2, 3072], P('section', 'dp')
- reduce_weight_gradient: float32 [2, 3072, 768], P('section', 'dp')
- reduce_bias_gradient: float32 [2, 768], P('section', 'dp')
- cross_gain_gradient: float32 [768], P('dp')
- cross_shift_gradient: float32 [768], P('dp')
- cross_query_gradient: float32 [768, 768], P('dp')
- cross_query_bias_gradient: float32 [768], P('dp')
- cross_key_gradient: float32 [768, 768], P('dp')
- cross_value_gradient: float32 [768, 768], P('dp')
- cross_value_bias_gradient: float32 [768], P('dp')
- cross_out_gradient: float32 [768, 768], P('dp')
- cross_out_bias_gradient: float32 [768], P('dp')
The draws below stay inside these ranges and needn't reach their ends.
Inputs may be any that keep to these rules, and one draw needn't show every extreme that they name: `lengths`: some caption uses all 64 slots and some caption uses 5.
All inputs are finite; a program needn't handle non-finite values.
Results may differ from the reference program's by a relative error of at most 0.023.
Values may be sent and summed in bfloat16 or wider, within the bound.
A program may use at most 320 MiB of HBM per device.

```python
import jax
import jax.numpy as jnp
from jax import lax

D = 768
HEADS = 12
HEAD_DIM = 64
FF = 3072
SLOTS = 64
IMG = 256
CAP_DEV = 4
CAPTIONS = 64


def draw_lengths(key, part):
    key = jax.random.fold_in(key, 7)
    base, first = jax.random.split(key, 2)
    values = jax.random.randint(base, (CAPTIONS,), 5, SLOTS + 1)
    spot = jax.random.randint(first, (), 0, CAPTIONS // 2)
    values = values.at[spot].set(SLOTS)
    values = values.at[spot + CAPTIONS // 2].set(5)
    return values.astype(jnp.int32)


def block_scale(stream_key, dims, pieces, least, high):
    def one(position, blocks):
        draws = jax.random.uniform(jax.random.fold_in(jax.random.fold_in(stream_key, 6), position), (blocks,), jnp.float32, least / len(pieces), high / len(pieces))
        return jnp.repeat(jnp.exp(draws), dims[position] // blocks).reshape((-1,) + (1,) * (len(dims) - position - 1))

    level = one(*pieces[0])
    for cut in pieces[1:]:
        level = level * one(*cut)
    return level


def noise(rng, extent, scale, reach, cuts=(), held_as=jnp.bfloat16):
    level = block_scale(rng, extent, cuts, -0.22, 0.18) if cuts else 1.0
    values = jax.random.normal(rng, extent, jnp.float32) * scale * level
    return jnp.minimum(jnp.maximum(values, -reach), reach).astype(held_as)


def setup_inputs(seed: int = 0) -> dict:
    key_of = jax.random.split(jax.random.key(seed), 27)
    tokens = noise(key_of[0], (CAPTIONS, SLOTS, D), 1.0, 6.0, ((0, 16),))
    images = noise(key_of[1], (CAPTIONS, IMG, D), 1.0, 6.0, ((0, 16), (1, 2)))
    lengths = draw_lengths(jax.random.fold_in(key_of[26], 71), 0)
    cotangent = noise(key_of[3], (2, CAPTIONS, SLOTS, D), 1.0, 6.0, ((0, 2), (1, 16)))
    attend_gain = jnp.clip(1.0 + 0.1 * jax.random.normal(key_of[4], (2, D), jnp.float32), 0.5, 1.5)
    attend_shift = noise(key_of[5], (2, D), 0.3, 2.0, ((0, 2),), jnp.float32)
    projections = noise(key_of[6], (2, D, 3 * D), D ** -0.5, 0.21875, ((0, 2),))
    query_bias = noise(key_of[7], (2, D), 0.5, 3.0, ((0, 2),), jnp.float32)
    value_bias = noise(key_of[8], (2, D), 0.3, 2.0, ((0, 2),), jnp.float32)
    output_weight = noise(key_of[9], (2, D, D), (D // 8) ** -0.5, 0.625, ((0, 2),))
    output_bias = noise(key_of[10], (2, D), 0.3, 2.0, ((0, 2),), jnp.float32)
    feed_gain = jnp.clip(1.0 + 0.1 * jax.random.normal(key_of[11], (2, D), jnp.float32), 0.5, 1.5)
    feed_shift = noise(key_of[12], (2, D), 0.3, 2.0, ((0, 2),), jnp.float32)
    expand_weight = noise(key_of[13], (2, D, FF), D ** -0.5, 0.21875, ((0, 2),))
    expand_bias = noise(key_of[14], (2, FF), 0.5, 3.0, ((0, 2),), jnp.float32)
    reduce_weight = noise(key_of[15], (2, FF, D), (FF // 4) ** -0.5, 0.21875, ((0, 2),))
    reduce_bias = noise(key_of[16], (2, D), 0.3, 2.0, ((0, 2),), jnp.float32)
    cross_gain = jnp.clip(1.0 + 0.1 * jax.random.normal(key_of[17], (D,), jnp.float32), 0.5, 1.5)
    cross_shift = noise(key_of[18], (D,), 0.3, 2.0, (), jnp.float32)
    cross_query = noise(key_of[19], (D, D), D ** -0.5, 0.21875)
    cross_query_bias = noise(key_of[20], (D,), 0.5, 3.0, (), jnp.float32)
    cross_key = noise(key_of[21], (D, D), D ** -0.5, 0.21875)
    cross_value = noise(key_of[22], (D, D), D ** -0.5, 0.21875)
    cross_value_bias = noise(key_of[23], (D,), 0.3, 2.0, (), jnp.float32)
    cross_out = noise(key_of[24], (D, D), (D // 32) ** -0.5, 1.25)
    cross_out_bias = noise(key_of[25], (D,), 0.3, 2.0, (), jnp.float32)
    return dict(tokens=tokens, images=images, lengths=lengths, cotangent=cotangent, attend_gain=attend_gain, attend_shift=attend_shift, projections=projections, query_bias=query_bias, value_bias=value_bias, output_weight=output_weight, output_bias=output_bias, feed_gain=feed_gain, feed_shift=feed_shift, expand_weight=expand_weight, expand_bias=expand_bias, reduce_weight=reduce_weight, reduce_bias=reduce_bias, cross_gain=cross_gain, cross_shift=cross_shift, cross_query=cross_query, cross_query_bias=cross_query_bias, cross_key=cross_key, cross_value=cross_value, cross_value_bias=cross_value_bias, cross_out=cross_out, cross_out_bias=cross_out_bias)


EPS = 1e-05
NEG = -1000000000.0
HIGH = lax.Precision.HIGHEST

@jax.custom_vjp
def low(v):
    return lax.optimization_barrier(v.astype(jnp.bfloat16)).astype(jnp.float32)

@jax.custom_vjp
def low_back(v):
    return v

def low_keep(v):
    return (low(v), None)

def low_pass(kept, grad):
    return (grad,)

def back_keep(v):
    return (v, None)

def back_low(kept, grad):
    return (low(grad),)
low.defvjp(low_keep, low_pass)
low_back.defvjp(back_keep, back_low)

def layer_norm(rows, gain, shift):
    mean = lax.optimization_barrier(jnp.mean(rows, -1, keepdims=True))
    centred = rows - mean
    inverse = lax.rsqrt(lax.optimization_barrier(jnp.mean(centred * centred, -1, keepdims=True)) + EPS)
    return centred * inverse * gain + shift

def product(rows, weight):
    return jnp.einsum('bsi,ij->bsj', rows, weight, precision=HIGH)

def attend(query, keys, values, mask):
    batch, length, width = query.shape
    query_heads = query.reshape(batch, length, HEADS, HEAD_DIM)
    key_heads = keys.reshape(batch, keys.shape[1], HEADS, HEAD_DIM)
    value_heads = values.reshape(batch, values.shape[1], HEADS, HEAD_DIM)
    scores = low_back(jnp.einsum('bqhd,bkhd->bhqk', query_heads, key_heads, precision=HIGH) * HEAD_DIM ** (-0.5))
    if mask is not None:
        scores = jnp.where(mask[:, None], scores, NEG)
    top = lax.optimization_barrier(jnp.max(scores, -1, keepdims=True))
    expo = jnp.exp(scores - top)
    probs = expo / lax.optimization_barrier(jnp.sum(expo, -1, keepdims=True))
    mixed = jnp.einsum('bhqk,bkhd->bqhd', low(probs), value_heads, precision=HIGH)
    return low_back(low(mixed.reshape(batch, length, width)))

def self_block(hidden, layer, mask):
    entry = low(layer_norm(hidden, layer[0], layer[1]))
    packed = product(entry, layer[2])
    query = low_back(low(packed[..., :D] + layer[3]))
    keys = low_back(low(packed[..., D:2 * D]))
    values = low_back(low(packed[..., 2 * D:] + layer[4]))
    mixed = attend(query, keys, values, mask)
    return hidden + low_back(product(mixed, layer[5]) + layer[6])

def cross_block(hidden, image_rows, cross):
    entry = low(layer_norm(hidden, cross[0], cross[1]))
    query = low_back(low(product(entry, cross[2]) + cross[3]))
    keys = low_back(low(product(image_rows, cross[4])))
    values = low_back(low(product(image_rows, cross[5]) + cross[6]))
    mixed = attend(query, keys, values, None)
    return hidden + low_back(product(mixed, cross[7]) + cross[8])

def feed_block(hidden, layer):
    entry = low(layer_norm(hidden, layer[7], layer[8]))
    expanded = low_back(product(entry, layer[9]) + layer[10])
    active = low(jax.nn.gelu(expanded, approximate=False))
    return hidden + low_back(product(active, layer[11]) + layer[12])

def forward(shared, cross, group_tokens, group_images, lift, mask):
    first_layer = tuple((weight[0] for weight in shared))
    second_layer = tuple((weight[1] for weight in shared))
    out_one = feed_block(self_block(group_tokens, first_layer, mask), first_layer)
    entering = low_back(low(out_one) + lift)
    middle = cross_block(self_block(entering, second_layer, mask), group_images, cross)
    out_two = feed_block(middle, second_layer)
    return (out_one, out_two)

def reference(tokens, images, lengths, cotangent, attend_gain, attend_shift, projections, query_bias, value_bias, output_weight, output_bias, feed_gain, feed_shift, expand_weight, expand_bias, reduce_weight, reduce_bias, cross_gain, cross_shift, cross_query, cross_query_bias, cross_key, cross_value, cross_value_bias, cross_out, cross_out_bias):
    shared = tuple((weight.astype(jnp.float32) for weight in (attend_gain, attend_shift, projections, query_bias, value_bias, output_weight, output_bias, feed_gain, feed_shift, expand_weight, expand_bias, reduce_weight, reduce_bias)))
    cross = tuple((weight.astype(jnp.float32) for weight in (cross_gain, cross_shift, cross_query, cross_query_bias, cross_key, cross_value, cross_value_bias, cross_out, cross_out_bias)))
    groups = CAPTIONS // CAP_DEV

    def split_groups(array):
        return array.reshape((groups, CAP_DEV) + array.shape[1:])
    cotangents = cotangent.astype(jnp.float32)
    items = (split_groups(tokens.astype(jnp.float32)), split_groups(images.astype(jnp.float32)), split_groups(lengths.astype(jnp.int32)), split_groups(cotangents[0]), split_groups(cotangents[1]))
    positions = jnp.arange(SLOTS, dtype=jnp.int32)
    causal = positions[None, :] <= positions[:, None]

    def group_step(totals, item):
        group_tokens, group_images, group_lengths, first_cot, second_cot = item
        live = positions[None, :] < group_lengths[:, None]
        allowed = live[:, None, :] & causal[None]
        row_weight = live[..., None].astype(jnp.float32)
        lift = jnp.zeros(group_tokens.shape, jnp.float32)

        def run(shared_weights, cross_weights, token_rows, image_rows, lifted):
            return forward(shared_weights, cross_weights, token_rows, image_rows, lifted, allowed)
        outputs, pullback = jax.vjp(run, shared, cross, group_tokens, group_images, lift)
        grads = pullback((first_cot * row_weight, second_cot * row_weight))
        totals = jax.tree.map(jnp.add, totals, (grads[0], grads[1]))
        return (totals, (outputs[0].astype(jnp.bfloat16), outputs[1].astype(jnp.bfloat16), grads[2], grads[4], grads[3]))
    start = (tuple((jnp.zeros(weight.shape, jnp.float32) for weight in shared)), tuple((jnp.zeros(weight.shape, jnp.float32) for weight in cross)))
    totals, stacked = lax.scan(group_step, start, items)

    def merge_groups(array):
        return array.reshape((CAPTIONS,) + array.shape[2:])
    layer_outputs = jnp.stack([merge_groups(stacked[0]), merge_groups(stacked[1])])
    input_gradient = jnp.stack([merge_groups(stacked[2]), merge_groups(stacked[3])])
    image_gradient = merge_groups(stacked[4])
    shared_grads, cross_grads = totals
    return (layer_outputs, input_gradient, image_gradient, shared_grads[0], shared_grads[1], shared_grads[2], shared_grads[3], shared_grads[4], shared_grads[5], shared_grads[6], shared_grads[7], shared_grads[8], shared_grads[9], shared_grads[10], shared_grads[11], shared_grads[12], cross_grads[0], cross_grads[1], cross_grads[2], cross_grads[3], cross_grads[4], cross_grads[5], cross_grads[6], cross_grads[7], cross_grads[8])
```

```python
import jax
import jax.numpy as jnp
from jax import lax
from jax.experimental import pallas as pl
from jax.experimental.pallas import tpu as pltpu
from jax.sharding import PartitionSpec as P

HEADS = 12
HEAD_DIM = 64
MB_CAPS = 4
MICRO = 1
ROWS = 48
CHUNKS = 16
SHARED_CHUNKS = 12
VECTORS = 24


EPS = 1e-05
NEG = -1000000000.0


def shifted(block, axis, distance):
    devices = range(lax.axis_size(axis))
    route = [(i - distance, i) for i in devices if i - distance in devices]
    return lax.ppermute(block, axis, route)


def for_sending(array):
    return jax.tree.map(lambda a: a.astype(jnp.bfloat16) if a.dtype == jnp.float32 else a, array)


def layer_norm(rows, gain, shift):
    mean = jnp.mean(rows, -1, keepdims=True)
    centred = rows - mean
    inverse = lax.rsqrt(jnp.mean(centred * centred, -1, keepdims=True) + EPS)
    normed = centred * inverse
    return (normed * gain + shift, normed, inverse)


def norm_back(grad, normed, inverse, gain):
    scaled = grad * gain
    inner = (
        scaled
        - jnp.mean(scaled, -1, keepdims=True)
        - normed * jnp.mean(scaled * normed, -1, keepdims=True)
    )
    return (inverse * inner, jnp.sum(grad * normed, axis=(0, 1)), jnp.sum(grad, axis=(0, 1)))


def product(rows, weight):
    return jnp.einsum("bsi,ij->bsj", rows, weight, preferred_element_type=jnp.float32)


def back_product(grad, weight):
    return jnp.einsum("bsj,ij->bsi", grad, weight, preferred_element_type=jnp.float32)


def weight_product(rows, grad):
    return jnp.einsum("bsi,bsj->ij", rows, grad, preferred_element_type=jnp.float32)


def column_sum(grad):
    return jnp.sum(grad.astype(jnp.float32), axis=(0, 1))


def split_heads(rows):
    return rows.reshape(rows.shape[0], rows.shape[1], HEADS, HEAD_DIM)


def scores_of(query, keys, mask):
    scores = jnp.einsum(
        "bqhd,bkhd->bhqk", split_heads(query), split_heads(keys), preferred_element_type=jnp.float32
    ) * HEAD_DIM ** (-0.5)
    if mask is None:
        return scores
    return jnp.where(mask[:, None], scores, NEG)


def attend(query, keys, values, mask):
    scores = scores_of(query, keys, mask)
    top = jnp.max(scores, -1, keepdims=True)
    expo = jnp.exp(scores - top)
    total = jnp.sum(expo, -1, keepdims=True)
    probs = (expo / total).astype(jnp.bfloat16)
    mixed = jnp.einsum(
        "bhqk,bkhd->bqhd", probs, split_heads(values), preferred_element_type=jnp.float32
    )
    return (mixed.reshape(query.shape).astype(jnp.bfloat16), top + jnp.log(total))


def attend_back(grad, query, keys, values, logsum, mask):
    scale = HEAD_DIM ** (-0.5)
    probs = jnp.exp(scores_of(query, keys, mask) - logsum)
    grad_heads = split_heads(grad)
    dprobs = jnp.einsum(
        "bqhd,bkhd->bhqk", grad_heads, split_heads(values), preferred_element_type=jnp.float32
    )
    rowdot = jnp.sum(probs * dprobs, -1, keepdims=True)
    dscores = (probs * (dprobs - rowdot)).astype(jnp.bfloat16)
    dquery = (
        jnp.einsum(
            "bhqk,bkhd->bqhd", dscores, split_heads(keys), preferred_element_type=jnp.float32
        )
        * scale
    )
    dkeys = (
        jnp.einsum(
            "bhqk,bqhd->bkhd", dscores, split_heads(query), preferred_element_type=jnp.float32
        )
        * scale
    )
    dvalues = jnp.einsum(
        "bhqk,bqhd->bkhd",
        probs.astype(jnp.bfloat16),
        grad_heads,
        preferred_element_type=jnp.float32,
    )
    return (
        dquery.reshape(query.shape).astype(jnp.bfloat16),
        dkeys.reshape(keys.shape).astype(jnp.bfloat16),
        dvalues.reshape(values.shape).astype(jnp.bfloat16),
    )


def self_forward(hidden, layer, mask):
    normal, normed, inverse = layer_norm(hidden, layer[0], layer[1])
    entry = normal.astype(jnp.bfloat16)
    packed = product(entry, layer[2])
    width = hidden.shape[-1]
    query = (packed[..., :width] + layer[3]).astype(jnp.bfloat16)
    keys = packed[..., width : 2 * width].astype(jnp.bfloat16)
    values = (packed[..., 2 * width :] + layer[4]).astype(jnp.bfloat16)
    mixed, logsum = attend(query, keys, values, mask)
    after = hidden + (product(mixed, layer[5]) + layer[6])
    return (after, (normed, inverse, entry, query, keys, values, mixed, logsum))


def self_back(grad, saved, layer, mask):
    normed, inverse, entry, query, keys, values, mixed, logsum = saved
    branch = grad.astype(jnp.bfloat16)
    out_weight_grad = weight_product(mixed, branch)
    out_bias_grad = column_sum(branch)
    dmixed = back_product(branch, layer[5]).astype(jnp.bfloat16)
    dquery, dkeys, dvalues = attend_back(dmixed, query, keys, values, logsum, mask)
    dpacked = jnp.concatenate([dquery, dkeys, dvalues], -1)
    packed_grad = weight_product(entry, dpacked)
    dentry = back_product(dpacked, layer[2])
    dhidden, gain_grad, shift_grad = norm_back(dentry, normed, inverse, layer[0])
    return (
        grad + dhidden,
        (
            gain_grad,
            shift_grad,
            packed_grad,
            column_sum(dquery),
            column_sum(dvalues),
            out_weight_grad,
            out_bias_grad,
        ),
    )


def gelu_slope(expanded):
    normal_cdf = 0.5 * (1.0 + jax.scipy.special.erf(expanded * 0.7071067811865476))
    return normal_cdf + expanded * jnp.exp(-0.5 * expanded * expanded) * 0.3989422804014327


def feed_forward(hidden, layer):
    normal, normed, inverse = layer_norm(hidden, layer[7], layer[8])
    entry = normal.astype(jnp.bfloat16)
    expanded = product(entry, layer[9]) + layer[10]
    active = jax.nn.gelu(expanded, approximate=False).astype(jnp.bfloat16)
    after = hidden + (product(active, layer[11]) + layer[12])
    return (after, (normed, inverse, entry, expanded, active))


def feed_back(grad, saved, layer):
    normed, inverse, entry, expanded, active = saved
    branch = grad.astype(jnp.bfloat16)
    reduce_grad = weight_product(active, branch)
    reduce_bias_grad = column_sum(branch)
    dactive = back_product(branch, layer[11])
    dexpanded = (dactive * gelu_slope(expanded)).astype(jnp.bfloat16)
    expand_grad = weight_product(entry, dexpanded)
    expand_bias_grad = column_sum(dexpanded)
    dentry = back_product(dexpanded, layer[9])
    dhidden, gain_grad, shift_grad = norm_back(dentry, normed, inverse, layer[7])
    return (
        grad + dhidden,
        (gain_grad, shift_grad, expand_grad, expand_bias_grad, reduce_grad, reduce_bias_grad),
    )


def cross_forward(hidden, pairs, cross):
    normal, normed, inverse = layer_norm(hidden, cross[0], cross[1])
    entry = normal.astype(jnp.bfloat16)
    query = (product(entry, cross[2]) + cross[3]).astype(jnp.bfloat16)
    width = hidden.shape[-1]
    mixed, logsum = attend(query, pairs[..., :width], pairs[..., width:], None)
    after = hidden + (product(mixed, cross[7]) + cross[8])
    return (after, (normed, inverse, entry, query, mixed, logsum))


def cross_back(grad, saved, pairs, cross):
    normed, inverse, entry, query, mixed, logsum = saved
    width = grad.shape[-1]
    branch = grad.astype(jnp.bfloat16)
    out_grad = weight_product(mixed, branch)
    out_bias_grad = column_sum(branch)
    dmixed = back_product(branch, cross[7]).astype(jnp.bfloat16)
    dquery, dkeys, dvalues = attend_back(
        dmixed, query, pairs[..., :width], pairs[..., width:], logsum, None
    )
    query_grad = weight_product(entry, dquery)
    dentry = back_product(dquery, cross[2])
    dhidden, gain_grad, shift_grad = norm_back(dentry, normed, inverse, cross[0])
    parts = (gain_grad, shift_grad, query_grad, column_sum(dquery), out_grad, out_bias_grad)
    return (grad + dhidden, parts, jnp.concatenate([dkeys, dvalues], -1))


def select_bit(rank, axes, bit, value):
    return tuple(value if axis == bit else slice(None) for axis in axes)


def add_blocks(into, term, count):
    lead = into.shape[:-2]

    def place(i):
        where = []
        for size in reversed(lead):
            where.append(lax.rem(i, size))
            i = lax.div(i, size)
        return tuple(reversed(where))

    if not lead:
        into[...] = into[...] + term[...]
        return

    @pl.loop(0, count)
    def _(i):
        into[place(i)] = into[place(i)] + term[place(i)]


def scatter_kernel(blocks, vectors, shards, totals, grads, *scratch):
    halves = scratch[:4]
    landed, load_sem, send_sem, recv_sem, vsend_sem, vrecv_sem = scratch[4:]
    section = lax.axis_index("section")
    dp = lax.axis_index("dp")
    bits = [lax.rem(lax.div(dp, 1 << k), 2) for k in range(4)]
    partners = [dp + (1 << k) * (1 - 2 * bits[k]) for k in range(4)]
    count = jnp.where(section == 1, CHUNKS, SHARED_CHUNKS)

    barrier = pltpu.get_barrier_semaphore()
    for partner in partners:
        pl.semaphore_signal(
            barrier, inc=1, device_id={"dp": partner}, device_id_type=pl.DeviceIdType.MESH
        )
    pl.semaphore_wait(barrier, 4)

    def step(chunk, k):
        axes = tuple(range(3, k - 1, -1))
        source = (grads if k == 0 else halves[k - 1]).at[chunk]
        send = source.at[select_bit(4, axes, k, 1 - bits[k])]
        keep = source.at[select_bit(4, axes, k, bits[k])]
        into = halves[k].at[chunk]
        copy = pltpu.make_async_remote_copy(
            src_ref=send,
            dst_ref=into,
            send_sem=send_sem.at[chunk, k],
            recv_sem=recv_sem.at[chunk, k],
            device_id={"dp": partners[k]},
            device_id_type=pl.DeviceIdType.MESH,
        )
        return copy, into, keep

    def load(chunk):
        return pltpu.make_async_copy(blocks.at[chunk], grads.at[chunk], load_sem.at[chunk])

    @pl.loop(0, count)
    def _(chunk):
        load(chunk).start()

    @pl.loop(0, count)
    def _(chunk):
        load(chunk).wait()
        step(chunk, 0)[0].start()

    totals[...] = vectors[...]
    for k in range(4):
        copy = pltpu.make_async_remote_copy(
            src_ref=totals,
            dst_ref=landed.at[k],
            send_sem=vsend_sem.at[k],
            recv_sem=vrecv_sem.at[k],
            device_id={"dp": partners[k]},
            device_id_type=pl.DeviceIdType.MESH,
        )
        copy.start()
        copy.wait()
        totals[...] = totals[...] + landed[k]

    @pl.loop(0, count + 3)
    def _(tick):
        for k in range(4):
            chunk = tick - k

            @pl.when((chunk >= 0) & (chunk < count))
            def _():
                copy, into, keep = step(chunk, k)
                copy.wait()
                add_blocks(into, keep, 8 >> k)
                if k < 3:
                    step(chunk, k + 1)[0].start()
                else:
                    shards[chunk] = into[...]


def scatter(blocks, vectors):
    lead = (2, 2, 2, 2)
    tail = blocks.shape[2:]
    blocks = blocks.reshape((CHUNKS,) + lead + tail)
    buffers = [pltpu.VMEM((CHUNKS,) + lead[k:] + tail, jnp.bfloat16) for k in range(5)]
    return pl.pallas_call(
        scatter_kernel,
        out_shape=(
            jax.ShapeDtypeStruct((CHUNKS,) + tail, jnp.bfloat16),
            jax.ShapeDtypeStruct(vectors.shape, jnp.float32),
        ),
        in_specs=[pl.BlockSpec(memory_space=pl.ANY), pl.BlockSpec(memory_space=pltpu.VMEM)],
        out_specs=[pl.BlockSpec(memory_space=pltpu.VMEM)] * 2,
        scratch_shapes=buffers
        + [pltpu.VMEM((4,) + vectors.shape, jnp.float32)]
        + [pltpu.SemaphoreType.DMA((CHUNKS,))]
        + [pltpu.SemaphoreType.DMA((CHUNKS, 4))] * 2
        + [pltpu.SemaphoreType.DMA((4,))] * 2,
        compiler_params=pltpu.CompilerParams(
            collective_id=0, has_side_effects=True, vmem_limit_bytes=60 * 2**20
        ),
        name="scatter",
    )(blocks, vectors)


def reduce_fast(layer_sums, cross_sums, section_index):
    gain, shift, packed, query_b, value_b, out_w, out_b, fgain, fshift, exp_w, exp_b, red_w, red_b = layer_sums
    cgain, cshift, cquery, cquery_b, ckey, cvalue, cvalue_b, cout, cout_b = cross_sums
    n = lax.axis_size("dp")
    width = cquery.shape[0]

    def columns(weight):
        parts = weight.shape[1] // width
        return weight.reshape(n, ROWS, parts, width).transpose(2, 0, 1, 3)

    chunks = [red_w.reshape(n, 4, ROWS, width).transpose(1, 0, 2, 3), columns(exp_w)]
    chunks += [columns(out_w), columns(packed)]
    chunks += [columns(w) for w in (cquery, ckey, cvalue, cout)]
    blocks = jnp.concatenate([c.astype(jnp.bfloat16) for c in chunks], 0)
    vectors = [gain, shift, query_b, value_b, out_b, fgain, fshift, red_b]
    vectors = [v[None] for v in vectors] + [exp_b.reshape(4, width)]
    vectors += [v[None] for v in (cgain, cshift, cquery_b, cvalue_b, cout_b)]
    vectors = jnp.concatenate(vectors + [jnp.zeros((VECTORS - 17, width), jnp.float32)], 0)
    shards, totals = scatter(blocks, vectors)
    from_two = [(1, 0)]
    is_two = section_index == 1
    cross_shards = shards[12:]
    cross_shards = jnp.where(is_two, cross_shards, lax.ppermute(cross_shards, "section", from_two))
    cross_totals = totals[12:17]
    cross_totals = jnp.where(is_two, cross_totals, lax.ppermute(cross_totals, "section", from_two))
    shards = shards.astype(jnp.float32)
    cross_shards = cross_shards.astype(jnp.float32)
    dp = lax.axis_index("dp")
    own = lax.dynamic_slice_in_dim(totals[:8], dp * ROWS, ROWS, 1)
    own_exp = lax.dynamic_slice_in_dim(totals[8:12].reshape(-1), dp * 4 * ROWS, 4 * ROWS, 0)
    own_cross = lax.dynamic_slice_in_dim(cross_totals, dp * ROWS, ROWS, 1)

    def joined(parts):
        return parts.transpose(1, 0, 2).reshape(ROWS, -1)

    layer = (
        own[0], own[1], joined(shards[9:12]), own[2], own[3], shards[8], own[4], own[5], own[6],
        joined(shards[4:8]), own_exp, shards[:4].reshape(4 * ROWS, width), own[7],
    )
    crossed = (
        own_cross[0], own_cross[1], cross_shards[0], own_cross[2], cross_shards[1], cross_shards[2],
        own_cross[3], cross_shards[3], own_cross[4],
    )
    return tuple(part[None] for part in layer), crossed


def body(
    tokens,
    images,
    lengths,
    cotangent,
    attend_gain,
    attend_shift,
    projections,
    query_bias,
    value_bias,
    output_weight,
    output_bias,
    feed_gain,
    feed_shift,
    expand_weight,
    expand_bias,
    reduce_weight,
    reduce_bias,
    cross_gain,
    cross_shift,
    cross_query,
    cross_query_bias,
    cross_key,
    cross_value,
    cross_value_bias,
    cross_out,
    cross_out_bias,
):
    layer = tuple(
        (
            weight[0]
            for weight in (
                attend_gain,
                attend_shift,
                projections,
                query_bias,
                value_bias,
                output_weight,
                output_bias,
                feed_gain,
                feed_shift,
                expand_weight,
                expand_bias,
                reduce_weight,
                reduce_bias,
            )
        )
    )
    cross = (
        cross_gain,
        cross_shift,
        cross_query,
        cross_query_bias,
        cross_key,
        cross_value,
        cross_value_bias,
        cross_out,
        cross_out_bias,
    )
    pair_weight = jnp.concatenate([cross_key, cross_value], 1)
    pair_bias = jnp.concatenate([jnp.zeros_like(cross_value_bias), cross_value_bias], 0)
    section_index = lax.axis_index("section")
    is_two = section_index == 1
    block = MB_CAPS
    half = images.shape[1]
    slots = tokens.shape[1]
    width = tokens.shape[2]
    positions = jnp.arange(slots, dtype=jnp.int32)
    causal = positions[None, :] <= positions[:, None]
    zero_cross = tuple((jnp.zeros(weight.shape, jnp.float32) for weight in cross))

    def image_project(image_rows):
        return (product(image_rows, pair_weight) + pair_bias).astype(jnp.bfloat16)

    def image_back(image_rows, dpairs):
        dimages = back_product(dpairs, pair_weight)
        pair_grad = weight_product(image_rows, dpairs)
        return (
            dimages,
            (pair_grad[:, :width], pair_grad[:, width:], column_sum(dpairs[..., width:])),
        )

    def cross_yes(hidden, image_data):
        pairs = image_project(image_data)
        after, saved = cross_forward(hidden, pairs, cross)
        return (after, saved, pairs)

    def cross_no(hidden, image_data):
        saved = (
            jnp.zeros((block, slots, width), jnp.float32),
            jnp.zeros((block, slots, 1), jnp.float32),
            jnp.zeros((block, slots, width), jnp.bfloat16),
            jnp.zeros((block, slots, width), jnp.bfloat16),
            jnp.zeros((block, slots, width), jnp.bfloat16),
            jnp.zeros((block, HEADS, slots, 1), jnp.float32),
        )
        return (hidden, saved, jnp.zeros((block, 2 * half, 2 * width), jnp.bfloat16))

    def back_yes(grad, saved, pairs, image_data):
        dgrad, parts, dpairs = cross_back(grad, saved, pairs, cross)
        dimages, image_terms = image_back(image_data, dpairs)
        return (dgrad, parts[:4] + image_terms + parts[4:], dimages)

    def back_no(grad, saved, pairs, image_data):
        return (grad, zero_cross, jnp.zeros((block, 2 * half, width), jnp.float32))

    received = jnp.zeros((block, slots, width), jnp.bfloat16)
    arriving = jnp.zeros((block, half, width), jnp.bfloat16)
    finished = jnp.zeros(tokens.shape, jnp.bfloat16)
    kept = []
    for tick in range(MICRO + 1):
        index = jnp.clip(tick - section_index, 0, MICRO - 1)
        start = index * block
        live = positions[None, :] < lax.dynamic_slice_in_dim(lengths, start, block, 0)[:, None]
        mask = live[:, None, :] & causal[None]
        own_tokens = lax.dynamic_slice_in_dim(tokens, start, block, 0)
        own_images = lax.dynamic_slice_in_dim(images, start, block, 0)
        hidden = jnp.where(is_two, received, own_tokens).astype(jnp.float32)
        after_self, self_saved = self_forward(hidden, layer, mask)
        image_data = jnp.concatenate([arriving, own_images], 1)
        after_cross, cross_saved, pairs = lax.cond(
            is_two, cross_yes, cross_no, after_self, image_data
        )
        final, feed_saved = feed_forward(after_cross, layer)
        result = final.astype(jnp.bfloat16)
        finished = lax.dynamic_update_slice_in_dim(finished, result, start, 0)
        kept.append((mask, live, self_saved, cross_saved, feed_saved, pairs, image_data))
        if tick < MICRO:
            received = shifted(result, "section", 1)
            arriving = shifted(own_images, "section", 1)
    layer_sums = tuple((jnp.zeros(weight.shape, jnp.float32) for weight in layer))
    cross_sums = zero_cross
    input_grads = jnp.zeros(tokens.shape, jnp.float32)
    image_grads = jnp.zeros(images.shape, jnp.float32)
    returning = jnp.zeros((block, slots, width), jnp.bfloat16)
    coming = jnp.zeros((block, half, width), jnp.float32)
    for turn in range(MICRO + 1):
        tick = MICRO - turn
        offset = tick - section_index
        index = jnp.clip(offset, 0, MICRO - 1)
        start = index * block
        valid = ((offset >= 0) & (offset < MICRO)).astype(jnp.float32)
        mask, live, self_saved, cross_saved, feed_saved, pairs, image_data = kept[tick]
        own_images = lax.dynamic_slice_in_dim(images, start, block, 0)
        seed_grad = lax.dynamic_slice_in_dim(cotangent[0], start, block, 0).astype(
            jnp.float32
        ) * live[..., None].astype(jnp.float32)
        grad = seed_grad + returning.astype(jnp.float32)
        grad, feed_grads = feed_back(grad, feed_saved, layer)
        grad, cross_grads, image_part = lax.cond(
            is_two, back_yes, back_no, grad, cross_saved, pairs, image_data
        )
        grad, self_grads = self_back(grad, self_saved, layer, mask)
        layer_sums = tuple(
            (total + valid * part for total, part in zip(layer_sums, self_grads + feed_grads))
        )
        cross_sums = tuple((total + valid * part for total, part in zip(cross_sums, cross_grads)))
        sent = grad.astype(jnp.bfloat16)
        stored = jnp.where(is_two, sent.astype(jnp.float32), grad)
        input_grads = jnp.where(
            valid > 0, lax.dynamic_update_slice_in_dim(input_grads, stored, start, 0), input_grads
        )
        own_dimages = jnp.where(is_two, image_part[:, half:], coming)
        image_grads = jnp.where(
            valid > 0,
            lax.dynamic_update_slice_in_dim(image_grads, own_dimages, start, 0),
            image_grads,
        )
        if turn < MICRO:
            returning = shifted(sent, "section", -1)
            coming = shifted(image_part[:, :half].astype(jnp.bfloat16), "section", -1).astype(
                jnp.float32
            )
    if lax.axis_size("dp") == 16:
        shared, crossed = reduce_fast(layer_sums, cross_sums, section_index)
    else:
        shared = lax.psum_scatter(
            tuple((total[None] for total in layer_sums)), "dp", scatter_dimension=1, tiled=True
        )
        scattered = lax.psum_scatter(cross_sums, "dp", scatter_dimension=0, tiled=True)
        crossed = jax.tree.map(
            lambda part: part.astype(jnp.float32), lax.psum(for_sending(tuple(scattered)), "section")
        )
    return (finished[None], input_grads[None], image_grads) + tuple(shared) + tuple(crossed)


def solution(mesh):
    placed = (
        P("dp", None, None),
        P("dp", "section", None),
        P("dp"),
        P("section", "dp", None, None),
        P("section", None),
        P("section", None),
        P("section", None, None),
        P("section", None),
        P("section", None),
        P("section", None, None),
        P("section", None),
        P("section", None),
        P("section", None),
        P("section", None, None),
        P("section", None),
        P("section", None, None),
        P("section", None),
        P(),
        P(),
        P(),
        P(),
        P(),
        P(),
        P(),
        P(),
        P(),
    )
    return jax.shard_map(
        body,
        mesh=mesh,
        in_specs=placed,
        out_specs=(
            P("section", "dp", None, None),
            P("section", "dp", None, None),
            P("dp", "section", None),
            P("section", "dp"),
            P("section", "dp"),
            P("section", "dp", None),
            P("section", "dp"),
            P("section", "dp"),
            P("section", "dp", None),
            P("section", "dp"),
            P("section", "dp"),
            P("section", "dp"),
            P("section", "dp", None),
            P("section", "dp"),
            P("section", "dp", None),
            P("section", "dp"),
            P("dp"),
            P("dp"),
            P("dp", None),
            P("dp"),
            P("dp", None),
            P("dp", None),
            P("dp"),
            P("dp", None),
            P("dp"),
        ),
        check_vma=False,
    )
```

```python
import jax
import jax.numpy as jnp
from jax import lax
from jax.experimental import pallas as pl
from jax.experimental.pallas import tpu as pltpu
from jax.sharding import PartitionSpec as P

HEADS = 12
HEAD_DIM = 64
MB_CAPS = 4
MICRO = 1


EPS = 1e-05
NEG = -1000000000.0


def shifted(block, axis, distance):
    devices = range(lax.axis_size(axis))
    route = [(i - distance, i) for i in devices if i - distance in devices]
    return lax.ppermute(block, axis, route)


def for_sending(array):
    return jax.tree.map(lambda a: a.astype(jnp.bfloat16) if a.dtype == jnp.float32 else a, array)


def layer_norm(rows, gain, shift):
    mean = jnp.mean(rows, -1, keepdims=True)
    centred = rows - mean
    inverse = lax.rsqrt(jnp.mean(centred * centred, -1, keepdims=True) + EPS)
    normed = centred * inverse
    return (normed * gain + shift, normed, inverse)


def norm_back(grad, normed, inverse, gain):
    scaled = grad * gain
    inner = (
        scaled
        - jnp.mean(scaled, -1, keepdims=True)
        - normed * jnp.mean(scaled * normed, -1, keepdims=True)
    )
    return (inverse * inner, jnp.sum(grad * normed, axis=(0, 1)), jnp.sum(grad, axis=(0, 1)))


def product(rows, weight):
    return jnp.einsum("bsi,ij->bsj", rows, weight, preferred_element_type=jnp.float32)


def back_product(grad, weight):
    return jnp.einsum("bsj,ij->bsi", grad, weight, preferred_element_type=jnp.float32)


def weight_product(rows, grad):
    return jnp.einsum("bsi,bsj->ij", rows, grad, preferred_element_type=jnp.float32)


def column_sum(grad):
    return jnp.sum(grad.astype(jnp.float32), axis=(0, 1))


def split_heads(rows):
    return rows.reshape(rows.shape[0], rows.shape[1], HEADS, HEAD_DIM)


def scores_of(query, keys, mask):
    scores = jnp.einsum(
        "bqhd,bkhd->bhqk", split_heads(query), split_heads(keys), preferred_element_type=jnp.float32
    ) * HEAD_DIM ** (-0.5)
    if mask is None:
        return scores
    return jnp.where(mask[:, None], scores, NEG)


def attend(query, keys, values, mask):
    scores = scores_of(query, keys, mask)
    top = jnp.max(scores, -1, keepdims=True)
    expo = jnp.exp(scores - top)
    total = jnp.sum(expo, -1, keepdims=True)
    probs = (expo / total).astype(jnp.bfloat16)
    mixed = jnp.einsum(
        "bhqk,bkhd->bqhd", probs, split_heads(values), preferred_element_type=jnp.float32
    )
    return (mixed.reshape(query.shape).astype(jnp.bfloat16), top + jnp.log(total))


def attend_back(grad, query, keys, values, logsum, mask):
    scale = HEAD_DIM ** (-0.5)
    probs = jnp.exp(scores_of(query, keys, mask) - logsum)
    grad_heads = split_heads(grad)
    dprobs = jnp.einsum(
        "bqhd,bkhd->bhqk", grad_heads, split_heads(values), preferred_element_type=jnp.float32
    )
    rowdot = jnp.sum(probs * dprobs, -1, keepdims=True)
    dscores = (probs * (dprobs - rowdot)).astype(jnp.bfloat16)
    dquery = (
        jnp.einsum(
            "bhqk,bkhd->bqhd", dscores, split_heads(keys), preferred_element_type=jnp.float32
        )
        * scale
    )
    dkeys = (
        jnp.einsum(
            "bhqk,bqhd->bkhd", dscores, split_heads(query), preferred_element_type=jnp.float32
        )
        * scale
    )
    dvalues = jnp.einsum(
        "bhqk,bqhd->bkhd",
        probs.astype(jnp.bfloat16),
        grad_heads,
        preferred_element_type=jnp.float32,
    )
    return (
        dquery.reshape(query.shape).astype(jnp.bfloat16),
        dkeys.reshape(keys.shape).astype(jnp.bfloat16),
        dvalues.reshape(values.shape).astype(jnp.bfloat16),
    )


def self_forward(hidden, layer, mask):
    normal, normed, inverse = layer_norm(hidden, layer[0], layer[1])
    entry = normal.astype(jnp.bfloat16)
    packed = product(entry, layer[2])
    width = hidden.shape[-1]
    query = (packed[..., :width] + layer[3]).astype(jnp.bfloat16)
    keys = packed[..., width : 2 * width].astype(jnp.bfloat16)
    values = (packed[..., 2 * width :] + layer[4]).astype(jnp.bfloat16)
    mixed, logsum = attend(query, keys, values, mask)
    after = hidden + (product(mixed, layer[5]) + layer[6])
    return (after, (normed, inverse, entry, query, keys, values, mixed, logsum))


def self_back(grad, saved, layer, mask):
    normed, inverse, entry, query, keys, values, mixed, logsum = saved
    branch = grad.astype(jnp.bfloat16)
    out_weight_grad = weight_product(mixed, branch)
    out_bias_grad = column_sum(branch)
    dmixed = back_product(branch, layer[5]).astype(jnp.bfloat16)
    dquery, dkeys, dvalues = attend_back(dmixed, query, keys, values, logsum, mask)
    dpacked = jnp.concatenate([dquery, dkeys, dvalues], -1)
    packed_grad = weight_product(entry, dpacked)
    dentry = back_product(dpacked, layer[2])
    dhidden, gain_grad, shift_grad = norm_back(dentry, normed, inverse, layer[0])
    return (
        grad + dhidden,
        (
            gain_grad,
            shift_grad,
            packed_grad,
            column_sum(dquery),
            column_sum(dvalues),
            out_weight_grad,
            out_bias_grad,
        ),
    )


def gelu_slope(expanded):
    normal_cdf = 0.5 * (1.0 + jax.scipy.special.erf(expanded * 0.7071067811865476))
    return normal_cdf + expanded * jnp.exp(-0.5 * expanded * expanded) * 0.3989422804014327


def feed_forward(hidden, layer):
    normal, normed, inverse = layer_norm(hidden, layer[7], layer[8])
    entry = normal.astype(jnp.bfloat16)
    expanded = product(entry, layer[9]) + layer[10]
    active = jax.nn.gelu(expanded, approximate=False).astype(jnp.bfloat16)
    after = hidden + (product(active, layer[11]) + layer[12])
    return (after, (normed, inverse, entry, expanded, active))


def feed_back(grad, saved, layer):
    normed, inverse, entry, expanded, active = saved
    branch = grad.astype(jnp.bfloat16)
    reduce_grad = weight_product(active, branch)
    reduce_bias_grad = column_sum(branch)
    dactive = back_product(branch, layer[11])
    dexpanded = (dactive * gelu_slope(expanded)).astype(jnp.bfloat16)
    expand_grad = weight_product(entry, dexpanded)
    expand_bias_grad = column_sum(dexpanded)
    dentry = back_product(dexpanded, layer[9])
    dhidden, gain_grad, shift_grad = norm_back(dentry, normed, inverse, layer[7])
    return (
        grad + dhidden,
        (gain_grad, shift_grad, expand_grad, expand_bias_grad, reduce_grad, reduce_bias_grad),
    )


def cross_forward(hidden, pairs, cross):
    normal, normed, inverse = layer_norm(hidden, cross[0], cross[1])
    entry = normal.astype(jnp.bfloat16)
    query = (product(entry, cross[2]) + cross[3]).astype(jnp.bfloat16)
    width = hidden.shape[-1]
    mixed, logsum = attend(query, pairs[..., :width], pairs[..., width:], None)
    after = hidden + (product(mixed, cross[7]) + cross[8])
    return (after, (normed, inverse, entry, query, mixed, logsum))


def cross_back(grad, saved, pairs, cross):
    normed, inverse, entry, query, mixed, logsum = saved
    width = grad.shape[-1]
    branch = grad.astype(jnp.bfloat16)
    out_grad = weight_product(mixed, branch)
    out_bias_grad = column_sum(branch)
    dmixed = back_product(branch, cross[7]).astype(jnp.bfloat16)
    dquery, dkeys, dvalues = attend_back(
        dmixed, query, pairs[..., :width], pairs[..., width:], logsum, None
    )
    query_grad = weight_product(entry, dquery)
    dentry = back_product(dquery, cross[2])
    dhidden, gain_grad, shift_grad = norm_back(dentry, normed, inverse, cross[0])
    parts = (gain_grad, shift_grad, query_grad, column_sum(dquery), out_grad, out_bias_grad)
    return (grad + dhidden, parts, jnp.concatenate([dkeys, dvalues], -1))


BF = jnp.bfloat16
F32 = jnp.float32
WIDE = 768
TOKENS = 256
CAPS = 4
SLOT = 64
PAIRS = 6
MESH = pl.DeviceIdType.MESH
RING = 5
LEAD = (2, 2, 2, 2)


def nn(a, b):
    return lax.dot_general(a, b, (((1,), (0,)), ((), ())), preferred_element_type=F32)


def nt(a, b):
    return lax.dot_general(a, b, (((1,), (1,)), ((), ())), preferred_element_type=F32)


def tn(a, b):
    return lax.dot_general(a, b, (((0,), (0,)), ((), ())), preferred_element_type=F32)


def rows_of(i, size):
    return pl.ds(pl.multiple_of(i * size, size), size)


def erf(x):
    return lax.erf(x)


def norm_rows(source, gain, shift, normed, inverse, entry):
    @pl.loop(0, TOKENS // 32)
    def _(i):
        r = rows_of(i, 32)
        x = source[r, :]
        centred = x - jnp.mean(x, -1, keepdims=True)
        inv = lax.rsqrt(jnp.mean(centred * centred, -1, keepdims=True) + EPS)
        n = centred * inv
        normed[r, :] = n.astype(normed.dtype)
        inverse[r, :] = inv
        entry[r, :] = (n * gain[...] + shift[...]).astype(BF)


def norm_rows_back(grad_entry, normed, inverse, gain, grad, vec, gain_row, shift_row):
    zero = jnp.zeros((8, WIDE), F32)

    def block(i, sums):
        r = rows_of(i, 32)
        d = grad_entry[r, :]
        n = normed[r, :].astype(F32)
        scaled = d * gain[...]
        first = jnp.mean(scaled, -1, keepdims=True)
        second = jnp.mean(scaled * n, -1, keepdims=True)
        grad[r, :] = grad[r, :] + inverse[r, :] * (scaled - first - n * second)
        dn = d * n
        return (
            sums[0] + jnp.sum(dn.reshape(4, 8, WIDE), 0),
            sums[1] + jnp.sum(d.reshape(4, 8, WIDE), 0),
        )

    by_gain, by_shift = lax.fori_loop(0, TOKENS // 32, block, (zero, zero))
    vec[gain_row : gain_row + 1, :] = jnp.sum(by_gain, 0, keepdims=True)
    vec[shift_row : shift_row + 1, :] = jnp.sum(by_shift, 0, keepdims=True)


def sum_columns(rows, count):
    def block(i, total):
        for k in range(count):
            part = rows(k, rows_of(i, 32)).astype(F32)
            total = total + jnp.sum(part.reshape(4, 8, WIDE), 0)
        return total

    total = lax.fori_loop(0, TOKENS // 32, block, jnp.zeros((8, WIDE), F32))
    return jnp.sum(total, 0, keepdims=True)


def mega_kernel(
    lengths, tokens, cotangent, images,
    again, ashift, qbias, vbias, obias, fgain, fshift, ebias, rbias,
    cgain, cshift, cqbias, cvbias, cobias,
    h_proj, h_out, h_exp, h_red, h_cq, h_ck, h_cv, h_co,
    out_h, out_in, out_img, out_shards, out_vec,
    GG, WP, WO, WC, R0, R1, R2, R3,
    H, G, D, N1, N2, N3, I1, I2, I3, E, ET1, ET2, ET3,
    QKV, M, MT, QC, C, CT, U, SL, A, AT, PT, PC, IM, IMT, KV, B1, B2, B3, DM,
    HB, HIN, DIN, DIM, MASK, VL, YS,
    wsem, lsem, osem, ysend, yrecv, send_sem, recv_sem, vsend, vrecv, credit,
):
    section = lax.axis_index("section")
    dp = lax.axis_index("dp")
    one = section == 0
    two = section == 1
    bits = [lax.rem(lax.div(dp, 1 << k), 2) for k in range(4)]
    partners = [dp + (1 << k) * (1 - 2 * bits[k]) for k in range(4)]
    count = jnp.where(two, 16, 12)

    barrier = pltpu.get_barrier_semaphore()
    for partner in partners:
        pl.semaphore_signal(barrier, inc=1, device_id={"dp": partner}, device_id_type=MESH)
    pl.semaphore_signal(barrier, inc=1, device_id={"section": 1 - section}, device_id_type=MESH)
    pl.semaphore_wait(barrier, 5)

    def across(source, target, i):
        return pltpu.make_async_remote_copy(
            src_ref=source, dst_ref=target, send_sem=ysend.at[i], recv_sem=yrecv.at[i],
            device_id={"section": 1 - section}, device_id_type=MESH,
        )

    images_a = across(images.at[0:2], IM.at[0:2, 0], 0)
    images_b = across(images.at[2:4], IM.at[2:4, 0], 1)
    send_h = across(HB, HIN, 2)
    send_d = across(HB, DIN, 3)
    send_i = across(IM.at[:, 0], DIM, 4)

    def load(source, target, i):
        return pltpu.make_async_copy(source, target, wsem.at[i])

    own_images = load(images, IM.at[:, 1], 0)
    loads = {
        "cross": [load(w, WC.at[i], 1 + i) for i, w in enumerate((h_cq, h_ck, h_cv, h_co))],
        "proj": [load(h_proj, WP, 5)],
        "out": [load(h_out, WO, 6)],
        "exp": [
            load(h_exp.at[:, :, :, :, :, pl.ds(WIDE * j, WIDE)], GG.at[12 + j], 7 + j)
            for j in range(4)
        ],
        "red": [load(h_red.at[j], GG.at[8 + j], 11 + j) for j in range(4)],
    }

    @pl.when(one)
    def _():
        images_a.start()

    @pl.when(two)
    def _():
        own_images.start()
        for i in (1, 2, 0, 3):
            loads["cross"][i].start()

    for name in ("proj", "out", "exp", "red"):
        for copy in loads[name]:
            copy.start()

    def arrived(name):
        for copy in loads[name]:
            copy.wait()

    out_vec[...] = jnp.zeros_like(out_vec)
    low_lane = lax.broadcasted_iota(jnp.int32, (1, 128), 1) < SLOT
    keep_low = low_lane.astype(F32).astype(BF)
    keep_high = jnp.logical_not(low_lane).astype(F32).astype(BF)

    def stacked(x):
        return jnp.concatenate([x * keep_low, x * keep_high], 0)

    def unstacked(x):
        half = x.shape[0] // 2
        return jnp.where(low_lane, x[:half], x[half:])

    eighth = jnp.asarray(0.125, BF)

    for pair in range(2):
        key = lax.broadcasted_iota(jnp.int32, (128, 256), 0)
        query = lax.rem(lax.broadcasted_iota(jnp.int32, (128, 256), 1), 128)
        first = key < SLOT
        length = jnp.where(first, lengths[2 * pair], lengths[2 * pair + 1] + SLOT)
        same = first == (query < SLOT)
        MASK[pair] = jnp.where(same & (key <= query) & (key < length), 1.0, 0.0)

    def pair_rows(which, half):
        rows = IM[2 * which : 2 * which + 2, half].reshape(TOKENS, WIDE)
        keys = nn(rows, WC[1])
        KV[2 * which : 2 * which + 2, half, :, :WIDE] = keys.astype(BF).reshape(2, 128, WIDE)
        values = nn(rows, WC[2]) + cvbias[...]
        KV[2 * which : 2 * which + 2, half, :, WIDE:] = values.astype(BF).reshape(2, 128, WIDE)

    def turn_images(which, half):
        for c in (2 * which, 2 * which + 1):
            IMT[:, pl.ds(c * 256 + 128 * half, 128)] = IM[c, half].T

    @pl.when(two)
    def _():
        for copy in loads["cross"]:
            copy.wait()
        own_images.wait()
        for which in range(2):
            pair_rows(which, 1)
            turn_images(which, 1)
        images_a.wait_recv()
        pair_rows(0, 0)
        turn_images(0, 0)
        send_h.wait_recv()
        H[...] = HIN[...].astype(F32)

    @pl.when(one)
    def _():
        H[...] = tokens[...].astype(F32)

    norm_rows(H, again, ashift, N1, I1, E)
    ET1[...] = E[...].T
    arrived("proj")
    QKV[0] = (nn(E[...], WP[:, 0:WIDE]) + qbias[...]).astype(BF)
    QKV[1] = nn(E[...], WP[:, WIDE : 2 * WIDE]).astype(BF)
    QKV[2] = (nn(E[...], WP[:, 2 * WIDE :]) + vbias[...]).astype(BF)

    def softmax_keys(scores):
        expo = jnp.exp(scores - jnp.max(scores, 0, keepdims=True))
        return expo * (1.0 / jnp.sum(expo, 0, keepdims=True))

    @pl.loop(0, PAIRS)
    def _(hp):
        cols = rows_of(hp, 128)
        for pair in range(2):
            rows = pl.ds(pair * 128, 128)
            query = stacked(QKV[0, rows, cols] * eighth)
            scores = nt(QKV[1, rows, cols], query)
            scores = jnp.where(MASK[pair] > 0.0, scores, NEG)
            probs = softmax_keys(scores).astype(BF)
            PT[2 * hp + pair] = probs
            M[rows, cols] = unstacked(tn(probs, QKV[2, rows, cols])).astype(BF)

    MT[...] = M[...].T
    arrived("out")
    H[...] = H[...] + (nn(M[...], WO[...]) + obias[...])

    @pl.when(two)
    def _():
        norm_rows(H, cgain, cshift, N2, I2, E)
        ET2[...] = E[...].T
        QC[...] = (nn(E[...], WC[0]) + cqbias[...]).astype(BF)
        images_b.wait_recv()
        pair_rows(1, 0)
        turn_images(1, 0)

        @pl.loop(0, PAIRS)
        def _(hp):
            cols = rows_of(hp, 128)
            vcols = pl.ds(pl.multiple_of(WIDE + hp * 128, 128), 128)
            for c in range(CAPS):
                rows = pl.ds(c * SLOT, SLOT)
                query = stacked(QC[rows, cols] * eighth)
                keys = KV[c, :, :, cols].reshape(256, 128)
                probs = softmax_keys(nt(keys, query)).astype(BF)
                PC[4 * hp + c] = probs
                values = KV[c, :, :, vcols].reshape(256, 128)
                C[rows, cols] = unstacked(tn(probs, values)).astype(BF)

        CT[...] = C[...].T
        H[...] = H[...] + (nn(C[...], WC[3]) + cobias[...])

    norm_rows(H, fgain, fshift, N3, I3, E)
    ET3[...] = E[...].T
    arrived("exp")
    arrived("red")
    H[...] = H[...] + rbias[...]

    @pl.loop(0, 4)
    def _(j):
        U[...] = nn(E[...], GG[12 + j].reshape(WIDE, WIDE)) + ebias[:, rows_of(j, WIDE)]

        @pl.loop(0, TOKENS // 16)
        def _(i):
            r = rows_of(i, 16)
            u = U[r, :]
            cdf = 0.5 * (1.0 + erf(u * 0.7071067811865476))
            A[r, :] = (u * cdf).astype(BF)
            SL[j, r, :] = (cdf + u * jnp.exp(-0.5 * u * u) * 0.3989422804014327).astype(BF)

        AT[rows_of(j, 4)] = A[...].T.reshape(4, 4, 48, TOKENS)
        H[...] = H[...] + nn(A[...], GG[8 + j].reshape(WIDE, WIDE))

    HB[...] = H[...].astype(BF)
    store_h = pltpu.make_async_copy(HB, out_h, osem.at[0])
    store_h.start()

    @pl.when(one)
    def _():
        send_h.start()
        send_h.wait_send()
        images_a.wait_send()
        images_b.start()

    @pl.loop(0, CAPS)
    def _(c):
        r = rows_of(c, SLOT)
        live = lax.broadcasted_iota(jnp.int32, (SLOT, 1), 0) < lengths[c]
        G[r, :] = jnp.where(live, cotangent[r, :].astype(F32), 0.0)

    @pl.when(one)
    def _():
        send_d.wait_recv()
        G[...] = G[...] + DIN[...].astype(F32)

    def where(c, k, bit):
        return (c,) + tuple(bits[a] if a < k else bit if a == k else slice(None) for a in (3, 2, 1, 0))

    landing = (R0, R1, R2, R3)
    rings = (RING, RING, 16, 16)

    def exchange(c, k):
        return pltpu.make_async_remote_copy(
            src_ref=GG.at[where(c, k, 1 - bits[k])],
            dst_ref=landing[k].at[lax.rem(c, rings[k])],
            send_sem=send_sem.at[c, k], recv_sem=recv_sem.at[c, k],
            device_id={"dp": partners[k]}, device_id_type=MESH,
        )

    def begin(c, k):
        if rings[k] < 16:
            @pl.when(c >= rings[k])
            def _():
                pl.semaphore_wait(credit.at[k], 1)
        exchange(c, k).start()

    def finish(c, k):
        exchange(c, k).wait()
        keep = GG.at[where(c, k, bits[k])]
        term = landing[k].at[lax.rem(c, rings[k])]
        if k == 3:
            keep[...] = keep[...] + term[...]
        elif k == 2:
            for i in range(2):
                keep[i] = keep[i] + term[i]
        elif k == 1:
            @pl.loop(0, 2)
            def _(i):
                for j in range(2):
                    keep[i, j] = keep[i, j] + term[i, j]
        else:
            @pl.loop(0, 4)
            def _(i):
                for j in range(2):
                    a, b = lax.div(i, 2), lax.rem(i, 2)
                    keep[a, b, j] = keep[a, b, j] + term[a, b, j]
        if rings[k] < 16:
            @pl.when(c + rings[k] < count)
            def _():
                pl.semaphore_signal(
                    credit.at[k], inc=1, device_id={"dp": partners[k]}, device_id_type=MESH
                )

    def weight_gradient(c, left, right):
        for t in range(3):
            part = nn(left, right(pl.ds(256 * t, 256)))
            GG[c, :, :, :, :, :, pl.ds(256 * t, 256)] = part.astype(BF).reshape(LEAD + (48, 256))

    B1[...] = G[...].astype(BF)
    out_vec[7:8, :] = sum_columns(lambda k, r: B1[r, :], 1)

    @pl.loop(0, 4)
    def _(i):
        weight_gradient(i, AT[:, i].reshape(WIDE, TOKENS), lambda t: B1[:, t])
        begin(i, 0)

    @pl.loop(0, 4)
    def _(j):
        U[...] = nt(B1[...], GG[8 + j].reshape(WIDE, WIDE))

        def block(i, total):
            r = rows_of(i, 32)
            du = (U[r, :] * SL[j, r, :].astype(F32)).astype(BF)
            SL[j, r, :] = du
            return total + jnp.sum(du.astype(F32).reshape(4, 8, WIDE), 0)

        total = lax.fori_loop(0, TOKENS // 32, block, jnp.zeros((8, WIDE), F32))
        out_vec[pl.ds(8 + j, 1), :] = jnp.sum(total, 0, keepdims=True)
        part = nt(SL[j], GG[12 + j].reshape(WIDE, WIDE))

        @pl.when(j == 0)
        def _():
            D[...] = part

        @pl.when(j > 0)
        def _():
            D[...] = D[...] + part

    norm_rows_back(D, N3, I3, fgain, G, out_vec, 5, 6)

    @pl.loop(0, 4)
    def _(i):
        finish(i, 0)
        begin(i, 1)

    @pl.when(two)
    def _():
        B2[...] = G[...].astype(BF)
        out_vec[16:17, :] = sum_columns(lambda k, r: B2[r, :], 1)
        DM[...] = nt(B2[...], WC[3]).astype(BF)

        @pl.loop(0, PAIRS)
        def _(hp):
            cols = rows_of(hp, 128)
            vcols = pl.ds(pl.multiple_of(WIDE + hp * 128, 128), 128)
            for c in range(CAPS):
                rows = pl.ds(c * SLOT, SLOT)
                query = stacked(QC[rows, cols] * eighth)
                grad = stacked(DM[rows, cols])
                keys = KV[c, :, :, cols].reshape(256, 128)
                values = KV[c, :, :, vcols].reshape(256, 128)
                probs = PC[4 * hp + c]
                wide = probs.astype(F32)
                dprobs = nt(values, grad)
                dscores = (wide * (dprobs - jnp.sum(wide * dprobs, 0, keepdims=True))).astype(BF)
                KV[c, :, :, cols] = nn(dscores, query).astype(BF).reshape(2, 128, 128)
                KV[c, :, :, vcols] = nn(probs, grad).astype(BF).reshape(2, 128, 128)
                QC[rows, cols] = (unstacked(tn(dscores, keys)) * 0.125).astype(BF)

        out_vec[14:15, :] = sum_columns(lambda k, r: QC[r, :], 1)
        D[...] = nt(QC[...], WC[0])
        norm_rows_back(D, N2, I2, cgain, G, out_vec, 12, 13)

    B3[...] = G[...].astype(BF)
    out_vec[4:5, :] = sum_columns(lambda k, r: B3[r, :], 1)
    DM[...] = nt(B3[...], WO[...]).astype(BF)

    @pl.loop(0, PAIRS)
    def _(hp):
        cols = rows_of(hp, 128)
        for pair in range(2):
            rows = pl.ds(pair * 128, 128)
            query = stacked(QKV[0, rows, cols] * eighth)
            grad = stacked(DM[rows, cols])
            keys = QKV[1, rows, cols]
            probs = PT[2 * hp + pair]
            wide = probs.astype(F32)
            dprobs = nt(QKV[2, rows, cols], grad)
            dscores = (wide * (dprobs - jnp.sum(wide * dprobs, 0, keepdims=True))).astype(BF)
            QKV[1, rows, cols] = nn(dscores, query).astype(BF)
            QKV[2, rows, cols] = nn(probs, grad).astype(BF)
            QKV[0, rows, cols] = (unstacked(tn(dscores, keys)) * 0.125).astype(BF)

    out_vec[2:3, :] = sum_columns(lambda k, r: QKV[0, r, :], 1)
    out_vec[3:4, :] = sum_columns(lambda k, r: QKV[2, r, :], 1)
    D[...] = nt(QKV[0], WP[:, 0:WIDE])
    D[...] = D[...] + nt(QKV[1], WP[:, WIDE : 2 * WIDE])
    D[...] = D[...] + nt(QKV[2], WP[:, 2 * WIDE :])
    norm_rows_back(D, N1, I1, again, G, out_vec, 0, 1)

    store_h.wait()

    @pl.when(two)
    def _():
        HB[...] = G[...].astype(BF)
        send_d.start()
        G[...] = HB[...].astype(F32)

    store_in = pltpu.make_async_copy(G, out_in, osem.at[1])
    store_in.start()

    @pl.loop(0, 4)
    def _(j):
        weight_gradient(4 + j, ET3[...], lambda t: SL[j, :, t])
        begin(4 + j, 0)

    @pl.loop(0, 3)
    def _(j):
        weight_gradient(8 + j, ET1[...], lambda t: QKV[j, :, t])

    weight_gradient(11, MT[...], lambda t: B3[:, t])

    @pl.when(two)
    def _():
        weight_gradient(12, ET2[...], lambda t: QC[:, t])
        for j in range(2):
            weight_gradient(
                13 + j, IMT[...],
                lambda t: KV[:, :, :, pl.ds(WIDE * j + t.start, t.size)].reshape(4 * 256, t.size),
            )
        weight_gradient(15, CT[...], lambda t: B2[:, t])
        out_vec[15:16, :] = sum_columns(
            lambda k, r: KV[k, :, pl.ds(pl.multiple_of(lax.div(r.start, 2), 16), 16), WIDE:].reshape(32, WIDE), 4
        )
        for c in range(CAPS):
            part = nt(KV[c, :, :, :WIDE].reshape(256, WIDE), WC[1])
            part = part + nt(KV[c, :, :, WIDE:].reshape(256, WIDE), WC[2])
            IM[c] = part.astype(BF).reshape(2, 128, WIDE)
        send_i.start()

    for k in range(4):
        copy = pltpu.make_async_remote_copy(
            src_ref=out_vec, dst_ref=VL.at[k], send_sem=vsend.at[k], recv_sem=vrecv.at[k],
            device_id={"dp": partners[k]}, device_id_type=MESH,
        )
        copy.start()
        copy.wait()
        out_vec[...] = out_vec[...] + VL[k]

    def shard_out(c):
        return pltpu.make_async_copy(
            GG.at[(c,) + tuple(bits[a] for a in (3, 2, 1, 0))], out_shards.at[c], lsem.at[c]
        )

    def shard_across(c):
        return across(GG.at[(c,) + tuple(bits[a] for a in (3, 2, 1, 0))], YS.at[c - 12], 6 + c - 12)

    @pl.loop(0, count + 2)
    def _(tick):
        ahead = tick + 5

        @pl.when((ahead >= 8) & (ahead < count))
        def _():
            begin(ahead, 0)

        @pl.when(tick + 4 < count)
        def _():
            finish(tick + 4, 0)
            begin(tick + 4, 1)

        @pl.when(tick < count)
        def _():
            finish(tick, 1)
            begin(tick, 2)

        @pl.when((tick >= 1) & (tick - 1 < count))
        def _():
            finish(tick - 1, 2)
            begin(tick - 1, 3)

        @pl.when((tick >= 2) & (tick - 2 < count))
        def _():
            finish(tick - 2, 3)
            shard_out(tick - 2).start()

            @pl.when(tick - 2 >= 12)
            def _():
                shard_across(tick - 2).start()

    @pl.when(two)
    def _():
        vec_copy = across(out_vec, VL.at[4], 5)
        vec_copy.start()
        vec_copy.wait_send()
        store_img = pltpu.make_async_copy(IM.at[:, 1], out_img, osem.at[2])
        store_img.start()
        store_img.wait()
        send_d.wait_send()
        send_i.wait_send()
        for c in range(12, 16):
            shard_across(c).wait_send()

    @pl.when(one)
    def _():
        images_b.wait_send()
        send_i.wait_recv()
        store_img = pltpu.make_async_copy(DIM, out_img, osem.at[2])
        store_img.start()
        across(out_vec, VL.at[4], 5).wait_recv()
        out_vec[12:17, :] = VL[4, 12:17, :]
        store_img.wait()
        for c in range(12, 16):
            across(YS.at[c - 12], YS.at[c - 12], 6 + c - 12).wait_recv()
            copy = pltpu.make_async_copy(YS.at[c - 12], out_shards.at[c], lsem.at[c])
            copy.start()
            copy.wait()

    store_in.wait()

    @pl.loop(0, count)
    def _(c):
        shard_out(c).wait()


def mega(args):
    (
        tokens, images, lengths, cotangent, again, ashift, proj, qb, vb, wo, ob, fg, fs, we, eb, wr, rb,
        cg, cs, cq, cqb, ck, cv, cvb, co, cob,
    ) = args
    row = lambda v: v.reshape(1, -1)
    vm = pl.BlockSpec(memory_space=pltpu.VMEM)
    hbm = pl.BlockSpec(memory_space=pl.ANY)
    operands = [
        (lengths, pl.BlockSpec(memory_space=pltpu.SMEM)),
        (tokens.reshape(TOKENS, WIDE), vm),
        (cotangent.reshape(TOKENS, WIDE), vm),
        (images, hbm),
    ]
    operands += [(row(v), vm) for v in (again, ashift, qb, vb, ob, fg, fs, eb, rb, cg, cs, cqb, cvb, cob)]
    operands += [
        (proj[0], hbm), (wo[0], hbm),
        (we.reshape(LEAD + (48, 4 * WIDE)), hbm), (wr.reshape((4,) + LEAD + (48, WIDE)), hbm),
        (cq, hbm), (ck, hbm), (cv, hbm), (co, hbm),
    ]
    s = jax.ShapeDtypeStruct
    dma = pltpu.SemaphoreType.DMA
    big = (TOKENS, WIDE)
    turned = (WIDE, TOKENS)
    b = lambda *shape: pltpu.VMEM(shape, BF)
    f = lambda *shape: pltpu.VMEM(shape, F32)
    return pl.pallas_call(
        mega_kernel,
        out_shape=(
            s(big, BF), s(big, F32), s((CAPS, 128, WIDE), BF), s((16, 48, WIDE), BF), s((24, WIDE), F32),
        ),
        in_specs=[spec for _, spec in operands],
        out_specs=[hbm, hbm, hbm, hbm, vm],
        scratch_shapes=[
            b(16, *LEAD, 48, WIDE), b(WIDE, 3 * WIDE), b(WIDE, WIDE), b(4, WIDE, WIDE),
            b(RING, 2, 2, 2, 48, WIDE), b(RING, 2, 2, 48, WIDE), b(16, 2, 48, WIDE), b(16, 48, WIDE),
            f(*big), f(*big), f(*big), b(*big), b(*big), b(*big), f(TOKENS, 1), f(TOKENS, 1), f(TOKENS, 1),
            b(*big), b(*turned), b(*turned), b(*turned),
            b(3, *big), b(*big), b(*turned), b(*big), b(*big), b(*turned), f(*big), b(4, *big), b(*big),
            b(16, 4, 48, TOKENS), b(12, 128, 256), b(24, 256, 128), b(CAPS, 2, 128, WIDE), b(WIDE, 1024),
            b(CAPS, 2, 128, 2 * WIDE), b(*big), b(*big), b(*big), b(*big),
            b(*big), b(*big), b(*big), b(CAPS, 128, WIDE), f(2, 128, 256), f(5, 24, WIDE), b(4, 48, WIDE),
            dma((15,)), dma((16,)), dma((3,)), dma((10,)), dma((10,)),
            dma((16, 4)), dma((16, 4)), dma((4,)), dma((4,)), pltpu.SemaphoreType.REGULAR((2,)),
        ],
        compiler_params=pltpu.CompilerParams(
            collective_id=0, has_side_effects=True, vmem_limit_bytes=63 * 2**20
        ),
        name="layers",
    )(*[x for x, _ in operands])


def finish_kernel(dp_ref, h, gin, img, shards, vec, *outs):
    (
        o_h, o_in, o_img, o_ag, o_as, o_proj, o_qb, o_vb, o_wo, o_ob, o_fg, o_fs, o_we, o_eb, o_wr, o_rb,
        o_cg, o_cs, o_cq, o_cqb, o_ck, o_cv, o_cvb, o_co, o_cob,
    ) = outs
    dp = dp_ref[0]
    o_h[...] = h[...].reshape(o_h.shape)
    o_in[...] = gin[...].reshape(o_in.shape)
    o_img[...] = img[...].astype(F32)
    for j in range(3):
        o_proj[0, :, WIDE * j : WIDE * (j + 1)] = shards[8 + j].astype(F32)
    o_wo[0] = shards[11].astype(F32)
    for j in range(4):
        o_we[0, :, WIDE * j : WIDE * (j + 1)] = shards[4 + j].astype(F32)
        o_wr[0, 48 * j : 48 * (j + 1), :] = shards[j].astype(F32)
    for j, out in enumerate((o_cq, o_ck, o_cv, o_co)):
        out[...] = shards[12 + j].astype(F32)
    mine = pltpu.roll(vec[...], WIDE - 48 * dp, 1)
    places = (
        (o_ag, 0), (o_as, 1), (o_qb, 2), (o_vb, 3), (o_ob, 4), (o_fg, 5), (o_fs, 6), (o_rb, 7),
        (o_cg, 12), (o_cs, 13), (o_cqb, 14), (o_cvb, 15), (o_cob, 16),
    )
    for out, i in places:
        out[...] = mine[i : i + 1, :48]
    part = lax.rem(dp, 4)
    own = pltpu.roll(vec[8:16, :], WIDE - 192 * part, 1)[:4, :192]
    chosen = lax.broadcasted_iota(jnp.int32, (4, 192), 0) == lax.div(dp, 4)
    o_eb[...] = jnp.sum(jnp.where(chosen, own, 0.0), 0, keepdims=True)


def finish_outputs(parts):
    vm = pl.BlockSpec(memory_space=pltpu.VMEM)
    small = (1, 48)
    shapes = [
        (1, CAPS, SLOT, WIDE), (1, CAPS, SLOT, WIDE), (CAPS, 128, WIDE),
        small, small, (1, 48, 3 * WIDE), small, small, (1, 48, WIDE), small, small, small,
        (1, 48, 4 * WIDE), (1, 192), (1, 192, WIDE), small,
        small, small, (48, WIDE), small, (48, WIDE), (48, WIDE), small, (48, WIDE), small,
    ]
    dp = lax.axis_index("dp").astype(jnp.int32).reshape(1)
    outs = pl.pallas_call(
        finish_kernel,
        out_shape=[jax.ShapeDtypeStruct(x, BF if i == 0 else F32) for i, x in enumerate(shapes)],
        in_specs=[pl.BlockSpec(memory_space=pltpu.SMEM)] + [vm] * 5,
        out_specs=[vm] * 25,
        compiler_params=pltpu.CompilerParams(vmem_limit_bytes=40 * 2**20),
        name="finish",
    )(dp, *parts)
    outs = list(outs)
    for i in (16, 17, 19, 22, 24):
        outs[i] = outs[i].reshape(-1)
    return tuple(outs)


def body(
    tokens,
    images,
    lengths,
    cotangent,
    attend_gain,
    attend_shift,
    projections,
    query_bias,
    value_bias,
    output_weight,
    output_bias,
    feed_gain,
    feed_shift,
    expand_weight,
    expand_bias,
    reduce_weight,
    reduce_bias,
    cross_gain,
    cross_shift,
    cross_query,
    cross_query_bias,
    cross_key,
    cross_value,
    cross_value_bias,
    cross_out,
    cross_out_bias,
):
    layer = tuple(
        (
            weight[0]
            for weight in (
                attend_gain,
                attend_shift,
                projections,
                query_bias,
                value_bias,
                output_weight,
                output_bias,
                feed_gain,
                feed_shift,
                expand_weight,
                expand_bias,
                reduce_weight,
                reduce_bias,
            )
        )
    )
    cross = (
        cross_gain,
        cross_shift,
        cross_query,
        cross_query_bias,
        cross_key,
        cross_value,
        cross_value_bias,
        cross_out,
        cross_out_bias,
    )
    pair_weight = jnp.concatenate([cross_key, cross_value], 1)
    pair_bias = jnp.concatenate([jnp.zeros_like(cross_value_bias), cross_value_bias], 0)
    section_index = lax.axis_index("section")
    is_two = section_index == 1
    block = MB_CAPS
    half = images.shape[1]
    slots = tokens.shape[1]
    width = tokens.shape[2]
    positions = jnp.arange(slots, dtype=jnp.int32)
    causal = positions[None, :] <= positions[:, None]
    zero_cross = tuple((jnp.zeros(weight.shape, jnp.float32) for weight in cross))

    def image_project(image_rows):
        return (product(image_rows, pair_weight) + pair_bias).astype(jnp.bfloat16)

    def image_back(image_rows, dpairs):
        dimages = back_product(dpairs, pair_weight)
        pair_grad = weight_product(image_rows, dpairs)
        return (
            dimages,
            (pair_grad[:, :width], pair_grad[:, width:], column_sum(dpairs[..., width:])),
        )

    def cross_yes(hidden, image_data):
        pairs = image_project(image_data)
        after, saved = cross_forward(hidden, pairs, cross)
        return (after, saved, pairs)

    def cross_no(hidden, image_data):
        saved = (
            jnp.zeros((block, slots, width), jnp.float32),
            jnp.zeros((block, slots, 1), jnp.float32),
            jnp.zeros((block, slots, width), jnp.bfloat16),
            jnp.zeros((block, slots, width), jnp.bfloat16),
            jnp.zeros((block, slots, width), jnp.bfloat16),
            jnp.zeros((block, HEADS, slots, 1), jnp.float32),
        )
        return (hidden, saved, jnp.zeros((block, 2 * half, 2 * width), jnp.bfloat16))

    def back_yes(grad, saved, pairs, image_data):
        dgrad, parts, dpairs = cross_back(grad, saved, pairs, cross)
        dimages, image_terms = image_back(image_data, dpairs)
        return (dgrad, parts[:4] + image_terms + parts[4:], dimages)

    def back_no(grad, saved, pairs, image_data):
        return (grad, zero_cross, jnp.zeros((block, 2 * half, width), jnp.float32))

    received = jnp.zeros((block, slots, width), jnp.bfloat16)
    arriving = jnp.zeros((block, half, width), jnp.bfloat16)
    finished = jnp.zeros(tokens.shape, jnp.bfloat16)
    kept = []
    for tick in range(MICRO + 1):
        index = jnp.clip(tick - section_index, 0, MICRO - 1)
        start = index * block
        live = positions[None, :] < lax.dynamic_slice_in_dim(lengths, start, block, 0)[:, None]
        mask = live[:, None, :] & causal[None]
        own_tokens = lax.dynamic_slice_in_dim(tokens, start, block, 0)
        own_images = lax.dynamic_slice_in_dim(images, start, block, 0)
        hidden = jnp.where(is_two, received, own_tokens).astype(jnp.float32)
        after_self, self_saved = self_forward(hidden, layer, mask)
        image_data = jnp.concatenate([arriving, own_images], 1)
        after_cross, cross_saved, pairs = lax.cond(
            is_two, cross_yes, cross_no, after_self, image_data
        )
        final, feed_saved = feed_forward(after_cross, layer)
        result = final.astype(jnp.bfloat16)
        finished = lax.dynamic_update_slice_in_dim(finished, result, start, 0)
        kept.append((mask, live, self_saved, cross_saved, feed_saved, pairs, image_data))
        if tick < MICRO:
            received = shifted(result, "section", 1)
            arriving = shifted(own_images, "section", 1)
    layer_sums = tuple((jnp.zeros(weight.shape, jnp.float32) for weight in layer))
    cross_sums = zero_cross
    input_grads = jnp.zeros(tokens.shape, jnp.float32)
    image_grads = jnp.zeros(images.shape, jnp.float32)
    returning = jnp.zeros((block, slots, width), jnp.bfloat16)
    coming = jnp.zeros((block, half, width), jnp.float32)
    for turn in range(MICRO + 1):
        tick = MICRO - turn
        offset = tick - section_index
        index = jnp.clip(offset, 0, MICRO - 1)
        start = index * block
        valid = ((offset >= 0) & (offset < MICRO)).astype(jnp.float32)
        mask, live, self_saved, cross_saved, feed_saved, pairs, image_data = kept[tick]
        own_images = lax.dynamic_slice_in_dim(images, start, block, 0)
        seed_grad = lax.dynamic_slice_in_dim(cotangent[0], start, block, 0).astype(
            jnp.float32
        ) * live[..., None].astype(jnp.float32)
        grad = seed_grad + returning.astype(jnp.float32)
        grad, feed_grads = feed_back(grad, feed_saved, layer)
        grad, cross_grads, image_part = lax.cond(
            is_two, back_yes, back_no, grad, cross_saved, pairs, image_data
        )
        grad, self_grads = self_back(grad, self_saved, layer, mask)
        layer_sums = tuple(
            (total + valid * part for total, part in zip(layer_sums, self_grads + feed_grads))
        )
        cross_sums = tuple((total + valid * part for total, part in zip(cross_sums, cross_grads)))
        sent = grad.astype(jnp.bfloat16)
        stored = jnp.where(is_two, sent.astype(jnp.float32), grad)
        input_grads = jnp.where(
            valid > 0, lax.dynamic_update_slice_in_dim(input_grads, stored, start, 0), input_grads
        )
        own_dimages = jnp.where(is_two, image_part[:, half:], coming)
        image_grads = jnp.where(
            valid > 0,
            lax.dynamic_update_slice_in_dim(image_grads, own_dimages, start, 0),
            image_grads,
        )
        if turn < MICRO:
            returning = shifted(sent, "section", -1)
            coming = shifted(image_part[:, :half].astype(jnp.bfloat16), "section", -1).astype(
                jnp.float32
            )
    shared = lax.psum_scatter(
        tuple((total[None] for total in layer_sums)), "dp", scatter_dimension=1, tiled=True
    )
    scattered = lax.psum_scatter(cross_sums, "dp", scatter_dimension=0, tiled=True)
    crossed = jax.tree.map(
        lambda part: part.astype(jnp.float32), lax.psum(for_sending(tuple(scattered)), "section")
    )
    return (finished[None], input_grads[None], image_grads) + tuple(shared) + tuple(crossed)


def one_kernel(*args):
    return finish_outputs(mega(args))


def solution(mesh):
    placed = (
        P("dp", None, None),
        P("dp", "section", None),
        P("dp"),
        P("section", "dp", None, None),
        P("section", None),
        P("section", None),
        P("section", None, None),
        P("section", None),
        P("section", None),
        P("section", None, None),
        P("section", None),
        P("section", None),
        P("section", None),
        P("section", None, None),
        P("section", None),
        P("section", None, None),
        P("section", None),
        P(),
        P(),
        P(),
        P(),
        P(),
        P(),
        P(),
        P(),
        P(),
    )
    return jax.shard_map(
        one_kernel if mesh.shape["dp"] == 16 else body,
        mesh=mesh,
        in_specs=placed,
        out_specs=(
            P("section", "dp", None, None),
            P("section", "dp", None, None),
            P("dp", "section", None),
            P("section", "dp"),
            P("section", "dp"),
            P("section", "dp", None),
            P("section", "dp"),
            P("section", "dp"),
            P("section", "dp", None),
            P("section", "dp"),
            P("section", "dp"),
            P("section", "dp"),
            P("section", "dp", None),
            P("section", "dp"),
            P("section", "dp", None),
            P("section", "dp"),
            P("dp"),
            P("dp"),
            P("dp", None),
            P("dp"),
            P("dp", None),
            P("dp", None),
            P("dp"),
            P("dp", None),
            P("dp"),
        ),
        check_vma=False,
    )
```

```python
import itertools

import jax
import jax.numpy as jnp
from jax import lax
from jax.experimental import pallas as pl
from jax.experimental.pallas import tpu as pltpu
from jax.sharding import PartitionSpec as P

HEADS = 12
HEAD_DIM = 64
MB_CAPS = 4
MICRO = 1


EPS = 1e-05
NEG = -1000000000.0


def shifted(block, axis, distance):
    devices = range(lax.axis_size(axis))
    route = [(i - distance, i) for i in devices if i - distance in devices]
    return lax.ppermute(block, axis, route)


def for_sending(array):
    return jax.tree.map(lambda a: a.astype(jnp.bfloat16) if a.dtype == jnp.float32 else a, array)


def layer_norm(rows, gain, shift):
    mean = jnp.mean(rows, -1, keepdims=True)
    centred = rows - mean
    inverse = lax.rsqrt(jnp.mean(centred * centred, -1, keepdims=True) + EPS)
    normed = centred * inverse
    return (normed * gain + shift, normed, inverse)


def norm_back(grad, normed, inverse, gain):
    scaled = grad * gain
    inner = (
        scaled
        - jnp.mean(scaled, -1, keepdims=True)
        - normed * jnp.mean(scaled * normed, -1, keepdims=True)
    )
    return (inverse * inner, jnp.sum(grad * normed, axis=(0, 1)), jnp.sum(grad, axis=(0, 1)))


def product(rows, weight):
    return jnp.einsum("bsi,ij->bsj", rows, weight, preferred_element_type=jnp.float32)


def back_product(grad, weight):
    return jnp.einsum("bsj,ij->bsi", grad, weight, preferred_element_type=jnp.float32)


def weight_product(rows, grad):
    return jnp.einsum("bsi,bsj->ij", rows, grad, preferred_element_type=jnp.float32)


def column_sum(grad):
    return jnp.sum(grad.astype(jnp.float32), axis=(0, 1))


def split_heads(rows):
    return rows.reshape(rows.shape[0], rows.shape[1], HEADS, HEAD_DIM)


def scores_of(query, keys, mask):
    scores = jnp.einsum(
        "bqhd,bkhd->bhqk", split_heads(query), split_heads(keys), preferred_element_type=jnp.float32
    ) * HEAD_DIM ** (-0.5)
    if mask is None:
        return scores
    return jnp.where(mask[:, None], scores, NEG)


def attend(query, keys, values, mask):
    scores = scores_of(query, keys, mask)
    top = jnp.max(scores, -1, keepdims=True)
    expo = jnp.exp(scores - top)
    total = jnp.sum(expo, -1, keepdims=True)
    probs = (expo / total).astype(jnp.bfloat16)
    mixed = jnp.einsum(
        "bhqk,bkhd->bqhd", probs, split_heads(values), preferred_element_type=jnp.float32
    )
    return (mixed.reshape(query.shape).astype(jnp.bfloat16), top + jnp.log(total))


def attend_back(grad, query, keys, values, logsum, mask):
    scale = HEAD_DIM ** (-0.5)
    probs = jnp.exp(scores_of(query, keys, mask) - logsum)
    grad_heads = split_heads(grad)
    dprobs = jnp.einsum(
        "bqhd,bkhd->bhqk", grad_heads, split_heads(values), preferred_element_type=jnp.float32
    )
    rowdot = jnp.sum(probs * dprobs, -1, keepdims=True)
    dscores = (probs * (dprobs - rowdot)).astype(jnp.bfloat16)
    dquery = (
        jnp.einsum(
            "bhqk,bkhd->bqhd", dscores, split_heads(keys), preferred_element_type=jnp.float32
        )
        * scale
    )
    dkeys = (
        jnp.einsum(
            "bhqk,bqhd->bkhd", dscores, split_heads(query), preferred_element_type=jnp.float32
        )
        * scale
    )
    dvalues = jnp.einsum(
        "bhqk,bqhd->bkhd",
        probs.astype(jnp.bfloat16),
        grad_heads,
        preferred_element_type=jnp.float32,
    )
    return (
        dquery.reshape(query.shape).astype(jnp.bfloat16),
        dkeys.reshape(keys.shape).astype(jnp.bfloat16),
        dvalues.reshape(values.shape).astype(jnp.bfloat16),
    )


def self_forward(hidden, layer, mask):
    normal, normed, inverse = layer_norm(hidden, layer[0], layer[1])
    entry = normal.astype(jnp.bfloat16)
    packed = product(entry, layer[2])
    width = hidden.shape[-1]
    query = (packed[..., :width] + layer[3]).astype(jnp.bfloat16)
    keys = packed[..., width : 2 * width].astype(jnp.bfloat16)
    values = (packed[..., 2 * width :] + layer[4]).astype(jnp.bfloat16)
    mixed, logsum = attend(query, keys, values, mask)
    after = hidden + (product(mixed, layer[5]) + layer[6])
    return (after, (normed, inverse, entry, query, keys, values, mixed, logsum))


def self_back(grad, saved, layer, mask):
    normed, inverse, entry, query, keys, values, mixed, logsum = saved
    branch = grad.astype(jnp.bfloat16)
    out_weight_grad = weight_product(mixed, branch)
    out_bias_grad = column_sum(branch)
    dmixed = back_product(branch, layer[5]).astype(jnp.bfloat16)
    dquery, dkeys, dvalues = attend_back(dmixed, query, keys, values, logsum, mask)
    dpacked = jnp.concatenate([dquery, dkeys, dvalues], -1)
    packed_grad = weight_product(entry, dpacked)
    dentry = back_product(dpacked, layer[2])
    dhidden, gain_grad, shift_grad = norm_back(dentry, normed, inverse, layer[0])
    return (
        grad + dhidden,
        (
            gain_grad,
            shift_grad,
            packed_grad,
            column_sum(dquery),
            column_sum(dvalues),
            out_weight_grad,
            out_bias_grad,
        ),
    )


def gelu_slope(expanded):
    normal_cdf = 0.5 * (1.0 + jax.scipy.special.erf(expanded * 0.7071067811865476))
    return normal_cdf + expanded * jnp.exp(-0.5 * expanded * expanded) * 0.3989422804014327


def feed_forward(hidden, layer):
    normal, normed, inverse = layer_norm(hidden, layer[7], layer[8])
    entry = normal.astype(jnp.bfloat16)
    expanded = product(entry, layer[9]) + layer[10]
    active = jax.nn.gelu(expanded, approximate=False).astype(jnp.bfloat16)
    after = hidden + (product(active, layer[11]) + layer[12])
    return (after, (normed, inverse, entry, expanded, active))


def feed_back(grad, saved, layer):
    normed, inverse, entry, expanded, active = saved
    branch = grad.astype(jnp.bfloat16)
    reduce_grad = weight_product(active, branch)
    reduce_bias_grad = column_sum(branch)
    dactive = back_product(branch, layer[11])
    dexpanded = (dactive * gelu_slope(expanded)).astype(jnp.bfloat16)
    expand_grad = weight_product(entry, dexpanded)
    expand_bias_grad = column_sum(dexpanded)
    dentry = back_product(dexpanded, layer[9])
    dhidden, gain_grad, shift_grad = norm_back(dentry, normed, inverse, layer[7])
    return (
        grad + dhidden,
        (gain_grad, shift_grad, expand_grad, expand_bias_grad, reduce_grad, reduce_bias_grad),
    )


def cross_forward(hidden, pairs, cross):
    normal, normed, inverse = layer_norm(hidden, cross[0], cross[1])
    entry = normal.astype(jnp.bfloat16)
    query = (product(entry, cross[2]) + cross[3]).astype(jnp.bfloat16)
    width = hidden.shape[-1]
    mixed, logsum = attend(query, pairs[..., :width], pairs[..., width:], None)
    after = hidden + (product(mixed, cross[7]) + cross[8])
    return (after, (normed, inverse, entry, query, mixed, logsum))


def cross_back(grad, saved, pairs, cross):
    normed, inverse, entry, query, mixed, logsum = saved
    width = grad.shape[-1]
    branch = grad.astype(jnp.bfloat16)
    out_grad = weight_product(mixed, branch)
    out_bias_grad = column_sum(branch)
    dmixed = back_product(branch, cross[7]).astype(jnp.bfloat16)
    dquery, dkeys, dvalues = attend_back(
        dmixed, query, pairs[..., :width], pairs[..., width:], logsum, None
    )
    query_grad = weight_product(entry, dquery)
    dentry = back_product(dquery, cross[2])
    dhidden, gain_grad, shift_grad = norm_back(dentry, normed, inverse, cross[0])
    parts = (gain_grad, shift_grad, query_grad, column_sum(dquery), out_grad, out_bias_grad)
    return (grad + dhidden, parts, jnp.concatenate([dkeys, dvalues], -1))


BF = jnp.bfloat16
F32 = jnp.float32
WIDE = 768
TOKENS = 256
CAPS = 4
SLOT = 64
PAIRS = 6
MESH = pl.DeviceIdType.MESH
LEAD = (2, 2, 2, 2)


def nn(a, b):
    return lax.dot_general(a, b, (((1,), (0,)), ((), ())), preferred_element_type=F32)


def nt(a, b):
    return lax.dot_general(a, b, (((1,), (1,)), ((), ())), preferred_element_type=F32)


def tn(a, b):
    return lax.dot_general(a, b, (((0,), (0,)), ((), ())), preferred_element_type=F32)


def rows_of(i, size):
    return pl.ds(pl.multiple_of(i * size, size), size)


def erf(x):
    return lax.erf(x)


def norm_rows(source, gain, shift, normed, inverse, entry):
    for i in range(TOKENS // 32):
        r = pl.ds(32 * i, 32)
        x = source[r, :]
        centred = x - jnp.mean(x, -1, keepdims=True)
        inv = lax.rsqrt(jnp.mean(centred * centred, -1, keepdims=True) + EPS)
        n = centred * inv
        normed[r, :] = n.astype(normed.dtype)
        inverse[r, :] = inv
        entry[r, :] = (n * gain[...] + shift[...]).astype(BF)


def norm_rows_back(grad_entry, normed, inverse, gain, grad, vec, gain_row, shift_row):
    by_gain = jnp.zeros((8, WIDE), F32)
    by_shift = jnp.zeros((8, WIDE), F32)
    for i in range(TOKENS // 32):
        r = pl.ds(32 * i, 32)
        d = grad_entry[r, :]
        n = normed[r, :].astype(F32)
        scaled = d * gain[...]
        first = jnp.mean(scaled, -1, keepdims=True)
        second = jnp.mean(scaled * n, -1, keepdims=True)
        grad[r, :] = grad[r, :] + inverse[r, :] * (scaled - first - n * second)
        dn = d * n
        by_gain = by_gain + jnp.sum(dn.reshape(4, 8, WIDE), 0)
        by_shift = by_shift + jnp.sum(d.reshape(4, 8, WIDE), 0)
    vec[gain_row : gain_row + 1, :] = jnp.sum(by_gain, 0, keepdims=True)
    vec[shift_row : shift_row + 1, :] = jnp.sum(by_shift, 0, keepdims=True)


def sum_columns(rows, count):
    total = jnp.zeros((8, WIDE), F32)
    for i in range(TOKENS // 32):
        for k in range(count):
            part = rows(k, pl.ds(32 * i, 32)).astype(F32)
            total = total + jnp.sum(part.reshape(4, 8, WIDE), 0)
    return jnp.sum(total, 0, keepdims=True)


def mega_kernel(
    lengths, tokens, cotangent, images, h_proj, h_out, h_exp, h_red, h_cq, h_ck, h_cv, h_co,
    again, ashift, qbias, vbias, obias, fgain, fshift, rbias, ebias, cgain, cshift, cqbias, cvbias, cobias,
    out_all,
    GG, WP, WO, WC, R0, R1, RZ, R2, R3,
    H, G, D, N1, N2, N3, I1, I2, I3, E, ET1, ET2, ET3,
    QKV, M, MT, QC, CT, SL, AT, PT, PC, IM, KV, B1, B2, B3,
    HB, HIN, MASK, VL, YS, VS, VB, PV,
    wsem, psem, lsem, osem, ysend, yrecv, send_sem, recv_sem, vsend, vrecv, credit,
):
    section = lax.axis_index("section")
    dp = lax.axis_index("dp")
    one = section == 0
    two = section == 1
    bits = [lax.rem(lax.div(dp, 1 << k), 2) for k in range(4)]
    partners = [dp + (1 << k) * (1 - 2 * bits[k]) for k in range(4)]

    barrier = pltpu.get_barrier_semaphore()
    for partner in partners:
        pl.semaphore_signal(barrier, inc=1, device_id={"dp": partner}, device_id_type=MESH)
    pl.semaphore_signal(barrier, inc=1, device_id={"section": 1 - section}, device_id_type=MESH)

    def across(source, target, i):
        return pltpu.make_async_remote_copy(
            src_ref=source, dst_ref=target, send_sem=ysend.at[i], recv_sem=yrecv.at[i],
            device_id={"section": 1 - section}, device_id_type=MESH,
        )

    store_h = pltpu.make_async_copy(HB, out_all.at[0:TOKENS], osem.at[0])
    late_h = pltpu.make_async_copy(M, out_all.at[0:TOKENS], osem.at[0])
    store_in = pltpu.make_async_copy(HB, out_all.at[TOKENS : 2 * TOKENS], osem.at[1])
    images_a = across(images.at[0:2], IM.at[0:2, 0], 0)
    images_b = across(images.at[2:4], IM.at[2:4, 0], 1)
    send_h = across(HB, HIN, 2)
    send_d = across(HB, HIN, 3)
    send_i = across(IM.at[:, 0], KV.at[:, 0, :, :WIDE], 4)

    def load(source, target, i):
        return pltpu.make_async_copy(source, target, wsem.at[i])

    own_images = load(images, IM.at[:, 1], 0)
    own_tokens = load(tokens, HIN, 15)
    own_cotangent = load(cotangent, B1, 16)
    loads = {
        "cross": [load(w, WC.at[i], 1 + i) for i, w in enumerate((h_cq, h_ck, h_cv, h_co))],
        "proj": [load(h_proj, WP, 5)],
        "out": [load(h_out, WO, 6)],
        "exp": [
            load(h_exp.at[:, :, :, :, :, pl.ds(WIDE * j, WIDE)], GG.at[12 + j], 7 + j)
            for j in range(4)
        ],
        "red": [load(h_red.at[j], GG.at[8 + j], 11 + j) for j in range(4)],
    }

    @pl.when(one)
    def _():
        own_tokens.start()

    small = [again, ashift, qbias, vbias, obias, fgain, fshift, rbias]
    small = [(v, PV.at[i : i + 1]) for i, v in enumerate(small)]
    small += [(ebias.at[:, pl.ds(WIDE * j, WIDE)], PV.at[8 + j : 9 + j]) for j in range(4)]
    small += [(v, PV.at[12 + i]) for i, v in enumerate((cgain, cshift, cqbias, cvbias, cobias))]
    small = [pltpu.make_async_copy(v, row, psem.at[i]) for i, (v, row) in enumerate(small)]

    @pl.when(two)
    def _():
        own_images.start()
        for i in (1, 2, 0, 3):
            loads["cross"][i].start()

    for name in ("proj", "out", "exp", "red"):
        for copy in loads[name]:
            copy.start()

    own_cotangent.start()
    for copy in small:
        copy.start()
    again, ashift, qbias, vbias, obias, fgain, fshift, rbias = (PV.at[i : i + 1] for i in range(8))
    cgain, cshift, cqbias, cvbias, cobias = (PV.at[i : i + 1] for i in range(12, 17))

    def arrived(name):
        for copy in loads[name]:
            copy.wait()

    VS[...] = jnp.zeros_like(VS)
    low_lane = lax.broadcasted_iota(jnp.int32, (1, 128), 1) < SLOT
    keep_low = low_lane.astype(F32).astype(BF)
    keep_high = jnp.logical_not(low_lane).astype(F32).astype(BF)

    def stacked(x):
        return jnp.concatenate([x * keep_low, x * keep_high], 0)

    def unstacked(x):
        half = x.shape[0] // 2
        return jnp.where(low_lane, x[:half], x[half:])

    eighth = jnp.asarray(0.125, BF)

    pl.semaphore_wait(barrier, 5)

    @pl.when(one)
    def _():
        images_a.start()

    for pair in range(2):
        key = lax.broadcasted_iota(jnp.int32, (128, 256), 0)
        query = lax.rem(lax.broadcasted_iota(jnp.int32, (128, 256), 1), 128)
        first = key < SLOT
        length = jnp.where(first, lengths[2 * pair], lengths[2 * pair + 1] + SLOT)
        same = first == (query < SLOT)
        MASK[pair] = jnp.where(same & (key <= query) & (key < length), 1.0, 0.0)

    for copy in small:
        copy.wait()

    own_cotangent.wait()
    for c in range(CAPS):
        r = pl.ds(SLOT * c, SLOT)
        live = lax.broadcasted_iota(jnp.int32, (SLOT, 1), 0) < lengths[c]
        G[r, :] = jnp.where(live, B1[r, :].astype(F32), 0.0)
    B1[...] = G[...].astype(BF)

    def pair_rows(which, half):
        rows = IM[2 * which : 2 * which + 2, half].reshape(TOKENS, WIDE)
        keys = nn(rows, WC[1])
        KV[2 * which : 2 * which + 2, half, :, :WIDE] = keys.astype(BF).reshape(2, 128, WIDE)
        values = nn(rows, WC[2]) + cvbias[...]
        KV[2 * which : 2 * which + 2, half, :, WIDE:] = values.astype(BF).reshape(2, 128, WIDE)

    @pl.when(two)
    def _():
        for copy in loads["cross"]:
            copy.wait()
        own_images.wait()
        for which in range(2):
            pair_rows(which, 1)
        images_a.wait_recv()
        pair_rows(0, 0)
        arrived("red")
        VS[7:8, :] = sum_columns(lambda k, r: B1[r, :], 1)
        for j in range(4):
            SL[j] = nt(B1[...], GG[8 + j].reshape(WIDE, WIDE)).astype(BF)
        send_h.wait_recv()
        H[...] = HIN[...].astype(F32)

    @pl.when(one)
    def _():
        own_tokens.wait()
        H[...] = HIN[...].astype(F32)

    @pl.when(one)
    def _():
        SL[...] = jnp.ones_like(SL)

    norm_rows(H, again, ashift, N1, I1, E)
    ET1[...] = E[...].T
    arrived("proj")
    QKV[0] = (nn(E[...], WP[:, 0:WIDE]) + qbias[...]).astype(BF)
    QKV[1] = nn(E[...], WP[:, WIDE : 2 * WIDE]).astype(BF)
    QKV[2] = (nn(E[...], WP[:, 2 * WIDE :]) + vbias[...]).astype(BF)

    def softmax_keys(scores):
        expo = jnp.exp(scores - jnp.max(scores, 0, keepdims=True))
        return expo * (1.0 / jnp.sum(expo, 0, keepdims=True))

    for hp in range(PAIRS):
        cols = pl.ds(128 * hp, 128)
        for pair in range(2):
            rows = pl.ds(pair * 128, 128)
            query = stacked(QKV[0, rows, cols] * eighth)
            scores = nt(QKV[1, rows, cols], query)
            scores = jnp.where(MASK[pair] > 0.0, scores, NEG)
            probs = softmax_keys(scores).astype(BF)
            PT[2 * hp + pair] = probs
            M[rows, cols] = unstacked(tn(probs, QKV[2, rows, cols])).astype(BF)

    MT[...] = M[...].T
    arrived("out")
    H[...] = H[...] + (nn(M[...], WO[...]) + obias[...])

    @pl.when(two)
    def _():
        norm_rows(H, cgain, cshift, N2, I2, E)
        ET2[...] = E[...].T
        QC[...] = (nn(E[...], WC[0]) + cqbias[...]).astype(BF)

    @pl.when(two)
    def _():
        images_b.wait_recv()

    @pl.when(two)
    def _():
        pair_rows(1, 0)

    @pl.when(two)
    def _():
        for hp in range(PAIRS):
            cols = pl.ds(128 * hp, 128)
            vcols = pl.ds(WIDE + 128 * hp, 128)
            for c in range(CAPS):
                rows = pl.ds(c * SLOT, SLOT)
                query = stacked(QC[rows, cols] * eighth)
                keys = KV[c, :, :, cols].reshape(256, 128)
                probs = softmax_keys(nt(keys, query)).astype(BF)
                PC[4 * hp + c] = probs
                values = KV[c, :, :, vcols].reshape(256, 128)
                M[rows, cols] = unstacked(tn(probs, values)).astype(BF)

    @pl.when(two)
    def _():
        CT[...] = M[...].T
        H[...] = H[...] + (nn(M[...], WC[3]) + cobias[...])

    norm_rows(H, fgain, fshift, N3, I3, E)
    ET3[...] = E[...].T
    arrived("exp")

    def widen(j):
        for t in range(3):
            cols = pl.ds(256 * t, 256)
            u = nn(E[...], GG[12 + j, :, :, :, :, :, cols].reshape(WIDE, 256)) + PV[8 + j : 9 + j, cols]
            cdf = 0.5 * (1.0 + erf(u * 0.7071067811865476))
            M[:, cols] = (u * cdf).astype(BF)
            slope = cdf + u * jnp.exp(-0.5 * u * u) * 0.3989422804014327
            SL[j, :, cols] = (SL[j, :, cols].astype(F32) * slope).astype(BF)
        AT[4 * j : 4 * j + 4] = M[...].T.reshape(4, 4, 48, TOKENS)

    @pl.when(one)
    def _():
        arrived("red")
        H[...] = H[...] + rbias[...]
        for j in range(4):
            widen(j)
            H[...] = H[...] + nn(M[...], GG[8 + j].reshape(WIDE, WIDE))
        HB[...] = H[...].astype(BF)
        send_h.start()
        store_h.start()
        send_h.wait_send()
        images_a.wait_send()
        images_b.start()

    @pl.when(two)
    def _():
        for j in range(4):
            widen(j)

    @pl.when(one)
    def _():
        send_d.wait_recv()
        G[...] = G[...] + HIN[...].astype(F32)
        B1[...] = G[...].astype(BF)

    def images_out(source, what):
        for c in range(CAPS):
            target = out_all.at[2 * TOKENS + 128 * c : 2 * TOKENS + 128 * (c + 1)]
            getattr(pltpu.make_async_copy(source.at[c], target, osem.at[2 + c]), what)()

    def shard_place(c):
        return out_all.at[pl.ds(pl.multiple_of(4 * TOKENS + 48 * c, 16), 48)]

    def order(p):
        return (0, 2, 1, 3) if p % 4 == 0 else (0, 1, 2, 3)

    def chunk(p):
        return p if p < 8 else jnp.where(one, p + 4, p)

    def where(p, k, bit):
        done, now = order(p)[:k], order(p)[k]
        places = [bits[a] if a in done else bit if a == now else slice(None) for a in (3, 2, 1, 0)]
        return (chunk(p), *places)

    def landing(p, k):
        if k == 0:
            return R0.at[p % 8]
        if k == 1:
            return RZ.at[p // 4] if p % 4 == 0 else R1.at[(p // 4 % 2) * 3 + p % 4 - 1]
        return (R2 if k == 2 else R3).at[p]

    def exchange(p, k):
        axis = order(p)[k]
        return pltpu.make_async_remote_copy(
            src_ref=GG.at[where(p, k, 1 - bits[axis])], dst_ref=landing(p, k),
            send_sem=send_sem.at[p, k], recv_sem=recv_sem.at[p, k],
            device_id={"dp": partners[axis]}, device_id_type=MESH,
        )

    def reused(p, k):
        return k == 0 or (k == 1 and p % 4 > 0)

    def begin(p, k):
        if reused(p, k) and p >= 8:
            pl.semaphore_wait(credit.at[k], 1)
        exchange(p, k).start()

    def finish(p, k):
        exchange(p, k).wait()
        axis = order(p)[k]
        keep, term = GG.at[where(p, k, bits[axis])], landing(p, k)
        for place in itertools.product(range(2), repeat=3 - k):
            keep[place] = keep[place] + term[place]
        if reused(p, k) and p < 8:
            def give():
                pl.semaphore_signal(
                    credit.at[k], inc=1, device_id={"dp": partners[axis]}, device_id_type=MESH
                )
            give() if p < 4 else pl.when(two)(give)

    def shard(p):
        return GG.at[(chunk(p), *(bits[a] for a in (3, 2, 1, 0)))]

    def shard_out(p):
        return pltpu.make_async_copy(shard(p), shard_place(chunk(p)), lsem.at[p])

    def shard_across(p):
        return across(shard(p), YS.at[p - 8], 6 + p - 8)

    def advance(p, k):
        finish(p, k - 1)
        if k < 4:
            begin(p, k)
        else:
            shard_out(p).start()
            if 8 <= p < 12:
                pl.when(two)(lambda: shard_across(p).start())

    def go(p, k):
        if p >= 12:
            pl.when(two)(lambda: advance(p, k) if k else begin(p, 0))
        elif k:
            advance(p, k)
        else:
            begin(p, 0)

    def sum_copy(k):
        return pltpu.make_async_remote_copy(
            src_ref=VS, dst_ref=VL.at[k], send_sem=vsend.at[k], recv_sem=vrecv.at[k],
            device_id={"dp": partners[k]}, device_id_type=MESH,
        )

    def weight_gradient(c, left, right):
        for t in range(3):
            part = nn(left, right(pl.ds(256 * t, 256)))
            GG[c, :, :, :, :, :, pl.ds(256 * t, 256)] = part.astype(BF).reshape(LEAD + (48, 256))


    for i in range(4):
        weight_gradient(i, AT[:, i].reshape(WIDE, TOKENS), lambda t: B1[:, t])
        go(i, 0)
        if i > 0:
            go(i - 1, 1)

    @pl.when(one)
    def _():
        for j in range(4):
            for i in range(2):
                r = pl.ds(128 * i, 128)
                da = nt(B1[r, :], GG[8 + j].reshape(WIDE, WIDE))
                SL[j, r, :] = (da * SL[j, r, :].astype(F32)).astype(BF)

    total = nt(SL[0], GG[12].reshape(WIDE, WIDE))
    for j in range(1, 4):
        total = total + nt(SL[j], GG[12 + j].reshape(WIDE, WIDE))
    D[...] = total

    norm_rows_back(D, N3, I3, fgain, G, VS, 5, 6)

    go(3, 1)

    @pl.when(two)
    def _():
        B2[...] = G[...].astype(BF)
        VS[16:17, :] = sum_columns(lambda k, r: B2[r, :], 1)
        E[...] = nt(B2[...], WC[3]).astype(BF)

    @pl.when(two)
    def _():
        for hp in range(PAIRS):
            cols = pl.ds(128 * hp, 128)
            vcols = pl.ds(WIDE + 128 * hp, 128)
            for c in range(CAPS):
                rows = pl.ds(c * SLOT, SLOT)
                query = stacked(QC[rows, cols] * eighth)
                grad = stacked(E[rows, cols])
                keys = KV[c, :, :, cols].reshape(256, 128)
                values = KV[c, :, :, vcols].reshape(256, 128)
                probs = PC[4 * hp + c]
                wide = probs.astype(F32)
                dprobs = nt(values, grad)
                dscores = (wide * (dprobs - jnp.sum(wide * dprobs, 0, keepdims=True))).astype(BF)
                KV[c, :, :, cols] = nn(dscores, query).astype(BF).reshape(2, 128, 128)
                KV[c, :, :, vcols] = nn(probs, grad).astype(BF).reshape(2, 128, 128)
                QC[rows, cols] = (unstacked(tn(dscores, keys)) * 0.125).astype(BF)

    @pl.when(two)
    def _():
        VS[14:15, :] = sum_columns(lambda k, r: QC[r, :], 1)
        D[...] = nt(QC[...], WC[0])
        norm_rows_back(D, N2, I2, cgain, G, VS, 12, 13)

    B3[...] = G[...].astype(BF)
    VS[4:5, :] = sum_columns(lambda k, r: B3[r, :], 1)
    E[...] = nt(B3[...], WO[...]).astype(BF)

    for hp in range(PAIRS):
        cols = pl.ds(128 * hp, 128)
        for pair in range(2):
            rows = pl.ds(pair * 128, 128)
            query = stacked(QKV[0, rows, cols] * eighth)
            grad = stacked(E[rows, cols])
            keys = QKV[1, rows, cols]
            probs = PT[2 * hp + pair]
            wide = probs.astype(F32)
            dprobs = nt(QKV[2, rows, cols], grad)
            dscores = (wide * (dprobs - jnp.sum(wide * dprobs, 0, keepdims=True))).astype(BF)
            QKV[1, rows, cols] = nn(dscores, query).astype(BF)
            QKV[2, rows, cols] = nn(probs, grad).astype(BF)
            QKV[0, rows, cols] = (unstacked(tn(dscores, keys)) * 0.125).astype(BF)

    VS[2:3, :] = sum_columns(lambda k, r: QKV[0, r, :], 1)
    VS[3:4, :] = sum_columns(lambda k, r: QKV[2, r, :], 1)
    D[...] = nt(QKV[0], WP[:, 0:WIDE])
    D[...] = D[...] + nt(QKV[1], WP[:, WIDE : 2 * WIDE])
    D[...] = D[...] + nt(QKV[2], WP[:, 2 * WIDE :])
    norm_rows_back(D, N1, I1, again, G, VS, 0, 1)

    @pl.when(one)
    def _():
        store_h.wait()
        VS[7:8, :] = sum_columns(lambda k, r: B1[r, :], 1)

    HB[...] = G[...].astype(BF)
    store_in.start()

    @pl.when(two)
    def _():
        send_d.start()
        H[...] = H[...] + rbias[...]
        for j in range(4):
            H[...] = H[...] + tn(AT[4 * j : 4 * j + 4].reshape(WIDE, TOKENS), GG[8 + j].reshape(WIDE, WIDE))
        M[...] = H[...].astype(BF)
        late_h.start()

    for j in range(4):
        VS[8 + j : 9 + j, :] = sum_columns(lambda k, r: SL[j, r, :], 1)

    for j in range(4):
        weight_gradient(4 + j, ET3[...], lambda t: SL[j, :, t])
        go(4 + j, 0)

    for j in range(3):
        weight_gradient(12 + j, ET1[...], lambda t: QKV[j, :, t])

    weight_gradient(15, MT[...], lambda t: B3[:, t])

    @pl.when(two)
    def _():
        weight_gradient(8, ET2[...], lambda t: QC[:, t])
        weight_gradient(11, CT[...], lambda t: B2[:, t])
        for c in range(CAPS):
            AT[4 * c : 4 * c + 4] = IM[c].reshape(256, WIDE).T.reshape(4, 4, 48, TOKENS)
        for j in range(2):
            for t in range(3):
                cols = pl.ds(WIDE * j + 256 * t, 256)
                part = sum(
                    nn(AT[4 * c : 4 * c + 4].reshape(WIDE, TOKENS), KV[c, :, :, cols].reshape(256, 256))
                    for c in range(CAPS)
                )
                GG[9 + j, :, :, :, :, :, pl.ds(256 * t, 256)] = part.astype(BF).reshape(LEAD + (48, 256))

    @pl.when(two)
    def _():
        VS[15:16, :] = sum_columns(
            lambda k, r: KV[k, :, pl.ds(r.start // 2, 16), WIDE:].reshape(32, WIDE), 4
        )
        for c in range(CAPS):
            part = nt(KV[c, :, :, :WIDE].reshape(256, WIDE), WC[1])
            part = part + nt(KV[c, :, :, WIDE:].reshape(256, WIDE), WC[2])
            IM[c] = part.astype(BF).reshape(2, 128, WIDE)

    @pl.when(two)
    def _():
        send_i.start()
        images_out(IM.at[:, 1], "start")

    for tick in range(18):
        for k, p in ((0, tick + 8), (1, tick + 4), (2, tick), (3, tick - 1), (4, tick - 2)):
            if 0 <= p < 16 and (k > 1 or p >= 4):
                go(p, k)
        if 0 < tick < 5:
            sum_copy(tick - 1).wait()
            VS[...] = VS[...] + VL[tick - 1]
        if tick < 4:
            sum_copy(tick).start()
        if tick == 4:
            pl.when(two)(lambda: across(VS, VL.at[4], 5).start())
        if tick == 9:
            @pl.when(one)
            def _():
                images_b.wait_send()
                send_i.wait_recv()
                images_out(KV.at[:, 0, :, :WIDE], "start")

    @pl.when(two)
    def _():
        across(VS, VL.at[4], 5).wait_send()
        images_out(IM.at[:, 1], "wait")
        send_d.wait_send()
        send_i.wait_send()
        late_h.wait()
        for p in range(8, 12):
            shard_across(p).wait_send()
        for p in range(12, 16):
            shard_out(p).wait()

    @pl.when(one)
    def _():
        across(VS, VL.at[4], 5).wait_recv()
        VS[12:17, :] = VL[4, 12:17, :]
        copies = [pltpu.make_async_copy(YS.at[i], shard_place(8 + i), lsem.at[12 + i]) for i in range(4)]
        for i in range(4):
            across(YS.at[i], YS.at[i], 6 + i).wait_recv()
            copies[i].start()
        for copy in copies:
            copy.wait()
        images_out(KV.at[:, 0, :, :WIDE], "wait")

    store_in.wait()
    high = VS[...].astype(BF)
    VB[0:24, :] = high
    VB[24:48, :] = (VS[...] - high.astype(F32)).astype(BF)
    store_v = pltpu.make_async_copy(VB, out_all.at[7 * TOKENS : 7 * TOKENS + 48], osem.at[6])
    store_v.start()
    store_v.wait()
    for p in range(12):
        shard_out(p).wait()


def mega(args):
    (
        tokens, images, lengths, cotangent, again, ashift, proj, qb, vb, wo, ob, fg, fs, we, eb, wr, rb,
        cg, cs, cq, cqb, ck, cv, cvb, co, cob,
    ) = args
    operands = (
        lengths, tokens.reshape(TOKENS, WIDE), cotangent.reshape(TOKENS, WIDE), images,
        proj[0], wo[0], we.reshape(LEAD + (48, 4 * WIDE)), wr.reshape((4,) + LEAD + (48, WIDE)), cq, ck, cv, co,
        again, ashift, qb, vb, ob, fg, fs, rb, eb, cg, cs, cqb, cvb, cob,
    )
    hbm = pl.BlockSpec(memory_space=pl.ANY)
    dma = pltpu.SemaphoreType.DMA
    big = (TOKENS, WIDE)
    turned = (WIDE, TOKENS)
    b = lambda *shape: pltpu.VMEM(shape, BF)
    f = lambda *shape: pltpu.VMEM(shape, F32)
    return pl.pallas_call(
        mega_kernel,
        out_shape=jax.ShapeDtypeStruct((7 * TOKENS + 48, WIDE), BF),
        in_specs=[pl.BlockSpec(memory_space=pltpu.SMEM)] + [hbm] * (len(operands) - 1),
        out_specs=hbm,
        scratch_shapes=[
            b(16, *LEAD, 48, WIDE), b(WIDE, 3 * WIDE), b(WIDE, WIDE), b(4, WIDE, WIDE),
            b(8, 2, 2, 2, 48, WIDE), b(6, 2, 2, 48, WIDE), b(4, 2, 2, 48, WIDE), b(16, 2, 48, WIDE), b(16, 48, WIDE),
            f(*big), f(*big), f(*big), b(*big), b(*big), b(*big), f(TOKENS, 1), f(TOKENS, 1), f(TOKENS, 1),
            b(*big), b(*turned), b(*turned), b(*turned),
            b(3, *big), b(*big), b(*turned), b(*big), b(*turned), b(4, *big),
            b(16, 4, 48, TOKENS), b(12, 128, 256), b(24, 256, 128), b(CAPS, 2, 128, WIDE),
            b(CAPS, 2, 128, 2 * WIDE), b(*big), b(*big), b(*big),
            b(*big), b(*big), f(2, 128, 256), f(5, 24, WIDE), b(4, 48, WIDE), f(24, WIDE), b(48, WIDE), f(24, WIDE),
            dma((17,)), dma((17,)), dma((16,)), dma((7,)), dma((10,)), dma((10,)),
            dma((16, 4)), dma((16, 4)), dma((4,)), dma((4,)), pltpu.SemaphoreType.REGULAR((2,)),
        ],
        compiler_params=pltpu.CompilerParams(
            collective_id=0, has_side_effects=True, vmem_limit_bytes=63 * 2**20
        ),
        name="layers",
    )(*operands)


def finish_kernel(dp_ref, every, *outs):
    (
        o_h, o_in, o_img, o_ag, o_as, o_proj, o_qb, o_vb, o_wo, o_ob, o_fg, o_fs, o_we, o_eb, o_wr, o_rb,
        o_cg, o_cs, o_cq, o_cqb, o_ck, o_cv, o_cvb, o_co, o_cob,
    ) = outs
    dp = dp_ref[0]
    o_h[...] = every[0:TOKENS, :].reshape(o_h.shape)
    o_in[...] = every[TOKENS : 2 * TOKENS, :].astype(F32).reshape(o_in.shape)
    o_img[...] = every[2 * TOKENS : 4 * TOKENS, :].astype(F32).reshape(o_img.shape)
    shards = [every[4 * TOKENS + 48 * j : 4 * TOKENS + 48 * (j + 1), :].astype(F32) for j in range(16)]
    vec = every[7 * TOKENS : 7 * TOKENS + 48, :].astype(F32)
    vec = vec[:24] + vec[24:]
    for j in range(3):
        o_proj[0, :, WIDE * j : WIDE * (j + 1)] = shards[12 + j]
    o_wo[0] = shards[15]
    for j in range(4):
        o_we[0, :, WIDE * j : WIDE * (j + 1)] = shards[4 + j]
        o_wr[0, 48 * j : 48 * (j + 1), :] = shards[j]
    for j, out in enumerate((o_cq, o_ck, o_cv, o_co)):
        out[...] = shards[8 + j]
    mine = pltpu.roll(vec, WIDE - 48 * dp, 1)
    places = (
        (o_ag, 0), (o_as, 1), (o_qb, 2), (o_vb, 3), (o_ob, 4), (o_fg, 5), (o_fs, 6), (o_rb, 7),
        (o_cg, 12), (o_cs, 13), (o_cqb, 14), (o_cvb, 15), (o_cob, 16),
    )
    for out, i in places:
        out[...] = mine[i : i + 1, :48]
    part = lax.rem(dp, 4)
    own = pltpu.roll(vec[8:16], WIDE - 192 * part, 1)[:4, :192]
    chosen = lax.broadcasted_iota(jnp.int32, (4, 192), 0) == lax.div(dp, 4)
    o_eb[...] = jnp.sum(jnp.where(chosen, own, 0.0), 0, keepdims=True)


def finish_outputs(every):
    vm = pl.BlockSpec(memory_space=pltpu.VMEM)
    small = (1, 48)
    shapes = [
        (1, CAPS, SLOT, WIDE), (1, CAPS, SLOT, WIDE), (CAPS, 128, WIDE),
        small, small, (1, 48, 3 * WIDE), small, small, (1, 48, WIDE), small, small, small,
        (1, 48, 4 * WIDE), (1, 192), (1, 192, WIDE), small,
        small, small, (48, WIDE), small, (48, WIDE), (48, WIDE), small, (48, WIDE), small,
    ]
    dp = lax.axis_index("dp").astype(jnp.int32).reshape(1)
    outs = pl.pallas_call(
        finish_kernel,
        out_shape=[jax.ShapeDtypeStruct(x, BF if i == 0 else F32) for i, x in enumerate(shapes)],
        in_specs=[pl.BlockSpec(memory_space=pltpu.SMEM), vm],
        out_specs=[vm] * 25,
        compiler_params=pltpu.CompilerParams(vmem_limit_bytes=40 * 2**20),
        name="finish",
    )(dp, every)
    outs = list(outs)
    for i in (16, 17, 19, 22, 24):
        outs[i] = outs[i].reshape(-1)
    return tuple(outs)


def body(
    tokens,
    images,
    lengths,
    cotangent,
    attend_gain,
    attend_shift,
    projections,
    query_bias,
    value_bias,
    output_weight,
    output_bias,
    feed_gain,
    feed_shift,
    expand_weight,
    expand_bias,
    reduce_weight,
    reduce_bias,
    cross_gain,
    cross_shift,
    cross_query,
    cross_query_bias,
    cross_key,
    cross_value,
    cross_value_bias,
    cross_out,
    cross_out_bias,
):
    layer = tuple(
        (
            weight[0]
            for weight in (
                attend_gain,
                attend_shift,
                projections,
                query_bias,
                value_bias,
                output_weight,
                output_bias,
                feed_gain,
                feed_shift,
                expand_weight,
                expand_bias,
                reduce_weight,
                reduce_bias,
            )
        )
    )
    cross = (
        cross_gain,
        cross_shift,
        cross_query,
        cross_query_bias,
        cross_key,
        cross_value,
        cross_value_bias,
        cross_out,
        cross_out_bias,
    )
    pair_weight = jnp.concatenate([cross_key, cross_value], 1)
    pair_bias = jnp.concatenate([jnp.zeros_like(cross_value_bias), cross_value_bias], 0)
    section_index = lax.axis_index("section")
    is_two = section_index == 1
    block = MB_CAPS
    half = images.shape[1]
    slots = tokens.shape[1]
    width = tokens.shape[2]
    positions = jnp.arange(slots, dtype=jnp.int32)
    causal = positions[None, :] <= positions[:, None]
    zero_cross = tuple((jnp.zeros(weight.shape, jnp.float32) for weight in cross))

    def image_project(image_rows):
        return (product(image_rows, pair_weight) + pair_bias).astype(jnp.bfloat16)

    def image_back(image_rows, dpairs):
        dimages = back_product(dpairs, pair_weight)
        pair_grad = weight_product(image_rows, dpairs)
        return (
            dimages,
            (pair_grad[:, :width], pair_grad[:, width:], column_sum(dpairs[..., width:])),
        )

    def cross_yes(hidden, image_data):
        pairs = image_project(image_data)
        after, saved = cross_forward(hidden, pairs, cross)
        return (after, saved, pairs)

    def cross_no(hidden, image_data):
        saved = (
            jnp.zeros((block, slots, width), jnp.float32),
            jnp.zeros((block, slots, 1), jnp.float32),
            jnp.zeros((block, slots, width), jnp.bfloat16),
            jnp.zeros((block, slots, width), jnp.bfloat16),
            jnp.zeros((block, slots, width), jnp.bfloat16),
            jnp.zeros((block, HEADS, slots, 1), jnp.float32),
        )
        return (hidden, saved, jnp.zeros((block, 2 * half, 2 * width), jnp.bfloat16))

    def back_yes(grad, saved, pairs, image_data):
        dgrad, parts, dpairs = cross_back(grad, saved, pairs, cross)
        dimages, image_terms = image_back(image_data, dpairs)
        return (dgrad, parts[:4] + image_terms + parts[4:], dimages)

    def back_no(grad, saved, pairs, image_data):
        return (grad, zero_cross, jnp.zeros((block, 2 * half, width), jnp.float32))

    received = jnp.zeros((block, slots, width), jnp.bfloat16)
    arriving = jnp.zeros((block, half, width), jnp.bfloat16)
    finished = jnp.zeros(tokens.shape, jnp.bfloat16)
    kept = []
    for tick in range(MICRO + 1):
        index = jnp.clip(tick - section_index, 0, MICRO - 1)
        start = index * block
        live = positions[None, :] < lax.dynamic_slice_in_dim(lengths, start, block, 0)[:, None]
        mask = live[:, None, :] & causal[None]
        own_tokens = lax.dynamic_slice_in_dim(tokens, start, block, 0)
        own_images = lax.dynamic_slice_in_dim(images, start, block, 0)
        hidden = jnp.where(is_two, received, own_tokens).astype(jnp.float32)
        after_self, self_saved = self_forward(hidden, layer, mask)
        image_data = jnp.concatenate([arriving, own_images], 1)
        after_cross, cross_saved, pairs = lax.cond(
            is_two, cross_yes, cross_no, after_self, image_data
        )
        final, feed_saved = feed_forward(after_cross, layer)
        result = final.astype(jnp.bfloat16)
        finished = lax.dynamic_update_slice_in_dim(finished, result, start, 0)
        kept.append((mask, live, self_saved, cross_saved, feed_saved, pairs, image_data))
        if tick < MICRO:
            received = shifted(result, "section", 1)
            arriving = shifted(own_images, "section", 1)
    layer_sums = tuple((jnp.zeros(weight.shape, jnp.float32) for weight in layer))
    cross_sums = zero_cross
    input_grads = jnp.zeros(tokens.shape, jnp.float32)
    image_grads = jnp.zeros(images.shape, jnp.float32)
    returning = jnp.zeros((block, slots, width), jnp.bfloat16)
    coming = jnp.zeros((block, half, width), jnp.float32)
    for turn in range(MICRO + 1):
        tick = MICRO - turn
        offset = tick - section_index
        index = jnp.clip(offset, 0, MICRO - 1)
        start = index * block
        valid = ((offset >= 0) & (offset < MICRO)).astype(jnp.float32)
        mask, live, self_saved, cross_saved, feed_saved, pairs, image_data = kept[tick]
        own_images = lax.dynamic_slice_in_dim(images, start, block, 0)
        seed_grad = lax.dynamic_slice_in_dim(cotangent[0], start, block, 0).astype(
            jnp.float32
        ) * live[..., None].astype(jnp.float32)
        grad = seed_grad + returning.astype(jnp.float32)
        grad, feed_grads = feed_back(grad, feed_saved, layer)
        grad, cross_grads, image_part = lax.cond(
            is_two, back_yes, back_no, grad, cross_saved, pairs, image_data
        )
        grad, self_grads = self_back(grad, self_saved, layer, mask)
        layer_sums = tuple(
            (total + valid * part for total, part in zip(layer_sums, self_grads + feed_grads))
        )
        cross_sums = tuple((total + valid * part for total, part in zip(cross_sums, cross_grads)))
        sent = grad.astype(jnp.bfloat16)
        stored = jnp.where(is_two, sent.astype(jnp.float32), grad)
        input_grads = jnp.where(
            valid > 0, lax.dynamic_update_slice_in_dim(input_grads, stored, start, 0), input_grads
        )
        own_dimages = jnp.where(is_two, image_part[:, half:], coming)
        image_grads = jnp.where(
            valid > 0,
            lax.dynamic_update_slice_in_dim(image_grads, own_dimages, start, 0),
            image_grads,
        )
        if turn < MICRO:
            returning = shifted(sent, "section", -1)
            coming = shifted(image_part[:, :half].astype(jnp.bfloat16), "section", -1).astype(
                jnp.float32
            )
    shared = lax.psum_scatter(
        tuple((total[None] for total in layer_sums)), "dp", scatter_dimension=1, tiled=True
    )
    scattered = lax.psum_scatter(cross_sums, "dp", scatter_dimension=0, tiled=True)
    crossed = jax.tree.map(
        lambda part: part.astype(jnp.float32), lax.psum(for_sending(tuple(scattered)), "section")
    )
    return (finished[None], input_grads[None], image_grads) + tuple(shared) + tuple(crossed)


def one_kernel(*args):
    return finish_outputs(mega(args))


def solution(mesh):
    placed = (
        P("dp", None, None),
        P("dp", "section", None),
        P("dp"),
        P("section", "dp", None, None),
        P("section", None),
        P("section", None),
        P("section", None, None),
        P("section", None),
        P("section", None),
        P("section", None, None),
        P("section", None),
        P("section", None),
        P("section", None),
        P("section", None, None),
        P("section", None),
        P("section", None, None),
        P("section", None),
        P(),
        P(),
        P(),
        P(),
        P(),
        P(),
        P(),
        P(),
        P(),
    )
    return jax.shard_map(
        one_kernel if mesh.shape["dp"] == 16 else body,
        mesh=mesh,
        in_specs=placed,
        out_specs=(
            P("section", "dp", None, None),
            P("section", "dp", None, None),
            P("dp", "section", None),
            P("section", "dp"),
            P("section", "dp"),
            P("section", "dp", None),
            P("section", "dp"),
            P("section", "dp"),
            P("section", "dp", None),
            P("section", "dp"),
            P("section", "dp"),
            P("section", "dp"),
            P("section", "dp", None),
            P("section", "dp"),
            P("section", "dp", None),
            P("section", "dp"),
            P("dp"),
            P("dp"),
            P("dp", None),
            P("dp"),
            P("dp", None),
            P("dp", None),
            P("dp"),
            P("dp", None),
            P("dp"),
        ),
        check_vma=False,
    )
```

```python
import functools
import itertools

import jax
import jax.numpy as jnp
from jax import lax
from jax.experimental import pallas as pl
from jax.experimental.pallas import tpu as pltpu
from jax.sharding import PartitionSpec as P

HEADS = 12
HEAD_DIM = 64
MB_CAPS = 4
MICRO = 1


EPS = 1e-05
NEG = -1000000000.0


def shifted(block, axis, distance):
    devices = range(lax.axis_size(axis))
    route = [(i - distance, i) for i in devices if i - distance in devices]
    return lax.ppermute(block, axis, route)


def for_sending(array):
    return jax.tree.map(lambda a: a.astype(jnp.bfloat16) if a.dtype == jnp.float32 else a, array)


def layer_norm(rows, gain, shift):
    mean = jnp.mean(rows, -1, keepdims=True)
    centred = rows - mean
    inverse = lax.rsqrt(jnp.mean(centred * centred, -1, keepdims=True) + EPS)
    normed = centred * inverse
    return (normed * gain + shift, normed, inverse)


def norm_back(grad, normed, inverse, gain):
    scaled = grad * gain
    inner = (
        scaled
        - jnp.mean(scaled, -1, keepdims=True)
        - normed * jnp.mean(scaled * normed, -1, keepdims=True)
    )
    return (inverse * inner, jnp.sum(grad * normed, axis=(0, 1)), jnp.sum(grad, axis=(0, 1)))


def product(rows, weight):
    return jnp.einsum("bsi,ij->bsj", rows, weight, preferred_element_type=jnp.float32)


def back_product(grad, weight):
    return jnp.einsum("bsj,ij->bsi", grad, weight, preferred_element_type=jnp.float32)


def weight_product(rows, grad):
    return jnp.einsum("bsi,bsj->ij", rows, grad, preferred_element_type=jnp.float32)


def column_sum(grad):
    return jnp.sum(grad.astype(jnp.float32), axis=(0, 1))


def split_heads(rows):
    return rows.reshape(rows.shape[0], rows.shape[1], HEADS, HEAD_DIM)


def scores_of(query, keys, mask):
    scores = jnp.einsum(
        "bqhd,bkhd->bhqk", split_heads(query), split_heads(keys), preferred_element_type=jnp.float32
    ) * HEAD_DIM ** (-0.5)
    if mask is None:
        return scores
    return jnp.where(mask[:, None], scores, NEG)


def attend(query, keys, values, mask):
    scores = scores_of(query, keys, mask)
    top = jnp.max(scores, -1, keepdims=True)
    expo = jnp.exp(scores - top)
    total = jnp.sum(expo, -1, keepdims=True)
    probs = (expo / total).astype(jnp.bfloat16)
    mixed = jnp.einsum(
        "bhqk,bkhd->bqhd", probs, split_heads(values), preferred_element_type=jnp.float32
    )
    return (mixed.reshape(query.shape).astype(jnp.bfloat16), top + jnp.log(total))


def attend_back(grad, query, keys, values, logsum, mask):
    scale = HEAD_DIM ** (-0.5)
    probs = jnp.exp(scores_of(query, keys, mask) - logsum)
    grad_heads = split_heads(grad)
    dprobs = jnp.einsum(
        "bqhd,bkhd->bhqk", grad_heads, split_heads(values), preferred_element_type=jnp.float32
    )
    rowdot = jnp.sum(probs * dprobs, -1, keepdims=True)
    dscores = (probs * (dprobs - rowdot)).astype(jnp.bfloat16)
    dquery = (
        jnp.einsum(
            "bhqk,bkhd->bqhd", dscores, split_heads(keys), preferred_element_type=jnp.float32
        )
        * scale
    )
    dkeys = (
        jnp.einsum(
            "bhqk,bqhd->bkhd", dscores, split_heads(query), preferred_element_type=jnp.float32
        )
        * scale
    )
    dvalues = jnp.einsum(
        "bhqk,bqhd->bkhd",
        probs.astype(jnp.bfloat16),
        grad_heads,
        preferred_element_type=jnp.float32,
    )
    return (
        dquery.reshape(query.shape).astype(jnp.bfloat16),
        dkeys.reshape(keys.shape).astype(jnp.bfloat16),
        dvalues.reshape(values.shape).astype(jnp.bfloat16),
    )


def self_forward(hidden, layer, mask):
    normal, normed, inverse = layer_norm(hidden, layer[0], layer[1])
    entry = normal.astype(jnp.bfloat16)
    packed = product(entry, layer[2])
    width = hidden.shape[-1]
    query = (packed[..., :width] + layer[3]).astype(jnp.bfloat16)
    keys = packed[..., width : 2 * width].astype(jnp.bfloat16)
    values = (packed[..., 2 * width :] + layer[4]).astype(jnp.bfloat16)
    mixed, logsum = attend(query, keys, values, mask)
    after = hidden + (product(mixed, layer[5]) + layer[6])
    return (after, (normed, inverse, entry, query, keys, values, mixed, logsum))


def self_back(grad, saved, layer, mask):
    normed, inverse, entry, query, keys, values, mixed, logsum = saved
    branch = grad.astype(jnp.bfloat16)
    out_weight_grad = weight_product(mixed, branch)
    out_bias_grad = column_sum(branch)
    dmixed = back_product(branch, layer[5]).astype(jnp.bfloat16)
    dquery, dkeys, dvalues = attend_back(dmixed, query, keys, values, logsum, mask)
    dpacked = jnp.concatenate([dquery, dkeys, dvalues], -1)
    packed_grad = weight_product(entry, dpacked)
    dentry = back_product(dpacked, layer[2])
    dhidden, gain_grad, shift_grad = norm_back(dentry, normed, inverse, layer[0])
    return (
        grad + dhidden,
        (
            gain_grad,
            shift_grad,
            packed_grad,
            column_sum(dquery),
            column_sum(dvalues),
            out_weight_grad,
            out_bias_grad,
        ),
    )


def gelu_slope(expanded):
    normal_cdf = 0.5 * (1.0 + jax.scipy.special.erf(expanded * 0.7071067811865476))
    return normal_cdf + expanded * jnp.exp(-0.5 * expanded * expanded) * 0.3989422804014327


def feed_forward(hidden, layer):
    normal, normed, inverse = layer_norm(hidden, layer[7], layer[8])
    entry = normal.astype(jnp.bfloat16)
    expanded = product(entry, layer[9]) + layer[10]
    active = jax.nn.gelu(expanded, approximate=False).astype(jnp.bfloat16)
    after = hidden + (product(active, layer[11]) + layer[12])
    return (after, (normed, inverse, entry, expanded, active))


def feed_back(grad, saved, layer):
    normed, inverse, entry, expanded, active = saved
    branch = grad.astype(jnp.bfloat16)
    reduce_grad = weight_product(active, branch)
    reduce_bias_grad = column_sum(branch)
    dactive = back_product(branch, layer[11])
    dexpanded = (dactive * gelu_slope(expanded)).astype(jnp.bfloat16)
    expand_grad = weight_product(entry, dexpanded)
    expand_bias_grad = column_sum(dexpanded)
    dentry = back_product(dexpanded, layer[9])
    dhidden, gain_grad, shift_grad = norm_back(dentry, normed, inverse, layer[7])
    return (
        grad + dhidden,
        (gain_grad, shift_grad, expand_grad, expand_bias_grad, reduce_grad, reduce_bias_grad),
    )


def cross_forward(hidden, pairs, cross):
    normal, normed, inverse = layer_norm(hidden, cross[0], cross[1])
    entry = normal.astype(jnp.bfloat16)
    query = (product(entry, cross[2]) + cross[3]).astype(jnp.bfloat16)
    width = hidden.shape[-1]
    mixed, logsum = attend(query, pairs[..., :width], pairs[..., width:], None)
    after = hidden + (product(mixed, cross[7]) + cross[8])
    return (after, (normed, inverse, entry, query, mixed, logsum))


def cross_back(grad, saved, pairs, cross):
    normed, inverse, entry, query, mixed, logsum = saved
    width = grad.shape[-1]
    branch = grad.astype(jnp.bfloat16)
    out_grad = weight_product(mixed, branch)
    out_bias_grad = column_sum(branch)
    dmixed = back_product(branch, cross[7]).astype(jnp.bfloat16)
    dquery, dkeys, dvalues = attend_back(
        dmixed, query, pairs[..., :width], pairs[..., width:], logsum, None
    )
    query_grad = weight_product(entry, dquery)
    dentry = back_product(dquery, cross[2])
    dhidden, gain_grad, shift_grad = norm_back(dentry, normed, inverse, cross[0])
    parts = (gain_grad, shift_grad, query_grad, column_sum(dquery), out_grad, out_bias_grad)
    return (grad + dhidden, parts, jnp.concatenate([dkeys, dvalues], -1))


BF = jnp.bfloat16
F32 = jnp.float32
WIDE = 768
TOKENS = 256
CAPS = 4
SLOT = 64
PAIRS = 6
MESH = pl.DeviceIdType.MESH
LEAD = (2, 2, 2, 2)
Z_FIRST = (3, 7, 11, 15)
EVENTS = (
    (0, 2), (3, 2), (16, 0), (16, 1), (16, 4), (11, 0), (16, 5), (6, 0), (11, 1), (6, 1), (16, 6), (1, 2),
    (7, 0), (5, 0), (4, 0), (2, 2), (10, 0), (7, 1), (4, 1), (0, 3), (5, 1), (9, 0), (1, 3), (9, 1), (8, 0),
    (16, 2), (8, 1), (15, 0), (2, 3), (4, 2), (16, 7), (6, 2), (5, 2), (12, 0), (3, 3), (4, 3), (14, 0),
    (9, 2), (10, 1), (1, 4), (6, 3), (16, 8), (7, 2), (13, 0), (13, 1), (5, 3), (12, 1), (8, 2), (9, 3),
    (11, 2), (16, 10), (15, 1), (8, 3), (2, 4), (10, 2), (5, 4), (16, 9), (13, 2), (7, 3), (10, 3), (8, 4),
    (14, 1), (0, 4), (12, 2), (13, 3), (11, 3), (15, 2), (4, 4), (3, 4), (12, 3), (13, 4), (9, 4), (14, 2),
    (15, 3), (10, 4), (14, 3), (7, 4), (12, 4), (6, 4), (11, 4), (15, 4), (14, 4),
)

def nn(a, b):
    return lax.dot_general(a, b, (((1,), (0,)), ((), ())), preferred_element_type=F32)


def nt(a, b):
    return lax.dot_general(a, b, (((1,), (1,)), ((), ())), preferred_element_type=F32)


def tn(a, b):
    return lax.dot_general(a, b, (((0,), (0,)), ((), ())), preferred_element_type=F32)


def rows_of(i, size):
    return pl.ds(pl.multiple_of(i * size, size), size)


def erf(x):
    return lax.erf(x)


def norm_rows(source, gain, shift, normed, inverse, entry):
    for i in range(TOKENS // 32):
        r = pl.ds(32 * i, 32)
        x = source[r, :]
        centred = x - jnp.mean(x, -1, keepdims=True)
        inv = lax.rsqrt(jnp.mean(centred * centred, -1, keepdims=True) + EPS)
        n = centred * inv
        normed[r, :] = n.astype(normed.dtype)
        inverse[r, :] = inv
        entry[r, :] = (n * gain[...] + shift[...]).astype(BF)


def norm_rows_back(grad_entry, normed, inverse, gain, grad, vec, gain_row, shift_row):
    by_gain = jnp.zeros((8, WIDE), F32)
    by_shift = jnp.zeros((8, WIDE), F32)
    for i in range(TOKENS // 32):
        r = pl.ds(32 * i, 32)
        d = grad_entry[r, :]
        n = normed[r, :].astype(F32)
        scaled = d * gain[...]
        first = jnp.mean(scaled, -1, keepdims=True)
        second = jnp.mean(scaled * n, -1, keepdims=True)
        grad[r, :] = grad[r, :] + inverse[r, :] * (scaled - first - n * second)
        dn = d * n
        by_gain = by_gain + jnp.sum(dn.reshape(4, 8, WIDE), 0)
        by_shift = by_shift + jnp.sum(d.reshape(4, 8, WIDE), 0)
    vec[gain_row : gain_row + 1, :] = jnp.sum(by_gain, 0, keepdims=True)
    vec[shift_row : shift_row + 1, :] = jnp.sum(by_shift, 0, keepdims=True)


def sum_columns(rows, count):
    total = jnp.zeros((8, WIDE), F32)
    for i in range(TOKENS // 32):
        for k in range(count):
            part = rows(k, pl.ds(32 * i, 32)).astype(F32)
            total = total + jnp.sum(part.reshape(4, 8, WIDE), 0)
    return jnp.sum(total, 0, keepdims=True)


def mega_kernel(
    lengths, tokens, cotangent, images, h_proj, h_out, h_exp, h_red, h_cq, h_ck, h_cv, h_co,
    again, ashift, qbias, vbias, obias, fgain, fshift, rbias, ebias, cgain, cshift, cqbias, cvbias, cobias,
    out_all,
    GG, WP, WO, WC, R0, R1, R2, R3,
    H, G, D, N1, N2, N3, I1, I2, I3, E, ET1, ET2, ET3,
    QKV, M, MT, QC, CT, SL, AT, PT, PC, IM, KV, B1, B2,
    HIN, MASK, YS, VS, VT, V0, V1, V2, V3, VY, VB, PV,
    wsem, psem, lsem, osem, ysend, yrecv, send_sem, recv_sem, vsend, vrecv, credit,
):
    section = lax.axis_index("section")
    dp = lax.axis_index("dp")
    one = section == 0
    two = section == 1
    bits = [lax.rem(lax.div(dp, 1 << k), 2) for k in range(4)]
    partners = [dp + (1 << k) * (1 - 2 * bits[k]) for k in range(4)]

    barrier = pltpu.get_barrier_semaphore()
    for partner in partners:
        pl.semaphore_signal(barrier, inc=1, device_id={"dp": partner}, device_id_type=MESH)
    pl.semaphore_signal(barrier, inc=1, device_id={"section": 1 - section}, device_id_type=MESH)

    def across(source, target, i):
        return pltpu.make_async_remote_copy(
            src_ref=source, dst_ref=target, send_sem=ysend.at[i], recv_sem=yrecv.at[i],
            device_id={"section": 1 - section}, device_id_type=MESH,
        )

    store_h = pltpu.make_async_copy(E, out_all.at[0:TOKENS], osem.at[0])
    late_h = pltpu.make_async_copy(M, out_all.at[0:TOKENS], osem.at[0])
    store_in = pltpu.make_async_copy(E, out_all.at[TOKENS : 2 * TOKENS], osem.at[1])
    images_a = across(images.at[0:2], IM.at[0:2, 0], 0)
    images_b = across(images.at[2:4], IM.at[2:4, 0], 1)
    send_h = across(E, HIN, 2)
    send_d = across(E, HIN, 3)
    send_i = across(IM.at[:, 0], KV.at[:, 0, :, :WIDE], 4)

    def load(source, target, i):
        return pltpu.make_async_copy(source, target, wsem.at[i])

    own_images = load(images, IM.at[:, 1], 0)
    own_tokens = load(tokens, HIN, 15)
    own_cotangent = load(cotangent, B1, 16)
    loads = {
        "cross": [load(w, WC.at[i], 1 + i) for i, w in enumerate((h_cq, h_ck, h_cv, h_co))],
        "proj": [load(h_proj, WP, 5)],
        "out": [load(h_out, WO, 6)],
        "exp": [
            load(h_exp.at[:, :, :, :, :, pl.ds(WIDE * j, WIDE)], GG.at[12 + j], 7 + j)
            for j in range(4)
        ],
        "red": [load(h_red.at[j], GG.at[8 + j], 11 + j) for j in range(4)],
    }

    @pl.when(one)
    def _():
        own_tokens.start()

    small = [again, ashift, qbias, vbias, obias, fgain, fshift, rbias]
    small = [(v, PV.at[i : i + 1]) for i, v in enumerate(small)]
    small += [(ebias.at[:, pl.ds(WIDE * j, WIDE)], PV.at[8 + j : 9 + j]) for j in range(4)]
    small += [(v, PV.at[12 + i]) for i, v in enumerate((cgain, cshift, cqbias, cvbias, cobias))]
    small = [pltpu.make_async_copy(v, row, psem.at[i]) for i, (v, row) in enumerate(small)]

    @pl.when(two)
    def _():
        own_images.start()
        for i in (1, 2, 0, 3):
            loads["cross"][i].start()

    for name in ("proj", "out", "exp", "red"):
        for copy in loads[name]:
            copy.start()

    own_cotangent.start()
    for copy in small:
        copy.start()
    again, ashift, qbias, vbias, obias, fgain, fshift, rbias = (PV.at[i : i + 1] for i in range(8))
    cgain, cshift, cqbias, cvbias, cobias = (PV.at[i : i + 1] for i in range(12, 17))

    def arrived(name):
        for copy in loads[name]:
            copy.wait()

    VS[...] = jnp.zeros_like(VS)
    low_lane = lax.broadcasted_iota(jnp.int32, (1, 128), 1) < SLOT
    keep_low = low_lane.astype(F32).astype(BF)
    keep_high = jnp.logical_not(low_lane).astype(F32).astype(BF)

    def stacked(x):
        return jnp.concatenate([x * keep_low, x * keep_high], 0)

    def unstacked(x):
        half = x.shape[0] // 2
        return jnp.where(low_lane, x[:half], x[half:])

    eighth = jnp.asarray(0.125, BF)

    VB[...] = jnp.zeros_like(VB)
    VT[...] = jnp.zeros_like(VT)
    VY[...] = jnp.zeros_like(VY)
    pl.semaphore_wait(barrier, 5)

    @pl.when(one)
    def _():
        images_a.start()

    for pair in range(2):
        key = lax.broadcasted_iota(jnp.int32, (128, 256), 0)
        query = lax.rem(lax.broadcasted_iota(jnp.int32, (128, 256), 1), 128)
        first = key < SLOT
        length = jnp.where(first, lengths[2 * pair], lengths[2 * pair + 1] + SLOT)
        same = first == (query < SLOT)
        MASK[pair] = jnp.where(same & (key <= query) & (key < length), 1.0, 0.0)

    for copy in small:
        copy.wait()

    own_cotangent.wait()
    for c in range(CAPS):
        r = pl.ds(SLOT * c, SLOT)
        live = lax.broadcasted_iota(jnp.int32, (SLOT, 1), 0) < lengths[c]
        G[r, :] = jnp.where(live, B1[r, :].astype(F32), 0.0)
    B1[...] = G[...].astype(BF)

    def pair_rows(which, half):
        rows = IM[2 * which : 2 * which + 2, half].reshape(TOKENS, WIDE)
        keys = nn(rows, WC[1])
        KV[2 * which : 2 * which + 2, half, :, :WIDE] = keys.astype(BF).reshape(2, 128, WIDE)
        values = nn(rows, WC[2]) + cvbias[...]
        KV[2 * which : 2 * which + 2, half, :, WIDE:] = values.astype(BF).reshape(2, 128, WIDE)

    @pl.when(two)
    def _():
        for copy in loads["cross"]:
            copy.wait()
        own_images.wait()
        for which in range(2):
            pair_rows(which, 1)
        images_a.wait_recv()
        pair_rows(0, 0)
        arrived("red")
        for j in range(4):
            SL[j] = nt(B1[...], GG[8 + j].reshape(WIDE, WIDE)).astype(BF)
        send_h.wait_recv()
        H[...] = HIN[...].astype(F32)

    @pl.when(one)
    def _():
        own_tokens.wait()
        H[...] = HIN[...].astype(F32)

    @pl.when(one)
    def _():
        SL[...] = jnp.ones_like(SL)

    norm_rows(H, again, ashift, N1, I1, E)
    ET1[...] = E[...].T
    arrived("proj")
    QKV[0] = (nn(E[...], WP[:, 0:WIDE]) + qbias[...]).astype(BF)
    QKV[1] = nn(E[...], WP[:, WIDE : 2 * WIDE]).astype(BF)
    QKV[2] = (nn(E[...], WP[:, 2 * WIDE :]) + vbias[...]).astype(BF)

    def softmax_keys(scores):
        expo = jnp.exp(scores - jnp.max(scores, 0, keepdims=True))
        return expo * (1.0 / jnp.sum(expo, 0, keepdims=True))

    for hp in range(PAIRS):
        cols = pl.ds(128 * hp, 128)
        for pair in range(2):
            rows = pl.ds(pair * 128, 128)
            query = stacked(QKV[0, rows, cols] * eighth)
            scores = nt(QKV[1, rows, cols], query)
            scores = jnp.where(MASK[pair] > 0.0, scores, NEG)
            probs = softmax_keys(scores).astype(BF)
            PT[2 * hp + pair] = probs
            M[rows, cols] = unstacked(tn(probs, QKV[2, rows, cols])).astype(BF)

    MT[...] = M[...].T
    arrived("out")
    H[...] = H[...] + (nn(M[...], WO[...]) + obias[...])

    @pl.when(two)
    def _():
        norm_rows(H, cgain, cshift, N2, I2, E)
        ET2[...] = E[...].T
        QC[...] = (nn(E[...], WC[0]) + cqbias[...]).astype(BF)

    @pl.when(two)
    def _():
        images_b.wait_recv()

    @pl.when(two)
    def _():
        pair_rows(1, 0)

    @pl.when(two)
    def _():
        for hp in range(PAIRS):
            cols = pl.ds(128 * hp, 128)
            vcols = pl.ds(WIDE + 128 * hp, 128)
            for c in range(CAPS):
                rows = pl.ds(c * SLOT, SLOT)
                query = stacked(QC[rows, cols] * eighth)
                keys = KV[c, :, :, cols].reshape(256, 128)
                probs = softmax_keys(nt(keys, query)).astype(BF)
                PC[4 * hp + c] = probs
                values = KV[c, :, :, vcols].reshape(256, 128)
                M[rows, cols] = unstacked(tn(probs, values)).astype(BF)

    @pl.when(two)
    def _():
        CT[...] = M[...].T
        H[...] = H[...] + (nn(M[...], WC[3]) + cobias[...])

    norm_rows(H, fgain, fshift, N3, I3, E)
    ET3[...] = E[...].T
    arrived("exp")

    def widen(j):
        for t in range(3):
            cols = pl.ds(256 * t, 256)
            u = nn(E[...], GG[12 + j, :, :, :, :, :, cols].reshape(WIDE, 256)) + PV[8 + j : 9 + j, cols]
            cdf = 0.5 * (1.0 + erf(u * 0.7071067811865476))
            M[:, cols] = (u * cdf).astype(BF)
            slope = cdf + u * jnp.exp(-0.5 * u * u) * 0.3989422804014327
            SL[j, :, cols] = (SL[j, :, cols].astype(F32) * slope).astype(BF)
        AT[4 * j : 4 * j + 4] = M[...].T.reshape(4, 4, 48, TOKENS)

    @pl.when(one)
    def _():
        arrived("red")
        H[...] = H[...] + rbias[...]
        for j in range(4):
            widen(j)
            H[...] = H[...] + nn(M[...], GG[8 + j].reshape(WIDE, WIDE))
        E[...] = H[...].astype(BF)
        send_h.start()
        store_h.start()
        send_h.wait_send()
        images_a.wait_send()
        images_b.start()

    @pl.when(two)
    def _():
        for j in range(4):
            widen(j)

    @pl.when(one)
    def _():
        store_h.wait()
        send_d.wait_recv()
        G[...] = G[...] + HIN[...].astype(F32)
        B1[...] = G[...].astype(BF)

    def images_out(source, what):
        for c in range(CAPS):
            target = out_all.at[2 * TOKENS + 128 * c : 2 * TOKENS + 128 * (c + 1)]
            getattr(pltpu.make_async_copy(source.at[c], target, osem.at[2 + c]), what)()

    def shard_place(c):
        return out_all.at[pl.ds(pl.multiple_of(4 * TOKENS + 48 * c, 16), 48)]

    def order(p):
        return (0, 2, 1, 3) if p in Z_FIRST else (0, 1, 2, 3)

    def chunk(p):
        return p if p < 8 else jnp.where(one, p + 4, p)

    def where(p, k, bit):
        done, now = order(p)[:k], order(p)[k]
        places = [bits[a] if a in done else bit if a == now else slice(None) for a in (3, 2, 1, 0)]
        return (chunk(p), *places)

    def landing(p, k):
        if k == 0:
            return R0.at[p % 8]
        return (R1, R2, R3)[k - 1].at[p]

    def exchange(p, k):
        axis = order(p)[k]
        return pltpu.make_async_remote_copy(
            src_ref=GG.at[where(p, k, 1 - bits[axis])], dst_ref=landing(p, k),
            send_sem=send_sem.at[p, k], recv_sem=recv_sem.at[p, k],
            device_id={"dp": partners[axis]}, device_id_type=MESH,
        )

    def begin(p, k):
        if k == 0 and p >= 8:
            pl.semaphore_wait(credit.at[p - 8], 1)
        exchange(p, k).start()

    def finish(p, k):
        exchange(p, k).wait()
        axis = order(p)[k]
        keep, term = GG.at[where(p, k, bits[axis])], landing(p, k)
        for place in itertools.product(range(2), repeat=3 - k):
            keep[place] = keep[place] + term[place]
        if k == 0 and p < 8:
            def give():
                pl.semaphore_signal(
                    credit.at[p], inc=1, device_id={"dp": partners[axis]}, device_id_type=MESH
                )
            give() if p < 4 else pl.when(two)(give)

    def shard(p):
        return GG.at[(chunk(p), *(bits[a] for a in (3, 2, 1, 0)))]

    def shard_out(p):
        return pltpu.make_async_copy(shard(p), shard_place(chunk(p)), lsem.at[p])

    def shard_across(p):
        return across(shard(p), YS.at[p - 8], 6 + p - 8)

    def advance(p, k):
        finish(p, k - 1)
        if k < 4:
            begin(p, k)
        else:
            shard_out(p).start()
            if 8 <= p < 12:
                pl.when(two)(lambda: shard_across(p).start())

    def go(p, k):
        if p >= 12:
            pl.when(two)(lambda: advance(p, k) if k else begin(p, 0))
        elif k:
            advance(p, k)
        else:
            begin(p, 0)

    def sum_part(k, bit):
        return VT.at[tuple(bits[a] if a < k else bit if a == k else slice(None) for a in (3, 2, 1, 0))]

    def sum_copy(k):
        return pltpu.make_async_remote_copy(
            src_ref=sum_part(k, 1 - bits[k]), dst_ref=(V0, V1, V2, V3)[k],
            send_sem=vsend.at[k], recv_sem=vrecv.at[k],
            device_id={"dp": partners[k]}, device_id_type=MESH,
        )

    def sum_add(k):
        sum_copy(k).wait()
        keep, term = sum_part(k, bits[k]), (V0, V1, V2, V3)[k]
        for place in itertools.product(range(2), repeat=3 - k):
            keep[place] = keep[place] + term[place]

    def sum_shards():
        for d in range(16):
            place = ((d >> 3) & 1, (d >> 2) & 1, (d >> 1) & 1, d & 1)
            VT[(*place, slice(None), slice(0, 48))] = VS[:, 48 * d : 48 * (d + 1)]
            for i in range(4):
                first = 192 * (d % 4) + 48 * i
                VT[(*place, slice(8 + i, 9 + i), slice(0, 48))] = VS[8 + d // 4 : 9 + d // 4, first : first + 48]

    def sum_result():
        return VT.at[tuple(bits[a] for a in (3, 2, 1, 0))]

    def weight_gradient(c, left, right):
        for t in range(3):
            part = nn(left, right(pl.ds(256 * t, 256)))
            GG[c, :, :, :, :, :, pl.ds(256 * t, 256)] = part.astype(BF).reshape(LEAD + (48, 256))


    def reduce_chunk(i):
        weight_gradient(i, AT[:, i].reshape(WIDE, TOKENS), lambda t: B1[:, t])
        go(i, 0)

    reduce_chunk(0)
    reduce_chunk(1)


    @pl.when(one)
    def _():
        for j in range(4):
            for i in range(2):
                r = pl.ds(128 * i, 128)
                da = nt(B1[r, :], GG[8 + j].reshape(WIDE, WIDE))
                SL[j, r, :] = (da * SL[j, r, :].astype(F32)).astype(BF)

    total = nt(SL[0], GG[12].reshape(WIDE, WIDE))
    for j in range(1, 4):
        total = total + nt(SL[j], GG[12 + j].reshape(WIDE, WIDE))
    D[...] = total

    go(0, 1)
    go(1, 1)
    reduce_chunk(2)
    reduce_chunk(3)

    norm_rows_back(D, N3, I3, fgain, G, VS, 5, 6)

    @pl.when(one)
    def _():
        go(2, 1)
        go(3, 1)


    @pl.when(two)
    def _():
        B2[...] = G[...].astype(BF)
        E[...] = nt(B2[...], WC[3]).astype(BF)
        go(2, 1)
        go(3, 1)

    @pl.when(two)
    def _():
        for hp in range(PAIRS):
            cols = pl.ds(128 * hp, 128)
            vcols = pl.ds(WIDE + 128 * hp, 128)
            for c in range(CAPS):
                rows = pl.ds(c * SLOT, SLOT)
                query = stacked(QC[rows, cols] * eighth)
                grad = stacked(E[rows, cols])
                keys = KV[c, :, :, cols].reshape(256, 128)
                values = KV[c, :, :, vcols].reshape(256, 128)
                probs = PC[4 * hp + c]
                wide = probs.astype(F32)
                dprobs = nt(values, grad)
                dscores = (wide * (dprobs - jnp.sum(wide * dprobs, 0, keepdims=True))).astype(BF)
                KV[c, :, :, cols] = nn(dscores, query).astype(BF).reshape(2, 128, 128)
                KV[c, :, :, vcols] = nn(probs, grad).astype(BF).reshape(2, 128, 128)
                QC[rows, cols] = (unstacked(tn(dscores, keys)) * 0.125).astype(BF)

    @pl.when(two)
    def _():
        D[...] = nt(QC[...], WC[0])
        norm_rows_back(D, N2, I2, cgain, G, VS, 12, 13)

    HIN[...] = G[...].astype(BF)
    E[...] = nt(HIN[...], WO[...]).astype(BF)

    for hp in range(PAIRS):
        cols = pl.ds(128 * hp, 128)
        for pair in range(2):
            rows = pl.ds(pair * 128, 128)
            query = stacked(QKV[0, rows, cols] * eighth)
            grad = stacked(E[rows, cols])
            keys = QKV[1, rows, cols]
            probs = PT[2 * hp + pair]
            wide = probs.astype(F32)
            dprobs = nt(QKV[2, rows, cols], grad)
            dscores = (wide * (dprobs - jnp.sum(wide * dprobs, 0, keepdims=True))).astype(BF)
            QKV[1, rows, cols] = nn(dscores, query).astype(BF)
            QKV[2, rows, cols] = nn(probs, grad).astype(BF)
            QKV[0, rows, cols] = (unstacked(tn(dscores, keys)) * 0.125).astype(BF)

    D[...] = nt(QKV[0], WP[:, 0:WIDE])
    D[...] = D[...] + nt(QKV[1], WP[:, WIDE : 2 * WIDE])
    D[...] = D[...] + nt(QKV[2], WP[:, 2 * WIDE :])
    norm_rows_back(D, N1, I1, again, G, VS, 0, 1)

    E[...] = G[...].astype(BF)
    store_in.start()
    pl.when(two)(lambda: send_d.start())

    def late_sums():
        for j in range(4):
            VS[8 + j : 9 + j, :] = sum_columns(lambda k, r: SL[j, r, :], 1)
        VS[7:8, :] = sum_columns(lambda k, r: B1[r, :], 1)
        VS[2:3, :] = sum_columns(lambda k, r: QKV[0, r, :], 1)
        VS[3:4, :] = sum_columns(lambda k, r: QKV[2, r, :], 1)
        VS[4:5, :] = sum_columns(lambda k, r: HIN[r, :], 1)

        @pl.when(two)
        def _():
            VS[14:15, :] = sum_columns(lambda k, r: QC[r, :], 1)
            VS[16:17, :] = sum_columns(lambda k, r: B2[r, :], 1)
            VS[15:16, :] = sum_columns(
                lambda k, r: KV[k, :, pl.ds(r.start // 2, 16), WIDE:].reshape(32, WIDE), 4
            )

    def late_output():
        @pl.when(two)
        def _():
            H[...] = H[...] + rbias[...]
            for j in range(4):
                a = AT[4 * j : 4 * j + 4].reshape(WIDE, TOKENS)
                H[...] = H[...] + tn(a, GG[8 + j].reshape(WIDE, WIDE))
            M[...] = H[...].astype(BF)
            late_h.start()

    def turn_images():
        @pl.when(two)
        def _():
            for c in range(CAPS):
                AT[4 * c : 4 * c + 4] = IM[c].reshape(256, WIDE).T.reshape(4, 4, 48, TOKENS)

    def image_gradient():
        @pl.when(two)
        def _():
            for c in range(CAPS):
                part = nt(KV[c, :, :, :WIDE].reshape(256, WIDE), WC[1])
                part = part + nt(KV[c, :, :, WIDE:].reshape(256, WIDE), WC[2])
                IM[c] = part.astype(BF).reshape(2, 128, WIDE)
            send_i.start()
            images_out(IM.at[:, 1], "start")

    def image_pairs(j):
        for t in range(3):
            cols = pl.ds(WIDE * j + 256 * t, 256)
            part = sum(
                nn(AT[4 * c : 4 * c + 4].reshape(WIDE, TOKENS), KV[c, :, :, cols].reshape(256, 256))
                for c in range(CAPS)
            )
            GG[9 + j, :, :, :, :, :, pl.ds(256 * t, 256)] = part.astype(BF).reshape(LEAD + (48, 256))

    def self_chunk(i):
        if i < 3:
            weight_gradient(12 + i, ET1[...], lambda t: QKV[i, :, t])
        else:
            weight_gradient(15, MT[...], lambda t: HIN[:, t])

    def cross_chunk(i):
        if i == 0:
            weight_gradient(8, ET2[...], lambda t: QC[:, t])
        elif i < 3:
            image_pairs(i - 1)
        else:
            weight_gradient(11, CT[...], lambda t: B2[:, t])

    def compute(p):
        if p < 8:
            weight_gradient(p, ET3[...], lambda t: SL[p - 4, :, t])
        elif p < 12:
            pl.when(one)(lambda: self_chunk(p - 8))
            pl.when(two)(lambda: cross_chunk(p - 8))
        else:
            pl.when(two)(lambda: self_chunk(p - 12))

    def sums(k):
        if k > 0:
            sum_add(k - 1)
        else:
            sum_shards()
        if k < 4:
            sum_copy(k).start()
        else:
            pl.when(two)(lambda: across(sum_result(), VY, 5).start())

    def images_end():
        @pl.when(one)
        def _():
            images_b.wait_send()
            send_i.wait_recv()
            images_out(KV.at[:, 0, :, :WIDE], "start")

    work = {0: late_sums, 1: late_output, 2: image_gradient, 4: turn_images, 10: images_end}
    work.update({5 + k: functools.partial(sums, k) for k in range(5)})

    for p, k in EVENTS:
        if p == 16:
            work[k]()
            continue
        if k == 0:
            compute(p)
        go(p, k)

    @pl.when(two)
    def _():
        across(sum_result(), VY, 5).wait_send()
        images_out(IM.at[:, 1], "wait")
        send_d.wait_send()
        send_i.wait_send()
        late_h.wait()
        for p in range(8, 12):
            shard_across(p).wait_send()
        for p in range(12, 16):
            shard_out(p).wait()

    @pl.when(one)
    def _():
        across(sum_result(), VY, 5).wait_recv()
        copies = [pltpu.make_async_copy(YS.at[i], shard_place(8 + i), lsem.at[12 + i]) for i in range(4)]
        for i in range(4):
            across(YS.at[i], YS.at[i], 6 + i).wait_recv()
            copies[i].start()
        for copy in copies:
            copy.wait()
        images_out(KV.at[:, 0, :, :WIDE], "wait")

    store_in.wait()
    crossed = lax.broadcasted_iota(jnp.int32, (24, 128), 0) >= 12
    final = jnp.where(crossed & one, VY[...], sum_result()[...])
    high = final.astype(BF)
    VB[0:24, 0:128] = high
    VB[24:48, 0:128] = (final - high.astype(F32)).astype(BF)
    store_v = pltpu.make_async_copy(VB, out_all.at[7 * TOKENS : 7 * TOKENS + 48], osem.at[6])
    store_v.start()
    store_v.wait()
    for p in range(12):
        shard_out(p).wait()


def mega(args):
    (
        tokens, images, lengths, cotangent, again, ashift, proj, qb, vb, wo, ob, fg, fs, we, eb, wr, rb,
        cg, cs, cq, cqb, ck, cv, cvb, co, cob,
    ) = args
    operands = (
        lengths, tokens.reshape(TOKENS, WIDE), cotangent.reshape(TOKENS, WIDE), images,
        proj[0], wo[0], we.reshape(LEAD + (48, 4 * WIDE)), wr.reshape((4,) + LEAD + (48, WIDE)), cq, ck, cv, co,
        again, ashift, qb, vb, ob, fg, fs, rb, eb, cg, cs, cqb, cvb, cob,
    )
    hbm = pl.BlockSpec(memory_space=pl.ANY)
    dma = pltpu.SemaphoreType.DMA
    big = (TOKENS, WIDE)
    turned = (WIDE, TOKENS)
    b = lambda *shape: pltpu.VMEM(shape, BF)
    f = lambda *shape: pltpu.VMEM(shape, F32)
    return pl.pallas_call(
        mega_kernel,
        out_shape=jax.ShapeDtypeStruct((7 * TOKENS + 48, WIDE), BF),
        in_specs=[pl.BlockSpec(memory_space=pltpu.SMEM)] + [hbm] * (len(operands) - 1),
        out_specs=hbm,
        scratch_shapes=[
            b(16, *LEAD, 48, WIDE), b(WIDE, 3 * WIDE), b(WIDE, WIDE), b(4, WIDE, WIDE),
            b(8, 2, 2, 2, 48, WIDE), b(16, 2, 2, 48, WIDE), b(16, 2, 48, WIDE), b(16, 48, WIDE),
            f(*big), f(*big), f(*big), b(*big), b(*big), b(*big), f(TOKENS, 1), f(TOKENS, 1), f(TOKENS, 1),
            b(*big), b(*turned), b(*turned), b(*turned),
            b(3, *big), b(*big), b(*turned), b(*big), b(*turned), b(4, *big),
            b(16, 4, 48, TOKENS), b(12, 128, 256), b(24, 256, 128), b(CAPS, 2, 128, WIDE),
            b(CAPS, 2, 128, 2 * WIDE), b(*big), b(*big),
            b(*big), f(2, 128, 256), b(4, 48, WIDE), f(24, WIDE), f(*LEAD, 24, 128), f(2, 2, 2, 24, 128), f(2, 2, 24, 128),
            f(2, 24, 128), f(24, 128), f(24, 128), b(48, WIDE), f(24, WIDE),
            dma((17,)), dma((17,)), dma((16,)), dma((7,)), dma((10,)), dma((10,)),
            dma((16, 4)), dma((16, 4)), dma((4,)), dma((4,)), pltpu.SemaphoreType.REGULAR((8,)),
        ],
        compiler_params=pltpu.CompilerParams(
            collective_id=0, has_side_effects=True, vmem_limit_bytes=63 * 2**20
        ),
        name="layers",
    )(*operands)


def finish_kernel(every, *outs):
    (
        o_h, o_in, o_img, o_ag, o_as, o_proj, o_qb, o_vb, o_wo, o_ob, o_fg, o_fs, o_we, o_eb, o_wr, o_rb,
        o_cg, o_cs, o_cq, o_cqb, o_ck, o_cv, o_cvb, o_co, o_cob,
    ) = outs
    o_h[...] = every[0:TOKENS, :].reshape(o_h.shape)
    o_in[...] = every[TOKENS : 2 * TOKENS, :].astype(F32).reshape(o_in.shape)
    o_img[...] = every[2 * TOKENS : 4 * TOKENS, :].astype(F32).reshape(o_img.shape)
    shards = [every[4 * TOKENS + 48 * j : 4 * TOKENS + 48 * (j + 1), :].astype(F32) for j in range(16)]
    vec = every[7 * TOKENS : 7 * TOKENS + 48, 0:128].astype(F32)
    vec = vec[:24] + vec[24:]
    for j in range(3):
        o_proj[0, :, WIDE * j : WIDE * (j + 1)] = shards[12 + j]
    o_wo[0] = shards[15]
    for j in range(4):
        o_we[0, :, WIDE * j : WIDE * (j + 1)] = shards[4 + j]
        o_wr[0, 48 * j : 48 * (j + 1), :] = shards[j]
    for j, out in enumerate((o_cq, o_ck, o_cv, o_co)):
        out[...] = shards[8 + j]
    places = (
        (o_ag, 0), (o_as, 1), (o_qb, 2), (o_vb, 3), (o_ob, 4), (o_fg, 5), (o_fs, 6), (o_rb, 7),
        (o_cg, 12), (o_cs, 13), (o_cqb, 14), (o_cvb, 15), (o_cob, 16),
    )
    for out, i in places:
        out[...] = vec[i : i + 1, :48]
    for i in range(4):
        o_eb[:, 48 * i : 48 * (i + 1)] = vec[8 + i : 9 + i, :48]


def finish_outputs(every):
    vm = pl.BlockSpec(memory_space=pltpu.VMEM)
    small = (1, 48)
    shapes = [
        (1, CAPS, SLOT, WIDE), (1, CAPS, SLOT, WIDE), (CAPS, 128, WIDE),
        small, small, (1, 48, 3 * WIDE), small, small, (1, 48, WIDE), small, small, small,
        (1, 48, 4 * WIDE), (1, 192), (1, 192, WIDE), small,
        small, small, (48, WIDE), small, (48, WIDE), (48, WIDE), small, (48, WIDE), small,
    ]
    outs = pl.pallas_call(
        finish_kernel,
        out_shape=[jax.ShapeDtypeStruct(x, BF if i == 0 else F32) for i, x in enumerate(shapes)],
        in_specs=[vm],
        out_specs=[vm] * 25,
        compiler_params=pltpu.CompilerParams(vmem_limit_bytes=40 * 2**20),
        name="finish",
    )(every)
    outs = list(outs)
    for i in (16, 17, 19, 22, 24):
        outs[i] = outs[i].reshape(-1)
    return tuple(outs)


def body(
    tokens,
    images,
    lengths,
    cotangent,
    attend_gain,
    attend_shift,
    projections,
    query_bias,
    value_bias,
    output_weight,
    output_bias,
    feed_gain,
    feed_shift,
    expand_weight,
    expand_bias,
    reduce_weight,
    reduce_bias,
    cross_gain,
    cross_shift,
    cross_query,
    cross_query_bias,
    cross_key,
    cross_value,
    cross_value_bias,
    cross_out,
    cross_out_bias,
):
    layer = tuple(
        (
            weight[0]
            for weight in (
                attend_gain,
                attend_shift,
                projections,
                query_bias,
                value_bias,
                output_weight,
                output_bias,
                feed_gain,
                feed_shift,
                expand_weight,
                expand_bias,
                reduce_weight,
                reduce_bias,
            )
        )
    )
    cross = (
        cross_gain,
        cross_shift,
        cross_query,
        cross_query_bias,
        cross_key,
        cross_value,
        cross_value_bias,
        cross_out,
        cross_out_bias,
    )
    pair_weight = jnp.concatenate([cross_key, cross_value], 1)
    pair_bias = jnp.concatenate([jnp.zeros_like(cross_value_bias), cross_value_bias], 0)
    section_index = lax.axis_index("section")
    is_two = section_index == 1
    block = MB_CAPS
    half = images.shape[1]
    slots = tokens.shape[1]
    width = tokens.shape[2]
    positions = jnp.arange(slots, dtype=jnp.int32)
    causal = positions[None, :] <= positions[:, None]
    zero_cross = tuple((jnp.zeros(weight.shape, jnp.float32) for weight in cross))

    def image_project(image_rows):
        return (product(image_rows, pair_weight) + pair_bias).astype(jnp.bfloat16)

    def image_back(image_rows, dpairs):
        dimages = back_product(dpairs, pair_weight)
        pair_grad = weight_product(image_rows, dpairs)
        return (
            dimages,
            (pair_grad[:, :width], pair_grad[:, width:], column_sum(dpairs[..., width:])),
        )

    def cross_yes(hidden, image_data):
        pairs = image_project(image_data)
        after, saved = cross_forward(hidden, pairs, cross)
        return (after, saved, pairs)

    def cross_no(hidden, image_data):
        saved = (
            jnp.zeros((block, slots, width), jnp.float32),
            jnp.zeros((block, slots, 1), jnp.float32),
            jnp.zeros((block, slots, width), jnp.bfloat16),
            jnp.zeros((block, slots, width), jnp.bfloat16),
            jnp.zeros((block, slots, width), jnp.bfloat16),
            jnp.zeros((block, HEADS, slots, 1), jnp.float32),
        )
        return (hidden, saved, jnp.zeros((block, 2 * half, 2 * width), jnp.bfloat16))

    def back_yes(grad, saved, pairs, image_data):
        dgrad, parts, dpairs = cross_back(grad, saved, pairs, cross)
        dimages, image_terms = image_back(image_data, dpairs)
        return (dgrad, parts[:4] + image_terms + parts[4:], dimages)

    def back_no(grad, saved, pairs, image_data):
        return (grad, zero_cross, jnp.zeros((block, 2 * half, width), jnp.float32))

    received = jnp.zeros((block, slots, width), jnp.bfloat16)
    arriving = jnp.zeros((block, half, width), jnp.bfloat16)
    finished = jnp.zeros(tokens.shape, jnp.bfloat16)
    kept = []
    for tick in range(MICRO + 1):
        index = jnp.clip(tick - section_index, 0, MICRO - 1)
        start = index * block
        live = positions[None, :] < lax.dynamic_slice_in_dim(lengths, start, block, 0)[:, None]
        mask = live[:, None, :] & causal[None]
        own_tokens = lax.dynamic_slice_in_dim(tokens, start, block, 0)
        own_images = lax.dynamic_slice_in_dim(images, start, block, 0)
        hidden = jnp.where(is_two, received, own_tokens).astype(jnp.float32)
        after_self, self_saved = self_forward(hidden, layer, mask)
        image_data = jnp.concatenate([arriving, own_images], 1)
        after_cross, cross_saved, pairs = lax.cond(
            is_two, cross_yes, cross_no, after_self, image_data
        )
        final, feed_saved = feed_forward(after_cross, layer)
        result = final.astype(jnp.bfloat16)
        finished = lax.dynamic_update_slice_in_dim(finished, result, start, 0)
        kept.append((mask, live, self_saved, cross_saved, feed_saved, pairs, image_data))
        if tick < MICRO:
            received = shifted(result, "section", 1)
            arriving = shifted(own_images, "section", 1)
    layer_sums = tuple((jnp.zeros(weight.shape, jnp.float32) for weight in layer))
    cross_sums = zero_cross
    input_grads = jnp.zeros(tokens.shape, jnp.float32)
    image_grads = jnp.zeros(images.shape, jnp.float32)
    returning = jnp.zeros((block, slots, width), jnp.bfloat16)
    coming = jnp.zeros((block, half, width), jnp.float32)
    for turn in range(MICRO + 1):
        tick = MICRO - turn
        offset = tick - section_index
        index = jnp.clip(offset, 0, MICRO - 1)
        start = index * block
        valid = ((offset >= 0) & (offset < MICRO)).astype(jnp.float32)
        mask, live, self_saved, cross_saved, feed_saved, pairs, image_data = kept[tick]
        own_images = lax.dynamic_slice_in_dim(images, start, block, 0)
        seed_grad = lax.dynamic_slice_in_dim(cotangent[0], start, block, 0).astype(
            jnp.float32
        ) * live[..., None].astype(jnp.float32)
        grad = seed_grad + returning.astype(jnp.float32)
        grad, feed_grads = feed_back(grad, feed_saved, layer)
        grad, cross_grads, image_part = lax.cond(
            is_two, back_yes, back_no, grad, cross_saved, pairs, image_data
        )
        grad, self_grads = self_back(grad, self_saved, layer, mask)
        layer_sums = tuple(
            (total + valid * part for total, part in zip(layer_sums, self_grads + feed_grads))
        )
        cross_sums = tuple((total + valid * part for total, part in zip(cross_sums, cross_grads)))
        sent = grad.astype(jnp.bfloat16)
        stored = jnp.where(is_two, sent.astype(jnp.float32), grad)
        input_grads = jnp.where(
            valid > 0, lax.dynamic_update_slice_in_dim(input_grads, stored, start, 0), input_grads
        )
        own_dimages = jnp.where(is_two, image_part[:, half:], coming)
        image_grads = jnp.where(
            valid > 0,
            lax.dynamic_update_slice_in_dim(image_grads, own_dimages, start, 0),
            image_grads,
        )
        if turn < MICRO:
            returning = shifted(sent, "section", -1)
            coming = shifted(image_part[:, :half].astype(jnp.bfloat16), "section", -1).astype(
                jnp.float32
            )
    shared = lax.psum_scatter(
        tuple((total[None] for total in layer_sums)), "dp", scatter_dimension=1, tiled=True
    )
    scattered = lax.psum_scatter(cross_sums, "dp", scatter_dimension=0, tiled=True)
    crossed = jax.tree.map(
        lambda part: part.astype(jnp.float32), lax.psum(for_sending(tuple(scattered)), "section")
    )
    return (finished[None], input_grads[None], image_grads) + tuple(shared) + tuple(crossed)


def one_kernel(*args):
    return finish_outputs(mega(args))


def solution(mesh):
    placed = (
        P("dp", None, None),
        P("dp", "section", None),
        P("dp"),
        P("section", "dp", None, None),
        P("section", None),
        P("section", None),
        P("section", None, None),
        P("section", None),
        P("section", None),
        P("section", None, None),
        P("section", None),
        P("section", None),
        P("section", None),
        P("section", None, None),
        P("section", None),
        P("section", None, None),
        P("section", None),
        P(),
        P(),
        P(),
        P(),
        P(),
        P(),
        P(),
        P(),
        P(),
    )
    return jax.shard_map(
        one_kernel if mesh.shape["dp"] == 16 else body,
        mesh=mesh,
        in_specs=placed,
        out_specs=(
            P("section", "dp", None, None),
            P("section", "dp", None, None),
            P("dp", "section", None),
            P("section", "dp"),
            P("section", "dp"),
            P("section", "dp", None),
            P("section", "dp"),
            P("section", "dp"),
            P("section", "dp", None),
            P("section", "dp"),
            P("section", "dp"),
            P("section", "dp"),
            P("section", "dp", None),
            P("section", "dp"),
            P("section", "dp", None),
            P("section", "dp"),
            P("dp"),
            P("dp"),
            P("dp", None),
            P("dp"),
            P("dp", None),
            P("dp", None),
            P("dp"),
            P("dp", None),
            P("dp"),
        ),
        check_vma=False,
    )
```

```python
import functools
import itertools

import jax
import jax.numpy as jnp
from jax import lax
from jax.experimental import pallas as pl
from jax.experimental.pallas import tpu as pltpu
from jax.sharding import PartitionSpec as P

HEADS = 12
HEAD_DIM = 64
MB_CAPS = 4
MICRO = 1


EPS = 1e-05
NEG = -1000000000.0


def shifted(block, axis, distance):
    devices = range(lax.axis_size(axis))
    route = [(i - distance, i) for i in devices if i - distance in devices]
    return lax.ppermute(block, axis, route)


def for_sending(array):
    return jax.tree.map(lambda a: a.astype(jnp.bfloat16) if a.dtype == jnp.float32 else a, array)


def layer_norm(rows, gain, shift):
    mean = jnp.mean(rows, -1, keepdims=True)
    centred = rows - mean
    inverse = lax.rsqrt(jnp.mean(centred * centred, -1, keepdims=True) + EPS)
    normed = centred * inverse
    return (normed * gain + shift, normed, inverse)


def norm_back(grad, normed, inverse, gain):
    scaled = grad * gain
    inner = (
        scaled
        - jnp.mean(scaled, -1, keepdims=True)
        - normed * jnp.mean(scaled * normed, -1, keepdims=True)
    )
    return (inverse * inner, jnp.sum(grad * normed, axis=(0, 1)), jnp.sum(grad, axis=(0, 1)))


def product(rows, weight):
    return jnp.einsum("bsi,ij->bsj", rows, weight, preferred_element_type=jnp.float32)


def back_product(grad, weight):
    return jnp.einsum("bsj,ij->bsi", grad, weight, preferred_element_type=jnp.float32)


def weight_product(rows, grad):
    return jnp.einsum("bsi,bsj->ij", rows, grad, preferred_element_type=jnp.float32)


def column_sum(grad):
    return jnp.sum(grad.astype(jnp.float32), axis=(0, 1))


def split_heads(rows):
    return rows.reshape(rows.shape[0], rows.shape[1], HEADS, HEAD_DIM)


def scores_of(query, keys, mask):
    scores = jnp.einsum(
        "bqhd,bkhd->bhqk", split_heads(query), split_heads(keys), preferred_element_type=jnp.float32
    ) * HEAD_DIM ** (-0.5)
    if mask is None:
        return scores
    return jnp.where(mask[:, None], scores, NEG)


def attend(query, keys, values, mask):
    scores = scores_of(query, keys, mask)
    top = jnp.max(scores, -1, keepdims=True)
    expo = jnp.exp(scores - top)
    total = jnp.sum(expo, -1, keepdims=True)
    probs = (expo / total).astype(jnp.bfloat16)
    mixed = jnp.einsum(
        "bhqk,bkhd->bqhd", probs, split_heads(values), preferred_element_type=jnp.float32
    )
    return (mixed.reshape(query.shape).astype(jnp.bfloat16), top + jnp.log(total))


def attend_back(grad, query, keys, values, logsum, mask):
    scale = HEAD_DIM ** (-0.5)
    probs = jnp.exp(scores_of(query, keys, mask) - logsum)
    grad_heads = split_heads(grad)
    dprobs = jnp.einsum(
        "bqhd,bkhd->bhqk", grad_heads, split_heads(values), preferred_element_type=jnp.float32
    )
    rowdot = jnp.sum(probs * dprobs, -1, keepdims=True)
    dscores = (probs * (dprobs - rowdot)).astype(jnp.bfloat16)
    dquery = (
        jnp.einsum(
            "bhqk,bkhd->bqhd", dscores, split_heads(keys), preferred_element_type=jnp.float32
        )
        * scale
    )
    dkeys = (
        jnp.einsum(
            "bhqk,bqhd->bkhd", dscores, split_heads(query), preferred_element_type=jnp.float32
        )
        * scale
    )
    dvalues = jnp.einsum(
        "bhqk,bqhd->bkhd",
        probs.astype(jnp.bfloat16),
        grad_heads,
        preferred_element_type=jnp.float32,
    )
    return (
        dquery.reshape(query.shape).astype(jnp.bfloat16),
        dkeys.reshape(keys.shape).astype(jnp.bfloat16),
        dvalues.reshape(values.shape).astype(jnp.bfloat16),
    )


def self_forward(hidden, layer, mask):
    normal, normed, inverse = layer_norm(hidden, layer[0], layer[1])
    entry = normal.astype(jnp.bfloat16)
    packed = product(entry, layer[2])
    width = hidden.shape[-1]
    query = (packed[..., :width] + layer[3]).astype(jnp.bfloat16)
    keys = packed[..., width : 2 * width].astype(jnp.bfloat16)
    values = (packed[..., 2 * width :] + layer[4]).astype(jnp.bfloat16)
    mixed, logsum = attend(query, keys, values, mask)
    after = hidden + (product(mixed, layer[5]) + layer[6])
    return (after, (normed, inverse, entry, query, keys, values, mixed, logsum))


def self_back(grad, saved, layer, mask):
    normed, inverse, entry, query, keys, values, mixed, logsum = saved
    branch = grad.astype(jnp.bfloat16)
    out_weight_grad = weight_product(mixed, branch)
    out_bias_grad = column_sum(branch)
    dmixed = back_product(branch, layer[5]).astype(jnp.bfloat16)
    dquery, dkeys, dvalues = attend_back(dmixed, query, keys, values, logsum, mask)
    dpacked = jnp.concatenate([dquery, dkeys, dvalues], -1)
    packed_grad = weight_product(entry, dpacked)
    dentry = back_product(dpacked, layer[2])
    dhidden, gain_grad, shift_grad = norm_back(dentry, normed, inverse, layer[0])
    return (
        grad + dhidden,
        (
            gain_grad,
            shift_grad,
            packed_grad,
            column_sum(dquery),
            column_sum(dvalues),
            out_weight_grad,
            out_bias_grad,
        ),
    )


def gelu_slope(expanded):
    normal_cdf = 0.5 * (1.0 + jax.scipy.special.erf(expanded * 0.7071067811865476))
    return normal_cdf + expanded * jnp.exp(-0.5 * expanded * expanded) * 0.3989422804014327


def feed_forward(hidden, layer):
    normal, normed, inverse = layer_norm(hidden, layer[7], layer[8])
    entry = normal.astype(jnp.bfloat16)
    expanded = product(entry, layer[9]) + layer[10]
    active = jax.nn.gelu(expanded, approximate=False).astype(jnp.bfloat16)
    after = hidden + (product(active, layer[11]) + layer[12])
    return (after, (normed, inverse, entry, expanded, active))


def feed_back(grad, saved, layer):
    normed, inverse, entry, expanded, active = saved
    branch = grad.astype(jnp.bfloat16)
    reduce_grad = weight_product(active, branch)
    reduce_bias_grad = column_sum(branch)
    dactive = back_product(branch, layer[11])
    dexpanded = (dactive * gelu_slope(expanded)).astype(jnp.bfloat16)
    expand_grad = weight_product(entry, dexpanded)
    expand_bias_grad = column_sum(dexpanded)
    dentry = back_product(dexpanded, layer[9])
    dhidden, gain_grad, shift_grad = norm_back(dentry, normed, inverse, layer[7])
    return (
        grad + dhidden,
        (gain_grad, shift_grad, expand_grad, expand_bias_grad, reduce_grad, reduce_bias_grad),
    )


def cross_forward(hidden, pairs, cross):
    normal, normed, inverse = layer_norm(hidden, cross[0], cross[1])
    entry = normal.astype(jnp.bfloat16)
    query = (product(entry, cross[2]) + cross[3]).astype(jnp.bfloat16)
    width = hidden.shape[-1]
    mixed, logsum = attend(query, pairs[..., :width], pairs[..., width:], None)
    after = hidden + (product(mixed, cross[7]) + cross[8])
    return (after, (normed, inverse, entry, query, mixed, logsum))


def cross_back(grad, saved, pairs, cross):
    normed, inverse, entry, query, mixed, logsum = saved
    width = grad.shape[-1]
    branch = grad.astype(jnp.bfloat16)
    out_grad = weight_product(mixed, branch)
    out_bias_grad = column_sum(branch)
    dmixed = back_product(branch, cross[7]).astype(jnp.bfloat16)
    dquery, dkeys, dvalues = attend_back(
        dmixed, query, pairs[..., :width], pairs[..., width:], logsum, None
    )
    query_grad = weight_product(entry, dquery)
    dentry = back_product(dquery, cross[2])
    dhidden, gain_grad, shift_grad = norm_back(dentry, normed, inverse, cross[0])
    parts = (gain_grad, shift_grad, query_grad, column_sum(dquery), out_grad, out_bias_grad)
    return (grad + dhidden, parts, jnp.concatenate([dkeys, dvalues], -1))


BF = jnp.bfloat16
F32 = jnp.float32
WIDE = 768
TOKENS = 256
CAPS = 4
SLOT = 64
PAIRS = 6
MESH = pl.DeviceIdType.MESH
LEAD = (2, 2, 2, 2)
Z_FIRST = (3, 7, 11, 15)
EVENTS = (
    (0, 2), (3, 2), (16, 0), (16, 1), (16, 4), (11, 0), (16, 5), (6, 0), (11, 1), (6, 1), (16, 6), (1, 2),
    (7, 0), (5, 0), (4, 0), (2, 2), (10, 0), (7, 1), (4, 1), (0, 3), (5, 1), (9, 0), (1, 3), (9, 1), (8, 0),
    (16, 2), (8, 1), (15, 0), (2, 3), (4, 2), (16, 7), (6, 2), (5, 2), (12, 0), (3, 3), (4, 3), (14, 0),
    (9, 2), (10, 1), (1, 4), (6, 3), (16, 8), (7, 2), (13, 0), (13, 1), (5, 3), (12, 1), (8, 2), (9, 3),
    (11, 2), (16, 10), (15, 1), (8, 3), (2, 4), (10, 2), (5, 4), (16, 9), (13, 2), (7, 3), (10, 3), (8, 4),
    (14, 1), (0, 4), (12, 2), (13, 3), (11, 3), (15, 2), (4, 4), (3, 4), (12, 3), (13, 4), (9, 4), (14, 2),
    (15, 3), (16, 11), (10, 4), (14, 3), (7, 4), (12, 4), (16, 12), (6, 4), (11, 4), (15, 4), (14, 4),
)

def nn(a, b):
    return lax.dot_general(a, b, (((1,), (0,)), ((), ())), preferred_element_type=F32)


def nt(a, b):
    return lax.dot_general(a, b, (((1,), (1,)), ((), ())), preferred_element_type=F32)


def tn(a, b):
    return lax.dot_general(a, b, (((0,), (0,)), ((), ())), preferred_element_type=F32)


def rows_of(i, size):
    return pl.ds(pl.multiple_of(i * size, size), size)


def erf(x):
    return lax.erf(x)


def norm_rows(source, gain, shift, normed, inverse, entry, blocks=range(8)):
    for i in blocks:
        r = pl.ds(32 * i, 32)
        x = source[r, :]
        centred = x - jnp.mean(x, -1, keepdims=True)
        inv = lax.rsqrt(jnp.mean(centred * centred, -1, keepdims=True) + EPS)
        n = centred * inv
        normed[r, :] = n.astype(normed.dtype)
        inverse[r, :] = inv
        entry[r, :] = (n * gain[...] + shift[...]).astype(BF)


def norm_rows_back(grad_entry, normed, inverse, gain, grad, vec, gain_row, shift_row, blocks=range(8)):
    by_gain = jnp.zeros((8, WIDE), F32)
    by_shift = jnp.zeros((8, WIDE), F32)
    for i in blocks:
        r = pl.ds(32 * i, 32)
        d = grad_entry[r, :]
        n = normed[r, :].astype(F32)
        scaled = d * gain[...]
        first = jnp.mean(scaled, -1, keepdims=True)
        second = jnp.mean(scaled * n, -1, keepdims=True)
        grad[r, :] = grad[r, :] + inverse[r, :] * (scaled - first - n * second)
        dn = d * n
        by_gain = by_gain + jnp.sum(dn.reshape(4, 8, WIDE), 0)
        by_shift = by_shift + jnp.sum(d.reshape(4, 8, WIDE), 0)
    for row, part in ((gain_row, by_gain), (shift_row, by_shift)):
        vec[row : row + 1, :] = vec[row : row + 1, :] + jnp.sum(part, 0, keepdims=True)


def sum_columns(rows, count):
    total = jnp.zeros((8, WIDE), F32)
    for i in range(TOKENS // 32):
        for k in range(count):
            part = rows(k, pl.ds(32 * i, 32)).astype(F32)
            total = total + jnp.sum(part.reshape(4, 8, WIDE), 0)
    return jnp.sum(total, 0, keepdims=True)


def mega_kernel(
    lengths, tokens, cotangent, images, h_proj, h_out, h_exp, h_red, h_cq, h_ck, h_cv, h_co,
    again, ashift, qbias, vbias, obias, fgain, fshift, rbias, ebias, cgain, cshift, cqbias, cvbias, cobias,
    out_all,
    GG, WP, WO, WC, R0, R1, R2, R3,
    H, G, D, N1, N2, N3, I1, I2, I3, E, ET1, ET2, ET3,
    QKV, M, MT, QC, CT, SL, AT, PT, PC, IM, KV, B1, B2,
    HIN, MASK, YS, VS, VT, V0, V1, V2, V3, VY, VB, PV,
    wsem, psem, lsem, osem, ysend, yrecv, send_sem, recv_sem, vsend, vrecv, credit,
):
    section = lax.axis_index("section")
    dp = lax.axis_index("dp")
    one = section == 0
    two = section == 1
    bits = [lax.rem(lax.div(dp, 1 << k), 2) for k in range(4)]
    partners = [dp + (1 << k) * (1 - 2 * bits[k]) for k in range(4)]

    barrier = pltpu.get_barrier_semaphore()
    for partner in partners:
        pl.semaphore_signal(barrier, inc=1, device_id={"dp": partner}, device_id_type=MESH)
    pl.semaphore_signal(barrier, inc=1, device_id={"section": 1 - section}, device_id_type=MESH)

    def across(source, target, i):
        return pltpu.make_async_remote_copy(
            src_ref=source, dst_ref=target, send_sem=ysend.at[i], recv_sem=yrecv.at[i],
            device_id={"section": 1 - section}, device_id_type=MESH,
        )

    store_h = pltpu.make_async_copy(E, out_all.at[0:TOKENS], osem.at[0])
    late_h = pltpu.make_async_copy(M, out_all.at[0:TOKENS], osem.at[0])
    store_in = pltpu.make_async_copy(E, out_all.at[TOKENS : 2 * TOKENS], osem.at[1])
    images_a = across(images.at[0:2], IM.at[0:2, 0], 0)
    images_b = across(images.at[2:4], IM.at[2:4, 0], 1)
    send_h = across(E, HIN, 2)
    send_d = [across(E.at[0:128], HIN.at[0:128], 3), across(E.at[128:256], HIN.at[128:256], 10)]
    send_i = across(IM.at[:, 0], KV.at[:, 0, :, :WIDE], 4)

    def load(source, target, i):
        return pltpu.make_async_copy(source, target, wsem.at[i])

    own_images = load(images, IM.at[:, 1], 0)
    own_tokens = load(tokens, HIN, 15)
    own_cotangent = load(cotangent, B1, 16)
    loads = {
        "cross": [load(w, WC.at[i], 1 + i) for i, w in enumerate((h_cq, h_ck, h_cv, h_co))],
        "proj": [load(h_proj, WP, 5)],
        "out": [load(h_out, WO, 6)],
        "exp": [
            load(h_exp.at[:, :, :, :, :, pl.ds(WIDE * j, WIDE)], GG.at[12 + j], 7 + j)
            for j in range(4)
        ],
        "red": [load(h_red.at[j], GG.at[8 + j], 11 + j) for j in range(4)],
    }

    @pl.when(one)
    def _():
        own_tokens.start()

    small = [again, ashift, qbias, vbias, obias, fgain, fshift, rbias]
    small = [(v, PV.at[i : i + 1]) for i, v in enumerate(small)]
    small += [(ebias.at[:, pl.ds(WIDE * j, WIDE)], PV.at[8 + j : 9 + j]) for j in range(4)]
    small += [(v, PV.at[12 + i]) for i, v in enumerate((cgain, cshift, cqbias, cvbias, cobias))]
    small = [pltpu.make_async_copy(v, row, psem.at[i]) for i, (v, row) in enumerate(small)]

    @pl.when(two)
    def _():
        own_images.start()
        for i in (1, 2, 0, 3):
            loads["cross"][i].start()

    for name in ("proj", "out", "exp", "red"):
        for copy in loads[name]:
            copy.start()

    own_cotangent.start()
    for copy in small:
        copy.start()
    again, ashift, qbias, vbias, obias, fgain, fshift, rbias = (PV.at[i : i + 1] for i in range(8))
    cgain, cshift, cqbias, cvbias, cobias = (PV.at[i : i + 1] for i in range(12, 17))

    def arrived(name):
        for copy in loads[name]:
            copy.wait()

    VS[...] = jnp.zeros_like(VS)
    low_lane = lax.broadcasted_iota(jnp.int32, (1, 128), 1) < SLOT
    keep_low = low_lane.astype(F32).astype(BF)
    keep_high = jnp.logical_not(low_lane).astype(F32).astype(BF)

    def stacked(x):
        return jnp.concatenate([x * keep_low, x * keep_high], 0)

    def unstacked(x):
        half = x.shape[0] // 2
        return jnp.where(low_lane, x[:half], x[half:])

    eighth = jnp.asarray(0.125, BF)

    VB[...] = jnp.zeros_like(VB)
    VT[...] = jnp.zeros_like(VT)
    VY[...] = jnp.zeros_like(VY)
    pl.semaphore_wait(barrier, 5)

    @pl.when(one)
    def _():
        images_a.start()

    for pair in range(2):
        key = lax.broadcasted_iota(jnp.int32, (128, 256), 0)
        query = lax.rem(lax.broadcasted_iota(jnp.int32, (128, 256), 1), 128)
        first = key < SLOT
        length = jnp.where(first, lengths[2 * pair], lengths[2 * pair + 1] + SLOT)
        same = first == (query < SLOT)
        MASK[pair] = jnp.where(same & (key <= query) & (key < length), 1.0, 0.0)

    for copy in small:
        copy.wait()

    own_cotangent.wait()
    for c in range(CAPS):
        r = pl.ds(SLOT * c, SLOT)
        live = lax.broadcasted_iota(jnp.int32, (SLOT, 1), 0) < lengths[c]
        G[r, :] = jnp.where(live, B1[r, :].astype(F32), 0.0)
    B1[...] = G[...].astype(BF)

    def pair_rows(which, half):
        rows = IM[2 * which : 2 * which + 2, half].reshape(TOKENS, WIDE)
        keys = nn(rows, WC[1])
        KV[2 * which : 2 * which + 2, half, :, :WIDE] = keys.astype(BF).reshape(2, 128, WIDE)
        values = nn(rows, WC[2]) + cvbias[...]
        KV[2 * which : 2 * which + 2, half, :, WIDE:] = values.astype(BF).reshape(2, 128, WIDE)

    @pl.when(two)
    def _():
        for copy in loads["cross"]:
            copy.wait()
        own_images.wait()
        for which in range(2):
            pair_rows(which, 1)
        images_a.wait_recv()
        pair_rows(0, 0)
        arrived("red")
        for j in range(4):
            SL[j] = nt(B1[...], GG[8 + j].reshape(WIDE, WIDE)).astype(BF)
        send_h.wait_recv()
        H[...] = HIN[...].astype(F32)

    @pl.when(one)
    def _():
        own_tokens.wait()
        H[...] = HIN[...].astype(F32)

    @pl.when(one)
    def _():
        SL[...] = jnp.ones_like(SL)

    norm_rows(H, again, ashift, N1, I1, E)
    ET1[...] = E[...].T
    arrived("proj")
    QKV[0] = (nn(E[...], WP[:, 0:WIDE]) + qbias[...]).astype(BF)
    QKV[1] = nn(E[...], WP[:, WIDE : 2 * WIDE]).astype(BF)
    QKV[2] = (nn(E[...], WP[:, 2 * WIDE :]) + vbias[...]).astype(BF)

    def softmax_keys(scores):
        expo = jnp.exp(scores - jnp.max(scores, 0, keepdims=True))
        return expo * (1.0 / jnp.sum(expo, 0, keepdims=True))

    for hp in range(PAIRS):
        cols = pl.ds(128 * hp, 128)
        for pair in range(2):
            rows = pl.ds(pair * 128, 128)
            query = stacked(QKV[0, rows, cols] * eighth)
            scores = nt(QKV[1, rows, cols], query)
            scores = jnp.where(MASK[pair] > 0.0, scores, NEG)
            probs = softmax_keys(scores).astype(BF)
            PT[2 * hp + pair] = probs
            M[rows, cols] = unstacked(tn(probs, QKV[2, rows, cols])).astype(BF)

    MT[...] = M[...].T
    arrived("out")
    H[...] = H[...] + (nn(M[...], WO[...]) + obias[...])

    @pl.when(two)
    def _():
        norm_rows(H, cgain, cshift, N2, I2, E)
        ET2[...] = E[...].T
        QC[...] = (nn(E[...], WC[0]) + cqbias[...]).astype(BF)

    def cross_forward(half):
        for hp in range(PAIRS):
            cols = pl.ds(128 * hp, 128)
            vcols = pl.ds(WIDE + 128 * hp, 128)
            for c in (2 * half, 2 * half + 1):
                rows = pl.ds(c * SLOT, SLOT)
                query = stacked(QC[rows, cols] * eighth)
                keys = KV[c, :, :, cols].reshape(256, 128)
                probs = softmax_keys(nt(keys, query)).astype(BF)
                PC[4 * hp + c] = probs
                values = KV[c, :, :, vcols].reshape(256, 128)
                M[rows, cols] = unstacked(tn(probs, values)).astype(BF)
        rows = pl.ds(128 * half, 128)
        CT[:, rows] = M[rows, :].T
        H[rows, :] = H[rows, :] + (nn(M[rows, :], WC[3]) + cobias[...])

    def widen(j, rows):
        for t in range(3):
            cols = pl.ds(256 * t, 256)
            u = nn(E[rows, :], GG[12 + j, :, :, :, :, :, cols].reshape(WIDE, 256)) + PV[8 + j : 9 + j, cols]
            cdf = 0.5 * (1.0 + erf(u * 0.7071067811865476))
            M[rows, cols] = (u * cdf).astype(BF)
            slope = cdf + u * jnp.exp(-0.5 * u * u) * 0.3989422804014327
            SL[j, rows, cols] = (SL[j, rows, cols].astype(F32) * slope).astype(BF)
        AT[4 * j : 4 * j + 4, :, :, rows] = M[rows, :].T.reshape(4, 4, 48, rows.size)

    @pl.when(two)
    def _():
        for half in range(2):
            if half == 0:
                arrived("exp")
            else:
                images_b.wait_recv()
                pair_rows(1, 0)
            cross_forward(half)
            rows = pl.ds(128 * half, 128)
            norm_rows(H, fgain, fshift, N3, I3, E, range(4 * half, 4 * half + 4))
            ET3[:, rows] = E[rows, :].T
            for j in range(4):
                widen(j, rows)

    @pl.when(one)
    def _():
        norm_rows(H, fgain, fshift, N3, I3, E)
        ET3[...] = E[...].T
        arrived("exp")
        arrived("red")
        H[...] = H[...] + rbias[...]
        for j in range(4):
            widen(j, pl.ds(0, TOKENS))
            H[...] = H[...] + nn(M[...], GG[8 + j].reshape(WIDE, WIDE))
        E[...] = H[...].astype(BF)
        send_h.start()
        images_b.start()
        store_h.start()
        images_a.wait_send()
        send_h.wait_send()

    @pl.when(one)
    def _():
        store_h.wait()
        send_d[0].wait_recv()
        send_d[1].wait_recv()
        G[...] = G[...] + HIN[...].astype(F32)
        B1[...] = G[...].astype(BF)

    def images_out(source, what):
        for c in range(CAPS):
            target = out_all.at[2 * TOKENS + 128 * c : 2 * TOKENS + 128 * (c + 1)]
            getattr(pltpu.make_async_copy(source.at[c], target, osem.at[2 + c]), what)()

    def shard_place(c):
        return out_all.at[pl.ds(pl.multiple_of(4 * TOKENS + 48 * c, 16), 48)]

    def order(p):
        return (0, 2, 1, 3) if p in Z_FIRST else (0, 1, 2, 3)

    def chunk(p):
        return p if p < 8 else jnp.where(one, p + 4, p)

    def where(p, k, bit):
        done, now = order(p)[:k], order(p)[k]
        places = [bits[a] if a in done else bit if a == now else slice(None) for a in (3, 2, 1, 0)]
        return (chunk(p), *places)

    def landing(p, k):
        if k == 0:
            return R0.at[p % 8]
        return (R1, R2, R3)[k - 1].at[p]

    def exchange(p, k):
        axis = order(p)[k]
        return pltpu.make_async_remote_copy(
            src_ref=GG.at[where(p, k, 1 - bits[axis])], dst_ref=landing(p, k),
            send_sem=send_sem.at[p, k], recv_sem=recv_sem.at[p, k],
            device_id={"dp": partners[axis]}, device_id_type=MESH,
        )

    def begin(p, k):
        if k == 0 and p >= 8:
            pl.semaphore_wait(credit.at[p - 8], 1)
        exchange(p, k).start()

    def finish(p, k):
        exchange(p, k).wait()
        axis = order(p)[k]
        keep, term = GG.at[where(p, k, bits[axis])], landing(p, k)
        for place in itertools.product(range(2), repeat=3 - k):
            keep[place] = keep[place] + term[place]
        if k == 0 and p < 8:
            def give():
                pl.semaphore_signal(
                    credit.at[p], inc=1, device_id={"dp": partners[axis]}, device_id_type=MESH
                )
            give() if p < 4 else pl.when(two)(give)

    def shard(p):
        return GG.at[(chunk(p), *(bits[a] for a in (3, 2, 1, 0)))]

    def shard_out(p):
        return pltpu.make_async_copy(shard(p), shard_place(chunk(p)), lsem.at[p])

    def shard_across(p):
        return across(shard(p), YS.at[p - 8], 6 + p - 8)

    def advance(p, k):
        finish(p, k - 1)
        if k < 4:
            begin(p, k)
        else:
            shard_out(p).start()
            if 8 <= p < 12:
                pl.when(two)(lambda: shard_across(p).start())

    def go(p, k):
        if p >= 12:
            pl.when(two)(lambda: advance(p, k) if k else begin(p, 0))
        elif k:
            advance(p, k)
        else:
            begin(p, 0)

    def sum_part(k, bit):
        return VT.at[tuple(bits[a] if a < k else bit if a == k else slice(None) for a in (3, 2, 1, 0))]

    def sum_copy(k):
        return pltpu.make_async_remote_copy(
            src_ref=sum_part(k, 1 - bits[k]), dst_ref=(V0, V1, V2, V3)[k],
            send_sem=vsend.at[k], recv_sem=vrecv.at[k],
            device_id={"dp": partners[k]}, device_id_type=MESH,
        )

    def sum_add(k):
        sum_copy(k).wait()
        keep, term = sum_part(k, bits[k]), (V0, V1, V2, V3)[k]
        for place in itertools.product(range(2), repeat=3 - k):
            keep[place] = keep[place] + term[place]

    def sum_shards():
        for d in range(16):
            place = ((d >> 3) & 1, (d >> 2) & 1, (d >> 1) & 1, d & 1)
            VT[(*place, slice(None), slice(0, 48))] = VS[:, 48 * d : 48 * (d + 1)]
            for i in range(4):
                first = 192 * (d % 4) + 48 * i
                VT[(*place, slice(8 + i, 9 + i), slice(0, 48))] = VS[8 + d // 4 : 9 + d // 4, first : first + 48]

    def sum_result():
        return VT.at[tuple(bits[a] for a in (3, 2, 1, 0))]

    def weight_gradient(c, left, right):
        for t in range(3):
            part = nn(left, right(pl.ds(256 * t, 256)))
            GG[c, :, :, :, :, :, pl.ds(256 * t, 256)] = part.astype(BF).reshape(LEAD + (48, 256))


    def reduce_chunk(i):
        weight_gradient(i, AT[:, i].reshape(WIDE, TOKENS), lambda t: B1[:, t])
        go(i, 0)

    reduce_chunk(0)
    reduce_chunk(1)


    @pl.when(one)
    def _():
        for j in range(4):
            for i in range(2):
                r = pl.ds(128 * i, 128)
                da = nt(B1[r, :], GG[8 + j].reshape(WIDE, WIDE))
                SL[j, r, :] = (da * SL[j, r, :].astype(F32)).astype(BF)

    total = nt(SL[0], GG[12].reshape(WIDE, WIDE))
    for j in range(1, 4):
        total = total + nt(SL[j], GG[12 + j].reshape(WIDE, WIDE))
    D[...] = total

    go(0, 1)
    go(1, 1)
    reduce_chunk(2)
    reduce_chunk(3)

    norm_rows_back(D, N3, I3, fgain, G, VS, 5, 6)

    @pl.when(one)
    def _():
        go(2, 1)
        go(3, 1)

    def cross_back(half):
        rows = pl.ds(128 * half, 128)
        B2[rows, :] = G[rows, :].astype(BF)
        E[rows, :] = nt(B2[rows, :], WC[3]).astype(BF)
        for hp in range(PAIRS):
            cols = pl.ds(128 * hp, 128)
            vcols = pl.ds(WIDE + 128 * hp, 128)
            for c in (2 * half, 2 * half + 1):
                own = pl.ds(c * SLOT, SLOT)
                query = stacked(QC[own, cols] * eighth)
                grad = stacked(E[own, cols])
                keys = KV[c, :, :, cols].reshape(256, 128)
                values = KV[c, :, :, vcols].reshape(256, 128)
                probs = PC[4 * hp + c]
                wide = probs.astype(F32)
                dprobs = nt(values, grad)
                dscores = (wide * (dprobs - jnp.sum(wide * dprobs, 0, keepdims=True))).astype(BF)
                KV[c, :, :, cols] = nn(dscores, query).astype(BF).reshape(2, 128, 128)
                KV[c, :, :, vcols] = nn(probs, grad).astype(BF).reshape(2, 128, 128)
                QC[own, cols] = (unstacked(tn(dscores, keys)) * 0.125).astype(BF)
        D[rows, :] = nt(QC[rows, :], WC[0])
        norm_rows_back(D, N2, I2, cgain, G, VS, 12, 13, range(4 * half, 4 * half + 4))

    def self_back(pairs):
        rows = pl.ds(128 * pairs[0], 128 * len(pairs))
        HIN[rows, :] = G[rows, :].astype(BF)
        E[rows, :] = nt(HIN[rows, :], WO[...]).astype(BF)
        for hp in range(PAIRS):
            cols = pl.ds(128 * hp, 128)
            for pair in pairs:
                own = pl.ds(pair * 128, 128)
                query = stacked(QKV[0, own, cols] * eighth)
                grad = stacked(E[own, cols])
                keys = QKV[1, own, cols]
                probs = PT[2 * hp + pair]
                wide = probs.astype(F32)
                dprobs = nt(QKV[2, own, cols], grad)
                dscores = (wide * (dprobs - jnp.sum(wide * dprobs, 0, keepdims=True))).astype(BF)
                QKV[1, own, cols] = nn(dscores, query).astype(BF)
                QKV[2, own, cols] = nn(probs, grad).astype(BF)
                QKV[0, own, cols] = (unstacked(tn(dscores, keys)) * 0.125).astype(BF)
        total = nt(QKV[0, rows, :], WP[:, 0:WIDE])
        total = total + nt(QKV[1, rows, :], WP[:, WIDE : 2 * WIDE])
        D[rows, :] = total + nt(QKV[2, rows, :], WP[:, 2 * WIDE :])
        norm_rows_back(D, N1, I1, again, G, VS, 0, 1, range(4 * pairs[0], 4 * pairs[-1] + 4))
        E[rows, :] = G[rows, :].astype(BF)

    @pl.when(two)
    def _():
        for half in range(2):
            cross_back(half)
            if half == 0:
                go(2, 1)
                go(3, 1)
            self_back((half,))
            send_d[half].start()

    @pl.when(one)
    def _():
        self_back((0, 1))

    store_in.start()

    def late_sums():
        for j in range(4):
            VS[8 + j : 9 + j, :] = sum_columns(lambda k, r: SL[j, r, :], 1)
        VS[7:8, :] = sum_columns(lambda k, r: B1[r, :], 1)
        VS[2:3, :] = sum_columns(lambda k, r: QKV[0, r, :], 1)
        VS[3:4, :] = sum_columns(lambda k, r: QKV[2, r, :], 1)
        VS[4:5, :] = sum_columns(lambda k, r: HIN[r, :], 1)

        @pl.when(two)
        def _():
            VS[14:15, :] = sum_columns(lambda k, r: QC[r, :], 1)
            VS[16:17, :] = sum_columns(lambda k, r: B2[r, :], 1)
            VS[15:16, :] = sum_columns(
                lambda k, r: KV[k, :, pl.ds(r.start // 2, 16), WIDE:].reshape(32, WIDE), 4
            )

    def late_output():
        @pl.when(two)
        def _():
            H[...] = H[...] + rbias[...]
            for j in range(4):
                a = AT[4 * j : 4 * j + 4].reshape(WIDE, TOKENS)
                H[...] = H[...] + tn(a, GG[8 + j].reshape(WIDE, WIDE))
            M[...] = H[...].astype(BF)
            late_h.start()

    def turn_images():
        @pl.when(two)
        def _():
            for c in range(CAPS):
                AT[4 * c : 4 * c + 4] = IM[c].reshape(256, WIDE).T.reshape(4, 4, 48, TOKENS)

    def image_gradient():
        @pl.when(two)
        def _():
            for c in range(CAPS):
                part = nt(KV[c, :, :, :WIDE].reshape(256, WIDE), WC[1])
                part = part + nt(KV[c, :, :, WIDE:].reshape(256, WIDE), WC[2])
                IM[c] = part.astype(BF).reshape(2, 128, WIDE)
            send_i.start()
            images_out(IM.at[:, 1], "start")

    def image_pairs(j):
        for t in range(3):
            cols = pl.ds(WIDE * j + 256 * t, 256)
            part = sum(
                nn(AT[4 * c : 4 * c + 4].reshape(WIDE, TOKENS), KV[c, :, :, cols].reshape(256, 256))
                for c in range(CAPS)
            )
            GG[9 + j, :, :, :, :, :, pl.ds(256 * t, 256)] = part.astype(BF).reshape(LEAD + (48, 256))

    def self_chunk(i):
        if i < 3:
            weight_gradient(12 + i, ET1[...], lambda t: QKV[i, :, t])
        else:
            weight_gradient(15, MT[...], lambda t: HIN[:, t])

    def cross_chunk(i):
        if i == 0:
            weight_gradient(8, ET2[...], lambda t: QC[:, t])
        elif i < 3:
            image_pairs(i - 1)
        else:
            weight_gradient(11, CT[...], lambda t: B2[:, t])

    def compute(p):
        if p < 8:
            weight_gradient(p, ET3[...], lambda t: SL[p - 4, :, t])
        elif p < 12:
            pl.when(one)(lambda: self_chunk(p - 8))
            pl.when(two)(lambda: cross_chunk(p - 8))
        else:
            pl.when(two)(lambda: self_chunk(p - 12))

    def sums(k):
        if k > 0:
            sum_add(k - 1)
        else:
            sum_shards()
        if k < 4:
            sum_copy(k).start()
        else:
            pl.when(two)(lambda: across(sum_result(), VY, 5).start())

    def images_end():
        @pl.when(one)
        def _():
            images_b.wait_send()
            send_i.wait_recv()
            images_out(KV.at[:, 0, :, :WIDE], "start")

    def sums_end():
        pl.when(one)(lambda: across(sum_result(), VY, 5).wait_recv())
        crossed = lax.broadcasted_iota(jnp.int32, (24, 128), 0) >= 12
        final = jnp.where(crossed & one, VY[...], sum_result()[...])
        high = final.astype(BF)
        VB[0:24, 0:128] = high
        VB[24:48, 0:128] = (final - high.astype(F32)).astype(BF)
        store_v.start()

    def shards_end():
        @pl.when(one)
        def _():
            for i in range(4):
                across(YS.at[i], YS.at[i], 6 + i).wait_recv()
                shard_copies[i].start()

    store_v = pltpu.make_async_copy(VB, out_all.at[7 * TOKENS : 7 * TOKENS + 48], osem.at[6])
    shard_copies = [pltpu.make_async_copy(YS.at[i], shard_place(8 + i), lsem.at[12 + i]) for i in range(4)]
    work = {0: late_sums, 1: late_output, 2: image_gradient, 4: turn_images, 10: images_end, 11: sums_end, 12: shards_end}
    work.update({5 + k: functools.partial(sums, k) for k in range(5)})

    for p, k in EVENTS:
        if p == 16:
            work[k]()
            continue
        if k == 0:
            compute(p)
        go(p, k)

    @pl.when(two)
    def _():
        across(sum_result(), VY, 5).wait_send()
        images_out(IM.at[:, 1], "wait")
        send_d[0].wait_send()
        send_d[1].wait_send()
        send_i.wait_send()
        late_h.wait()
        for p in range(8, 12):
            shard_across(p).wait_send()
        for p in range(12, 16):
            shard_out(p).wait()

    @pl.when(one)
    def _():
        for copy in shard_copies:
            copy.wait()
        images_out(KV.at[:, 0, :, :WIDE], "wait")

    store_in.wait()
    store_v.wait()
    for p in range(12):
        shard_out(p).wait()


def mega(args):
    (
        tokens, images, lengths, cotangent, again, ashift, proj, qb, vb, wo, ob, fg, fs, we, eb, wr, rb,
        cg, cs, cq, cqb, ck, cv, cvb, co, cob,
    ) = args
    operands = (
        lengths, tokens.reshape(TOKENS, WIDE), cotangent.reshape(TOKENS, WIDE), images,
        proj[0], wo[0], we.reshape(LEAD + (48, 4 * WIDE)), wr.reshape((4,) + LEAD + (48, WIDE)), cq, ck, cv, co,
        again, ashift, qb, vb, ob, fg, fs, rb, eb, cg, cs, cqb, cvb, cob,
    )
    hbm = pl.BlockSpec(memory_space=pl.ANY)
    dma = pltpu.SemaphoreType.DMA
    big = (TOKENS, WIDE)
    turned = (WIDE, TOKENS)
    b = lambda *shape: pltpu.VMEM(shape, BF)
    f = lambda *shape: pltpu.VMEM(shape, F32)
    return pl.pallas_call(
        mega_kernel,
        out_shape=jax.ShapeDtypeStruct((7 * TOKENS + 48, WIDE), BF),
        in_specs=[pl.BlockSpec(memory_space=pltpu.SMEM)] + [hbm] * (len(operands) - 1),
        out_specs=hbm,
        scratch_shapes=[
            b(16, *LEAD, 48, WIDE), b(WIDE, 3 * WIDE), b(WIDE, WIDE), b(4, WIDE, WIDE),
            b(8, 2, 2, 2, 48, WIDE), b(16, 2, 2, 48, WIDE), b(16, 2, 48, WIDE), b(16, 48, WIDE),
            f(*big), f(*big), f(*big), b(*big), b(*big), b(*big), f(TOKENS, 1), f(TOKENS, 1), f(TOKENS, 1),
            b(*big), b(*turned), b(*turned), b(*turned),
            b(3, *big), b(*big), b(*turned), b(*big), b(*turned), b(4, *big),
            b(16, 4, 48, TOKENS), b(12, 128, 256), b(24, 256, 128), b(CAPS, 2, 128, WIDE),
            b(CAPS, 2, 128, 2 * WIDE), b(*big), b(*big),
            b(*big), f(2, 128, 256), b(4, 48, WIDE), f(24, WIDE), f(*LEAD, 24, 128), f(2, 2, 2, 24, 128), f(2, 2, 24, 128),
            f(2, 24, 128), f(24, 128), f(24, 128), b(48, WIDE), f(24, WIDE),
            dma((17,)), dma((17,)), dma((16,)), dma((7,)), dma((11,)), dma((11,)),
            dma((16, 4)), dma((16, 4)), dma((4,)), dma((4,)), pltpu.SemaphoreType.REGULAR((8,)),
        ],
        compiler_params=pltpu.CompilerParams(
            collective_id=0, has_side_effects=True, vmem_limit_bytes=63 * 2**20
        ),
        name="layers",
    )(*operands)


def finish_kernel(every, *outs):
    (
        o_h, o_in, o_img, o_ag, o_as, o_proj, o_qb, o_vb, o_wo, o_ob, o_fg, o_fs, o_we, o_eb, o_wr, o_rb,
        o_cg, o_cs, o_cq, o_cqb, o_ck, o_cv, o_cvb, o_co, o_cob,
    ) = outs
    o_h[...] = every[0:TOKENS, :].reshape(o_h.shape)
    o_in[...] = every[TOKENS : 2 * TOKENS, :].astype(F32).reshape(o_in.shape)
    o_img[...] = every[2 * TOKENS : 4 * TOKENS, :].astype(F32).reshape(o_img.shape)
    shards = [every[4 * TOKENS + 48 * j : 4 * TOKENS + 48 * (j + 1), :].astype(F32) for j in range(16)]
    vec = every[7 * TOKENS : 7 * TOKENS + 48, 0:128].astype(F32)
    vec = vec[:24] + vec[24:]
    for j in range(3):
        o_proj[0, :, WIDE * j : WIDE * (j + 1)] = shards[12 + j]
    o_wo[0] = shards[15]
    for j in range(4):
        o_we[0, :, WIDE * j : WIDE * (j + 1)] = shards[4 + j]
        o_wr[0, 48 * j : 48 * (j + 1), :] = shards[j]
    for j, out in enumerate((o_cq, o_ck, o_cv, o_co)):
        out[...] = shards[8 + j]
    places = (
        (o_ag, 0), (o_as, 1), (o_qb, 2), (o_vb, 3), (o_ob, 4), (o_fg, 5), (o_fs, 6), (o_rb, 7),
        (o_cg, 12), (o_cs, 13), (o_cqb, 14), (o_cvb, 15), (o_cob, 16),
    )
    for out, i in places:
        out[...] = vec[i : i + 1, :48]
    for i in range(4):
        o_eb[:, 48 * i : 48 * (i + 1)] = vec[8 + i : 9 + i, :48]


def finish_outputs(every):
    vm = pl.BlockSpec(memory_space=pltpu.VMEM)
    small = (1, 48)
    shapes = [
        (1, CAPS, SLOT, WIDE), (1, CAPS, SLOT, WIDE), (CAPS, 128, WIDE),
        small, small, (1, 48, 3 * WIDE), small, small, (1, 48, WIDE), small, small, small,
        (1, 48, 4 * WIDE), (1, 192), (1, 192, WIDE), small,
        small, small, (48, WIDE), small, (48, WIDE), (48, WIDE), small, (48, WIDE), small,
    ]
    outs = pl.pallas_call(
        finish_kernel,
        out_shape=[jax.ShapeDtypeStruct(x, BF if i == 0 else F32) for i, x in enumerate(shapes)],
        in_specs=[vm],
        out_specs=[vm] * 25,
        compiler_params=pltpu.CompilerParams(vmem_limit_bytes=40 * 2**20),
        name="finish",
    )(every)
    outs = list(outs)
    for i in (16, 17, 19, 22, 24):
        outs[i] = outs[i].reshape(-1)
    return tuple(outs)


def body(
    tokens,
    images,
    lengths,
    cotangent,
    attend_gain,
    attend_shift,
    projections,
    query_bias,
    value_bias,
    output_weight,
    output_bias,
    feed_gain,
    feed_shift,
    expand_weight,
    expand_bias,
    reduce_weight,
    reduce_bias,
    cross_gain,
    cross_shift,
    cross_query,
    cross_query_bias,
    cross_key,
    cross_value,
    cross_value_bias,
    cross_out,
    cross_out_bias,
):
    layer = tuple(
        (
            weight[0]
            for weight in (
                attend_gain,
                attend_shift,
                projections,
                query_bias,
                value_bias,
                output_weight,
                output_bias,
                feed_gain,
                feed_shift,
                expand_weight,
                expand_bias,
                reduce_weight,
                reduce_bias,
            )
        )
    )
    cross = (
        cross_gain,
        cross_shift,
        cross_query,
        cross_query_bias,
        cross_key,
        cross_value,
        cross_value_bias,
        cross_out,
        cross_out_bias,
    )
    pair_weight = jnp.concatenate([cross_key, cross_value], 1)
    pair_bias = jnp.concatenate([jnp.zeros_like(cross_value_bias), cross_value_bias], 0)
    section_index = lax.axis_index("section")
    is_two = section_index == 1
    block = MB_CAPS
    half = images.shape[1]
    slots = tokens.shape[1]
    width = tokens.shape[2]
    positions = jnp.arange(slots, dtype=jnp.int32)
    causal = positions[None, :] <= positions[:, None]
    zero_cross = tuple((jnp.zeros(weight.shape, jnp.float32) for weight in cross))

    def image_project(image_rows):
        return (product(image_rows, pair_weight) + pair_bias).astype(jnp.bfloat16)

    def image_back(image_rows, dpairs):
        dimages = back_product(dpairs, pair_weight)
        pair_grad = weight_product(image_rows, dpairs)
        return (
            dimages,
            (pair_grad[:, :width], pair_grad[:, width:], column_sum(dpairs[..., width:])),
        )

    def cross_yes(hidden, image_data):
        pairs = image_project(image_data)
        after, saved = cross_forward(hidden, pairs, cross)
        return (after, saved, pairs)

    def cross_no(hidden, image_data):
        saved = (
            jnp.zeros((block, slots, width), jnp.float32),
            jnp.zeros((block, slots, 1), jnp.float32),
            jnp.zeros((block, slots, width), jnp.bfloat16),
            jnp.zeros((block, slots, width), jnp.bfloat16),
            jnp.zeros((block, slots, width), jnp.bfloat16),
            jnp.zeros((block, HEADS, slots, 1), jnp.float32),
        )
        return (hidden, saved, jnp.zeros((block, 2 * half, 2 * width), jnp.bfloat16))

    def back_yes(grad, saved, pairs, image_data):
        dgrad, parts, dpairs = cross_back(grad, saved, pairs, cross)
        dimages, image_terms = image_back(image_data, dpairs)
        return (dgrad, parts[:4] + image_terms + parts[4:], dimages)

    def back_no(grad, saved, pairs, image_data):
        return (grad, zero_cross, jnp.zeros((block, 2 * half, width), jnp.float32))

    received = jnp.zeros((block, slots, width), jnp.bfloat16)
    arriving = jnp.zeros((block, half, width), jnp.bfloat16)
    finished = jnp.zeros(tokens.shape, jnp.bfloat16)
    kept = []
    for tick in range(MICRO + 1):
        index = jnp.clip(tick - section_index, 0, MICRO - 1)
        start = index * block
        live = positions[None, :] < lax.dynamic_slice_in_dim(lengths, start, block, 0)[:, None]
        mask = live[:, None, :] & causal[None]
        own_tokens = lax.dynamic_slice_in_dim(tokens, start, block, 0)
        own_images = lax.dynamic_slice_in_dim(images, start, block, 0)
        hidden = jnp.where(is_two, received, own_tokens).astype(jnp.float32)
        after_self, self_saved = self_forward(hidden, layer, mask)
        image_data = jnp.concatenate([arriving, own_images], 1)
        after_cross, cross_saved, pairs = lax.cond(
            is_two, cross_yes, cross_no, after_self, image_data
        )
        final, feed_saved = feed_forward(after_cross, layer)
        result = final.astype(jnp.bfloat16)
        finished = lax.dynamic_update_slice_in_dim(finished, result, start, 0)
        kept.append((mask, live, self_saved, cross_saved, feed_saved, pairs, image_data))
        if tick < MICRO:
            received = shifted(result, "section", 1)
            arriving = shifted(own_images, "section", 1)
    layer_sums = tuple((jnp.zeros(weight.shape, jnp.float32) for weight in layer))
    cross_sums = zero_cross
    input_grads = jnp.zeros(tokens.shape, jnp.float32)
    image_grads = jnp.zeros(images.shape, jnp.float32)
    returning = jnp.zeros((block, slots, width), jnp.bfloat16)
    coming = jnp.zeros((block, half, width), jnp.float32)
    for turn in range(MICRO + 1):
        tick = MICRO - turn
        offset = tick - section_index
        index = jnp.clip(offset, 0, MICRO - 1)
        start = index * block
        valid = ((offset >= 0) & (offset < MICRO)).astype(jnp.float32)
        mask, live, self_saved, cross_saved, feed_saved, pairs, image_data = kept[tick]
        own_images = lax.dynamic_slice_in_dim(images, start, block, 0)
        seed_grad = lax.dynamic_slice_in_dim(cotangent[0], start, block, 0).astype(
            jnp.float32
        ) * live[..., None].astype(jnp.float32)
        grad = seed_grad + returning.astype(jnp.float32)
        grad, feed_grads = feed_back(grad, feed_saved, layer)
        grad, cross_grads, image_part = lax.cond(
            is_two, back_yes, back_no, grad, cross_saved, pairs, image_data
        )
        grad, self_grads = self_back(grad, self_saved, layer, mask)
        layer_sums = tuple(
            (total + valid * part for total, part in zip(layer_sums, self_grads + feed_grads))
        )
        cross_sums = tuple((total + valid * part for total, part in zip(cross_sums, cross_grads)))
        sent = grad.astype(jnp.bfloat16)
        stored = jnp.where(is_two, sent.astype(jnp.float32), grad)
        input_grads = jnp.where(
            valid > 0, lax.dynamic_update_slice_in_dim(input_grads, stored, start, 0), input_grads
        )
        own_dimages = jnp.where(is_two, image_part[:, half:], coming)
        image_grads = jnp.where(
            valid > 0,
            lax.dynamic_update_slice_in_dim(image_grads, own_dimages, start, 0),
            image_grads,
        )
        if turn < MICRO:
            returning = shifted(sent, "section", -1)
            coming = shifted(image_part[:, :half].astype(jnp.bfloat16), "section", -1).astype(
                jnp.float32
            )
    shared = lax.psum_scatter(
        tuple((total[None] for total in layer_sums)), "dp", scatter_dimension=1, tiled=True
    )
    scattered = lax.psum_scatter(cross_sums, "dp", scatter_dimension=0, tiled=True)
    crossed = jax.tree.map(
        lambda part: part.astype(jnp.float32), lax.psum(for_sending(tuple(scattered)), "section")
    )
    return (finished[None], input_grads[None], image_grads) + tuple(shared) + tuple(crossed)


def one_kernel(*args):
    return finish_outputs(mega(args))


def solution(mesh):
    placed = (
        P("dp", None, None),
        P("dp", "section", None),
        P("dp"),
        P("section", "dp", None, None),
        P("section", None),
        P("section", None),
        P("section", None, None),
        P("section", None),
        P("section", None),
        P("section", None, None),
        P("section", None),
        P("section", None),
        P("section", None),
        P("section", None, None),
        P("section", None),
        P("section", None, None),
        P("section", None),
        P(),
        P(),
        P(),
        P(),
        P(),
        P(),
        P(),
        P(),
        P(),
    )
    return jax.shard_map(
        one_kernel if mesh.shape["dp"] == 16 else body,
        mesh=mesh,
        in_specs=placed,
        out_specs=(
            P("section", "dp", None, None),
            P("section", "dp", None, None),
            P("dp", "section", None),
            P("section", "dp"),
            P("section", "dp"),
            P("section", "dp", None),
            P("section", "dp"),
            P("section", "dp"),
            P("section", "dp", None),
            P("section", "dp"),
            P("section", "dp"),
            P("section", "dp"),
            P("section", "dp", None),
            P("section", "dp"),
            P("section", "dp", None),
            P("section", "dp"),
            P("dp"),
            P("dp"),
            P("dp", None),
            P("dp"),
            P("dp", None),
            P("dp", None),
            P("dp"),
            P("dp", None),
            P("dp"),
        ),
        check_vma=False,
    )
```

```python
import functools
import itertools

import jax
import jax.numpy as jnp
from jax import lax
from jax.experimental import pallas as pl
from jax.experimental.pallas import tpu as pltpu
from jax.sharding import PartitionSpec as P

HEADS = 12
HEAD_DIM = 64
MB_CAPS = 4
MICRO = 1


EPS = 1e-05
NEG = -1000000000.0


def shifted(block, axis, distance):
    devices = range(lax.axis_size(axis))
    route = [(i - distance, i) for i in devices if i - distance in devices]
    return lax.ppermute(block, axis, route)


def for_sending(array):
    return jax.tree.map(lambda a: a.astype(jnp.bfloat16) if a.dtype == jnp.float32 else a, array)


def layer_norm(rows, gain, shift):
    mean = jnp.mean(rows, -1, keepdims=True)
    centred = rows - mean
    inverse = lax.rsqrt(jnp.mean(centred * centred, -1, keepdims=True) + EPS)
    normed = centred * inverse
    return (normed * gain + shift, normed, inverse)


def norm_back(grad, normed, inverse, gain):
    scaled = grad * gain
    inner = (
        scaled
        - jnp.mean(scaled, -1, keepdims=True)
        - normed * jnp.mean(scaled * normed, -1, keepdims=True)
    )
    return (inverse * inner, jnp.sum(grad * normed, axis=(0, 1)), jnp.sum(grad, axis=(0, 1)))


def product(rows, weight):
    return jnp.einsum("bsi,ij->bsj", rows, weight, preferred_element_type=jnp.float32)


def back_product(grad, weight):
    return jnp.einsum("bsj,ij->bsi", grad, weight, preferred_element_type=jnp.float32)


def weight_product(rows, grad):
    return jnp.einsum("bsi,bsj->ij", rows, grad, preferred_element_type=jnp.float32)


def column_sum(grad):
    return jnp.sum(grad.astype(jnp.float32), axis=(0, 1))


def split_heads(rows):
    return rows.reshape(rows.shape[0], rows.shape[1], HEADS, HEAD_DIM)


def scores_of(query, keys, mask):
    scores = jnp.einsum(
        "bqhd,bkhd->bhqk", split_heads(query), split_heads(keys), preferred_element_type=jnp.float32
    ) * HEAD_DIM ** (-0.5)
    if mask is None:
        return scores
    return jnp.where(mask[:, None], scores, NEG)


def attend(query, keys, values, mask):
    scores = scores_of(query, keys, mask)
    top = jnp.max(scores, -1, keepdims=True)
    expo = jnp.exp(scores - top)
    total = jnp.sum(expo, -1, keepdims=True)
    probs = (expo / total).astype(jnp.bfloat16)
    mixed = jnp.einsum(
        "bhqk,bkhd->bqhd", probs, split_heads(values), preferred_element_type=jnp.float32
    )
    return (mixed.reshape(query.shape).astype(jnp.bfloat16), top + jnp.log(total))


def attend_back(grad, query, keys, values, logsum, mask):
    scale = HEAD_DIM ** (-0.5)
    probs = jnp.exp(scores_of(query, keys, mask) - logsum)
    grad_heads = split_heads(grad)
    dprobs = jnp.einsum(
        "bqhd,bkhd->bhqk", grad_heads, split_heads(values), preferred_element_type=jnp.float32
    )
    rowdot = jnp.sum(probs * dprobs, -1, keepdims=True)
    dscores = (probs * (dprobs - rowdot)).astype(jnp.bfloat16)
    dquery = (
        jnp.einsum(
            "bhqk,bkhd->bqhd", dscores, split_heads(keys), preferred_element_type=jnp.float32
        )
        * scale
    )
    dkeys = (
        jnp.einsum(
            "bhqk,bqhd->bkhd", dscores, split_heads(query), preferred_element_type=jnp.float32
        )
        * scale
    )
    dvalues = jnp.einsum(
        "bhqk,bqhd->bkhd",
        probs.astype(jnp.bfloat16),
        grad_heads,
        preferred_element_type=jnp.float32,
    )
    return (
        dquery.reshape(query.shape).astype(jnp.bfloat16),
        dkeys.reshape(keys.shape).astype(jnp.bfloat16),
        dvalues.reshape(values.shape).astype(jnp.bfloat16),
    )


def self_forward(hidden, layer, mask):
    normal, normed, inverse = layer_norm(hidden, layer[0], layer[1])
    entry = normal.astype(jnp.bfloat16)
    packed = product(entry, layer[2])
    width = hidden.shape[-1]
    query = (packed[..., :width] + layer[3]).astype(jnp.bfloat16)
    keys = packed[..., width : 2 * width].astype(jnp.bfloat16)
    values = (packed[..., 2 * width :] + layer[4]).astype(jnp.bfloat16)
    mixed, logsum = attend(query, keys, values, mask)
    after = hidden + (product(mixed, layer[5]) + layer[6])
    return (after, (normed, inverse, entry, query, keys, values, mixed, logsum))


def self_back(grad, saved, layer, mask):
    normed, inverse, entry, query, keys, values, mixed, logsum = saved
    branch = grad.astype(jnp.bfloat16)
    out_weight_grad = weight_product(mixed, branch)
    out_bias_grad = column_sum(branch)
    dmixed = back_product(branch, layer[5]).astype(jnp.bfloat16)
    dquery, dkeys, dvalues = attend_back(dmixed, query, keys, values, logsum, mask)
    dpacked = jnp.concatenate([dquery, dkeys, dvalues], -1)
    packed_grad = weight_product(entry, dpacked)
    dentry = back_product(dpacked, layer[2])
    dhidden, gain_grad, shift_grad = norm_back(dentry, normed, inverse, layer[0])
    return (
        grad + dhidden,
        (
            gain_grad,
            shift_grad,
            packed_grad,
            column_sum(dquery),
            column_sum(dvalues),
            out_weight_grad,
            out_bias_grad,
        ),
    )


def gelu_slope(expanded):
    normal_cdf = 0.5 * (1.0 + jax.scipy.special.erf(expanded * 0.7071067811865476))
    return normal_cdf + expanded * jnp.exp(-0.5 * expanded * expanded) * 0.3989422804014327


def feed_forward(hidden, layer):
    normal, normed, inverse = layer_norm(hidden, layer[7], layer[8])
    entry = normal.astype(jnp.bfloat16)
    expanded = product(entry, layer[9]) + layer[10]
    active = jax.nn.gelu(expanded, approximate=False).astype(jnp.bfloat16)
    after = hidden + (product(active, layer[11]) + layer[12])
    return (after, (normed, inverse, entry, expanded, active))


def feed_back(grad, saved, layer):
    normed, inverse, entry, expanded, active = saved
    branch = grad.astype(jnp.bfloat16)
    reduce_grad = weight_product(active, branch)
    reduce_bias_grad = column_sum(branch)
    dactive = back_product(branch, layer[11])
    dexpanded = (dactive * gelu_slope(expanded)).astype(jnp.bfloat16)
    expand_grad = weight_product(entry, dexpanded)
    expand_bias_grad = column_sum(dexpanded)
    dentry = back_product(dexpanded, layer[9])
    dhidden, gain_grad, shift_grad = norm_back(dentry, normed, inverse, layer[7])
    return (
        grad + dhidden,
        (gain_grad, shift_grad, expand_grad, expand_bias_grad, reduce_grad, reduce_bias_grad),
    )


def cross_forward(hidden, pairs, cross):
    normal, normed, inverse = layer_norm(hidden, cross[0], cross[1])
    entry = normal.astype(jnp.bfloat16)
    query = (product(entry, cross[2]) + cross[3]).astype(jnp.bfloat16)
    width = hidden.shape[-1]
    mixed, logsum = attend(query, pairs[..., :width], pairs[..., width:], None)
    after = hidden + (product(mixed, cross[7]) + cross[8])
    return (after, (normed, inverse, entry, query, mixed, logsum))


def cross_back(grad, saved, pairs, cross):
    normed, inverse, entry, query, mixed, logsum = saved
    width = grad.shape[-1]
    branch = grad.astype(jnp.bfloat16)
    out_grad = weight_product(mixed, branch)
    out_bias_grad = column_sum(branch)
    dmixed = back_product(branch, cross[7]).astype(jnp.bfloat16)
    dquery, dkeys, dvalues = attend_back(
        dmixed, query, pairs[..., :width], pairs[..., width:], logsum, None
    )
    query_grad = weight_product(entry, dquery)
    dentry = back_product(dquery, cross[2])
    dhidden, gain_grad, shift_grad = norm_back(dentry, normed, inverse, cross[0])
    parts = (gain_grad, shift_grad, query_grad, column_sum(dquery), out_grad, out_bias_grad)
    return (grad + dhidden, parts, jnp.concatenate([dkeys, dvalues], -1))


BF = jnp.bfloat16
F32 = jnp.float32
WIDE = 768
TOKENS = 256
CAPS = 4
SLOT = 64
PAIRS = 6
MESH = pl.DeviceIdType.MESH
LEAD = (2, 2, 2, 2)
Z_FIRST = (1, 5, 9, 13, 17, 21, 25, 29)
EVENTS = (
    (32, 0), (32, 5), (8, 0), (10, 0), (9, 0), (11, 0), (12, 0), (13, 0), (14, 0), (0, 2), (1, 2), (15, 0),
    (32, 1), (32, 4), (16, 0), (2, 2), (0, 3), (8, 1), (3, 2), (17, 0), (18, 0), (9, 1), (4, 2), (1, 3),
    (2, 3), (32, 6), (0, 4), (10, 1), (5, 2), (3, 3), (19, 0), (20, 0), (11, 1), (6, 2), (4, 3), (1, 4),
    (2, 4), (32, 7), (12, 1), (7, 2), (3, 4), (21, 0), (22, 0), (13, 1), (8, 2), (5, 3), (6, 3), (4, 4),
    (14, 1), (32, 8), (9, 2), (7, 3), (23, 0), (24, 0), (15, 1), (10, 2), (8, 3), (5, 4), (6, 4), (16, 1),
    (11, 2), (32, 9), (7, 4), (25, 0), (26, 0), (17, 1), (32, 2), (12, 2), (9, 3), (10, 3), (8, 4), (18, 1),
    (13, 2), (11, 3), (27, 0), (28, 0), (19, 1), (14, 2), (12, 3), (9, 4), (10, 4), (20, 1), (15, 2), (11, 4),
    (29, 0), (30, 0), (21, 1), (16, 2), (13, 3), (14, 3), (12, 4), (22, 1), (17, 2), (15, 3), (31, 0), (23, 1),
    (18, 2), (16, 3), (13, 4), (14, 4), (24, 1), (19, 2), (15, 4), (25, 1), (20, 2), (17, 3), (18, 3), (16, 4),
    (26, 1), (21, 2), (19, 3), (27, 1), (22, 2), (20, 3), (17, 4), (18, 4), (28, 1), (32, 10), (23, 2),
    (19, 4), (29, 1), (24, 2), (21, 3), (22, 3), (20, 4), (30, 1), (25, 2), (23, 3), (31, 1), (26, 2), (24, 3),
    (21, 4), (22, 4), (27, 2), (23, 4), (28, 2), (25, 3), (26, 3), (24, 4), (29, 2), (27, 3), (30, 2), (28, 3),
    (25, 4), (26, 4), (31, 2), (32, 11), (27, 4), (29, 3), (30, 3), (28, 4), (31, 3), (32, 12), (29, 4),
    (30, 4), (31, 4),
)

def nn(a, b):
    return lax.dot_general(a, b, (((1,), (0,)), ((), ())), preferred_element_type=F32)


def nt(a, b):
    return lax.dot_general(a, b, (((1,), (1,)), ((), ())), preferred_element_type=F32)


def tn(a, b):
    return lax.dot_general(a, b, (((0,), (0,)), ((), ())), preferred_element_type=F32)


def rows_of(i, size):
    return pl.ds(pl.multiple_of(i * size, size), size)


def erf(x):
    return lax.erf(x)


def norm_rows(source, gain, shift, normed, inverse, entry, blocks=range(8)):
    for i in blocks:
        r = pl.ds(32 * i, 32)
        x = source[r, :]
        centred = x - jnp.mean(x, -1, keepdims=True)
        inv = lax.rsqrt(jnp.mean(centred * centred, -1, keepdims=True) + EPS)
        n = centred * inv
        normed[r, :] = n.astype(normed.dtype)
        inverse[r, :] = inv
        entry[r, :] = (n * gain[...] + shift[...]).astype(BF)


def norm_rows_back(grad_entry, normed, inverse, gain, grad, vec, gain_row, shift_row, blocks=range(8)):
    by_gain = jnp.zeros((8, WIDE), F32)
    by_shift = jnp.zeros((8, WIDE), F32)
    for i in blocks:
        r = pl.ds(32 * i, 32)
        d = grad_entry[r, :]
        n = normed[r, :].astype(F32)
        scaled = d * gain[...]
        first = jnp.mean(scaled, -1, keepdims=True)
        second = jnp.mean(scaled * n, -1, keepdims=True)
        grad[r, :] = grad[r, :] + inverse[r, :] * (scaled - first - n * second)
        dn = d * n
        by_gain = by_gain + jnp.sum(dn.reshape(4, 8, WIDE), 0)
        by_shift = by_shift + jnp.sum(d.reshape(4, 8, WIDE), 0)
    for row, part in ((gain_row, by_gain), (shift_row, by_shift)):
        vec[row : row + 1, :] = vec[row : row + 1, :] + jnp.sum(part, 0, keepdims=True)


def sum_columns(rows, count):
    total = jnp.zeros((8, WIDE), F32)
    for i in range(TOKENS // 32):
        for k in range(count):
            part = rows(k, pl.ds(32 * i, 32)).astype(F32)
            total = total + jnp.sum(part.reshape(4, 8, WIDE), 0)
    return jnp.sum(total, 0, keepdims=True)


def mega_kernel(
    lengths, tokens, cotangent, images, h_proj, h_out, h_exp, h_red, h_cq, h_ck, h_cv, h_co,
    again, ashift, qbias, vbias, obias, fgain, fshift, rbias, ebias, cgain, cshift, cqbias, cvbias, cobias,
    out_all,
    GG, WP, WO, WC, R0, R1, R2, R3,
    H, G, D, N1, N2, N3, I1, I2, I3, E, ET1, ET2, ET3,
    QKV, M, MT, QC, CT, SL, AT, PT, PC, IM, KV, B1, B2,
    HIN, MASK, YS, VS, VT, V0, V1, V2, V3, VY, VB, PV,
    wsem, psem, lsem, osem, ysend, yrecv, send_sem, recv_sem, vsend, vrecv, credit,
):
    section = lax.axis_index("section")
    dp = lax.axis_index("dp")
    one = section == 0
    two = section == 1
    bits = [lax.rem(lax.div(dp, 1 << k), 2) for k in range(4)]
    partners = [dp + (1 << k) * (1 - 2 * bits[k]) for k in range(4)]

    barrier = pltpu.get_barrier_semaphore()
    for partner in partners:
        pl.semaphore_signal(barrier, inc=1, device_id={"dp": partner}, device_id_type=MESH)
    pl.semaphore_signal(barrier, inc=1, device_id={"section": 1 - section}, device_id_type=MESH)

    def across(source, target, i):
        return pltpu.make_async_remote_copy(
            src_ref=source, dst_ref=target, send_sem=ysend.at[i], recv_sem=yrecv.at[i],
            device_id={"section": 1 - section}, device_id_type=MESH,
        )

    store_h = pltpu.make_async_copy(E, out_all.at[0:TOKENS], osem.at[0])
    late_h = pltpu.make_async_copy(M, out_all.at[0:TOKENS], osem.at[0])
    store_in = pltpu.make_async_copy(E, out_all.at[TOKENS : 2 * TOKENS], osem.at[1])
    images_a = across(images.at[0:2], IM.at[0:2, 0], 0)
    images_b = across(images.at[2:4], IM.at[2:4, 0], 1)
    send_h = across(E, HIN, 2)
    send_d = [across(E.at[0:128], HIN.at[0:128], 3), across(E.at[128:256], HIN.at[128:256], 10)]
    send_i = across(IM.at[:, 0], KV.at[:, 0, :, :WIDE], 4)

    def load(source, target, i):
        return pltpu.make_async_copy(source, target, wsem.at[i])

    own_images = load(images, IM.at[:, 1], 0)
    own_tokens = load(tokens, HIN, 15)
    own_cotangent = load(cotangent, B1, 16)
    loads = {
        "cross": [load(w, WC.at[i], 1 + i) for i, w in enumerate((h_cq, h_ck, h_cv, h_co))],
        "proj": [load(h_proj, WP, 5)],
        "out": [load(h_out, WO, 6)],
        "exp": [
            load(h_exp.at[:, :, :, :, :, pl.ds(WIDE * j, WIDE)], GG.at[12 + j], 7 + j)
            for j in range(4)
        ],
        "red": [load(h_red.at[j], GG.at[8 + j], 11 + j) for j in range(4)],
    }

    @pl.when(one)
    def _():
        own_tokens.start()

    small = [again, ashift, qbias, vbias, obias, fgain, fshift, rbias]
    small = [(v, PV.at[i : i + 1]) for i, v in enumerate(small)]
    small += [(ebias.at[:, pl.ds(WIDE * j, WIDE)], PV.at[8 + j : 9 + j]) for j in range(4)]
    small += [(v, PV.at[12 + i]) for i, v in enumerate((cgain, cshift, cqbias, cvbias, cobias))]
    small = [pltpu.make_async_copy(v, row, psem.at[i]) for i, (v, row) in enumerate(small)]

    @pl.when(two)
    def _():
        own_images.start()
        for i in (1, 2, 0, 3):
            loads["cross"][i].start()

    for name in ("proj", "out", "exp", "red"):
        for copy in loads[name]:
            copy.start()

    own_cotangent.start()
    for copy in small:
        copy.start()
    again, ashift, qbias, vbias, obias, fgain, fshift, rbias = (PV.at[i : i + 1] for i in range(8))
    cgain, cshift, cqbias, cvbias, cobias = (PV.at[i : i + 1] for i in range(12, 17))

    def arrived(name):
        for copy in loads[name]:
            copy.wait()

    VS[...] = jnp.zeros_like(VS)
    low_lane = lax.broadcasted_iota(jnp.int32, (1, 128), 1) < SLOT
    keep_low = low_lane.astype(F32).astype(BF)
    keep_high = jnp.logical_not(low_lane).astype(F32).astype(BF)

    def stacked(x):
        return jnp.concatenate([x * keep_low, x * keep_high], 0)

    def unstacked(x):
        half = x.shape[0] // 2
        return jnp.where(low_lane, x[:half], x[half:])

    eighth = jnp.asarray(0.125, BF)

    VB[...] = jnp.zeros_like(VB)
    VT[...] = jnp.zeros_like(VT)
    VY[...] = jnp.zeros_like(VY)
    pl.semaphore_wait(barrier, 5)

    @pl.when(one)
    def _():
        images_a.start()

    for pair in range(2):
        key = lax.broadcasted_iota(jnp.int32, (128, 256), 0)
        query = lax.rem(lax.broadcasted_iota(jnp.int32, (128, 256), 1), 128)
        first = key < SLOT
        length = jnp.where(first, lengths[2 * pair], lengths[2 * pair + 1] + SLOT)
        same = first == (query < SLOT)
        MASK[pair] = jnp.where(same & (key <= query) & (key < length), 1.0, 0.0)

    for copy in small:
        copy.wait()

    own_cotangent.wait()
    for c in range(CAPS):
        r = pl.ds(SLOT * c, SLOT)
        live = lax.broadcasted_iota(jnp.int32, (SLOT, 1), 0) < lengths[c]
        G[r, :] = jnp.where(live, B1[r, :].astype(F32), 0.0)
    B1[...] = G[...].astype(BF)

    def pair_rows(which, half):
        rows = IM[2 * which : 2 * which + 2, half].reshape(TOKENS, WIDE)
        keys = nn(rows, WC[1])
        KV[2 * which : 2 * which + 2, half, :, :WIDE] = keys.astype(BF).reshape(2, 128, WIDE)
        values = nn(rows, WC[2]) + cvbias[...]
        KV[2 * which : 2 * which + 2, half, :, WIDE:] = values.astype(BF).reshape(2, 128, WIDE)

    @pl.when(two)
    def _():
        for copy in loads["cross"]:
            copy.wait()
        own_images.wait()
        for which in range(2):
            pair_rows(which, 1)
        images_a.wait_recv()
        pair_rows(0, 0)
        arrived("red")
        for j in range(4):
            SL[j] = nt(B1[...], GG[8 + j].reshape(WIDE, WIDE)).astype(BF)
        send_h.wait_recv()
        H[...] = HIN[...].astype(F32)

    @pl.when(one)
    def _():
        own_tokens.wait()
        H[...] = HIN[...].astype(F32)

    @pl.when(one)
    def _():
        SL[...] = jnp.ones_like(SL)

    norm_rows(H, again, ashift, N1, I1, E)
    ET1[...] = E[...].T
    arrived("proj")
    QKV[0] = (nn(E[...], WP[:, 0:WIDE]) + qbias[...]).astype(BF)
    QKV[1] = nn(E[...], WP[:, WIDE : 2 * WIDE]).astype(BF)
    QKV[2] = (nn(E[...], WP[:, 2 * WIDE :]) + vbias[...]).astype(BF)

    def softmax_keys(scores):
        expo = jnp.exp(scores - jnp.max(scores, 0, keepdims=True))
        return expo * (1.0 / jnp.sum(expo, 0, keepdims=True))

    for hp in range(PAIRS):
        cols = pl.ds(128 * hp, 128)
        for pair in range(2):
            rows = pl.ds(pair * 128, 128)
            query = stacked(QKV[0, rows, cols] * eighth)
            scores = nt(QKV[1, rows, cols], query)
            scores = jnp.where(MASK[pair] > 0.0, scores, NEG)
            probs = softmax_keys(scores).astype(BF)
            PT[2 * hp + pair] = probs
            M[rows, cols] = unstacked(tn(probs, QKV[2, rows, cols])).astype(BF)

    MT[...] = M[...].T
    arrived("out")
    H[...] = H[...] + (nn(M[...], WO[...]) + obias[...])

    @pl.when(two)
    def _():
        norm_rows(H, cgain, cshift, N2, I2, E)
        ET2[...] = E[...].T
        QC[...] = (nn(E[...], WC[0]) + cqbias[...]).astype(BF)

    def cross_forward(half):
        for hp in range(PAIRS):
            cols = pl.ds(128 * hp, 128)
            vcols = pl.ds(WIDE + 128 * hp, 128)
            for c in (2 * half, 2 * half + 1):
                rows = pl.ds(c * SLOT, SLOT)
                query = stacked(QC[rows, cols] * eighth)
                keys = KV[c, :, :, cols].reshape(256, 128)
                probs = softmax_keys(nt(keys, query)).astype(BF)
                PC[4 * hp + c] = probs
                values = KV[c, :, :, vcols].reshape(256, 128)
                M[rows, cols] = unstacked(tn(probs, values)).astype(BF)
        rows = pl.ds(128 * half, 128)
        CT[:, rows] = M[rows, :].T
        H[rows, :] = H[rows, :] + (nn(M[rows, :], WC[3]) + cobias[...])

    def widen(j, rows):
        for t in range(3):
            cols = pl.ds(256 * t, 256)
            u = nn(E[rows, :], GG[12 + j, :, :, :, :, :, cols].reshape(WIDE, 256)) + PV[8 + j : 9 + j, cols]
            cdf = 0.5 * (1.0 + erf(u * 0.7071067811865476))
            M[rows, cols] = (u * cdf).astype(BF)
            slope = cdf + u * jnp.exp(-0.5 * u * u) * 0.3989422804014327
            SL[j, rows, cols] = (SL[j, rows, cols].astype(F32) * slope).astype(BF)
        AT[4 * j : 4 * j + 4, :, :, rows] = M[rows, :].T.reshape(4, 4, 48, rows.size)

    @pl.when(two)
    def _():
        for half in range(2):
            if half == 0:
                arrived("exp")
            else:
                images_b.wait_recv()
                pair_rows(1, 0)
            cross_forward(half)
            rows = pl.ds(128 * half, 128)
            norm_rows(H, fgain, fshift, N3, I3, E, range(4 * half, 4 * half + 4))
            ET3[:, rows] = E[rows, :].T
            for j in range(4):
                widen(j, rows)

    @pl.when(one)
    def _():
        norm_rows(H, fgain, fshift, N3, I3, E)
        ET3[...] = E[...].T
        arrived("exp")
        arrived("red")
        H[...] = H[...] + rbias[...]
        for j in range(4):
            widen(j, pl.ds(0, TOKENS))
            H[...] = H[...] + nn(M[...], GG[8 + j].reshape(WIDE, WIDE))
        E[...] = H[...].astype(BF)
        send_h.start()
        images_b.start()
        store_h.start()
        images_a.wait_send()
        send_h.wait_send()

    @pl.when(one)
    def _():
        store_h.wait()
        send_d[0].wait_recv()
        send_d[1].wait_recv()
        G[...] = G[...] + HIN[...].astype(F32)
        B1[...] = G[...].astype(BF)

    def images_out(source, what):
        for c in range(CAPS):
            target = out_all.at[2 * TOKENS + 128 * c : 2 * TOKENS + 128 * (c + 1)]
            getattr(pltpu.make_async_copy(source.at[c], target, osem.at[2 + c]), what)()

    def shard_place(c):
        return out_all.at[pl.ds(pl.multiple_of(4 * TOKENS + 48 * c, 16), 48)]

    def order(q):
        return (0, 2, 1, 3) if q in Z_FIRST else (0, 1, 2, 3)

    def chunk(q):
        return q // 2 if q < 16 else jnp.where(one, q // 2 + 4, q // 2)

    def half_of(q):
        return (slice(None), pl.ds(384 * (q % 2), 384))

    def where(q, k, bit):
        done, now = order(q)[:k], order(q)[k]
        places = [bits[a] if a in done else bit if a == now else slice(None) for a in (3, 2, 1, 0)]
        return (chunk(q), *places, *half_of(q))

    def landing(q, k):
        p = q // 2
        return (R0, R1, R2, R3)[k].at[(p % 8 if k == 0 else p, *([slice(None)] * (3 - k)), *half_of(q))]

    def exchange(q, k):
        axis = order(q)[k]
        return pltpu.make_async_remote_copy(
            src_ref=GG.at[where(q, k, 1 - bits[axis])], dst_ref=landing(q, k),
            send_sem=send_sem.at[q, k], recv_sem=recv_sem.at[q, k],
            device_id={"dp": partners[axis]}, device_id_type=MESH,
        )

    def begin(q, k):
        if k == 0 and q >= 16:
            pl.semaphore_wait(credit.at[q - 16], 1)
        exchange(q, k).start()

    def finish(q, k):
        exchange(q, k).wait()
        axis = order(q)[k]
        keep, term = GG.at[where(q, k, bits[axis])], landing(q, k)
        for place in itertools.product(range(2), repeat=3 - k):
            keep[place] = keep[place] + term[place]
        if k == 0 and q < 16:
            def give():
                pl.semaphore_signal(
                    credit.at[q], inc=1, device_id={"dp": partners[axis]}, device_id_type=MESH
                )
            give() if q < 8 else pl.when(two)(give)

    def shard(q):
        return GG.at[(chunk(q), *(bits[a] for a in (3, 2, 1, 0)), *half_of(q))]

    def shard_out(q):
        return pltpu.make_async_copy(shard(q), shard_place(chunk(q)).at[half_of(q)], lsem.at[q])

    def shard_across(q):
        return across(shard(q), YS.at[(q // 2 - 8, *half_of(q))], 11 + q - 16)

    def advance(q, k):
        finish(q, k - 1)
        if k < 4:
            begin(q, k)
        else:
            shard_out(q).start()
            if 16 <= q < 24:
                pl.when(two)(lambda: shard_across(q).start())

    def go(q, k):
        if q >= 24:
            pl.when(two)(lambda: advance(q, k) if k else begin(q, 0))
        elif k:
            advance(q, k)
        else:
            begin(q, 0)

    def sum_part(k, bit):
        return VT.at[tuple(bits[a] if a < k else bit if a == k else slice(None) for a in (3, 2, 1, 0))]

    def sum_copy(k):
        return pltpu.make_async_remote_copy(
            src_ref=sum_part(k, 1 - bits[k]), dst_ref=(V0, V1, V2, V3)[k],
            send_sem=vsend.at[k], recv_sem=vrecv.at[k],
            device_id={"dp": partners[k]}, device_id_type=MESH,
        )

    def sum_add(k):
        sum_copy(k).wait()
        keep, term = sum_part(k, bits[k]), (V0, V1, V2, V3)[k]
        for place in itertools.product(range(2), repeat=3 - k):
            keep[place] = keep[place] + term[place]

    def sum_shards():
        for d in range(16):
            place = ((d >> 3) & 1, (d >> 2) & 1, (d >> 1) & 1, d & 1)
            VT[(*place, slice(None), slice(0, 48))] = VS[:, 48 * d : 48 * (d + 1)]
            for i in range(4):
                first = 192 * (d % 4) + 48 * i
                VT[(*place, slice(8 + i, 9 + i), slice(0, 48))] = VS[8 + d // 4 : 9 + d // 4, first : first + 48]

    def sum_result():
        return VT.at[tuple(bits[a] for a in (3, 2, 1, 0))]

    def weight_gradient(c, left, right):
        for t in range(3):
            part = nn(left, right(pl.ds(256 * t, 256)))
            GG[c, :, :, :, :, :, pl.ds(256 * t, 256)] = part.astype(BF).reshape(LEAD + (48, 256))


    def reduce_chunk(i):
        weight_gradient(i, AT[:, i].reshape(WIDE, TOKENS), lambda t: B1[:, t])
        go(2 * i, 0)
        go(2 * i + 1, 0)

    reduce_chunk(0)
    reduce_chunk(1)


    @pl.when(one)
    def _():
        for j in range(4):
            for i in range(2):
                r = pl.ds(128 * i, 128)
                da = nt(B1[r, :], GG[8 + j].reshape(WIDE, WIDE))
                SL[j, r, :] = (da * SL[j, r, :].astype(F32)).astype(BF)

    total = nt(SL[0], GG[12].reshape(WIDE, WIDE))
    for j in range(1, 4):
        total = total + nt(SL[j], GG[12 + j].reshape(WIDE, WIDE))
    D[...] = total

    for q in range(4):
        go(q, 1)
    reduce_chunk(2)
    reduce_chunk(3)

    norm_rows_back(D, N3, I3, fgain, G, VS, 5, 6)

    @pl.when(one)
    def _():
        for q in range(4, 8):
            go(q, 1)

    def cross_back(half):
        rows = pl.ds(128 * half, 128)
        B2[rows, :] = G[rows, :].astype(BF)
        E[rows, :] = nt(B2[rows, :], WC[3]).astype(BF)
        for hp in range(PAIRS):
            cols = pl.ds(128 * hp, 128)
            vcols = pl.ds(WIDE + 128 * hp, 128)
            for c in (2 * half, 2 * half + 1):
                own = pl.ds(c * SLOT, SLOT)
                query = stacked(QC[own, cols] * eighth)
                grad = stacked(E[own, cols])
                keys = KV[c, :, :, cols].reshape(256, 128)
                values = KV[c, :, :, vcols].reshape(256, 128)
                probs = PC[4 * hp + c]
                wide = probs.astype(F32)
                dprobs = nt(values, grad)
                dscores = (wide * (dprobs - jnp.sum(wide * dprobs, 0, keepdims=True))).astype(BF)
                KV[c, :, :, cols] = nn(dscores, query).astype(BF).reshape(2, 128, 128)
                KV[c, :, :, vcols] = nn(probs, grad).astype(BF).reshape(2, 128, 128)
                QC[own, cols] = (unstacked(tn(dscores, keys)) * 0.125).astype(BF)
        D[rows, :] = nt(QC[rows, :], WC[0])
        norm_rows_back(D, N2, I2, cgain, G, VS, 12, 13, range(4 * half, 4 * half + 4))

    def self_back(pairs):
        rows = pl.ds(128 * pairs[0], 128 * len(pairs))
        HIN[rows, :] = G[rows, :].astype(BF)
        E[rows, :] = nt(HIN[rows, :], WO[...]).astype(BF)
        for hp in range(PAIRS):
            cols = pl.ds(128 * hp, 128)
            for pair in pairs:
                own = pl.ds(pair * 128, 128)
                query = stacked(QKV[0, own, cols] * eighth)
                grad = stacked(E[own, cols])
                keys = QKV[1, own, cols]
                probs = PT[2 * hp + pair]
                wide = probs.astype(F32)
                dprobs = nt(QKV[2, own, cols], grad)
                dscores = (wide * (dprobs - jnp.sum(wide * dprobs, 0, keepdims=True))).astype(BF)
                QKV[1, own, cols] = nn(dscores, query).astype(BF)
                QKV[2, own, cols] = nn(probs, grad).astype(BF)
                QKV[0, own, cols] = (unstacked(tn(dscores, keys)) * 0.125).astype(BF)
        total = nt(QKV[0, rows, :], WP[:, 0:WIDE])
        total = total + nt(QKV[1, rows, :], WP[:, WIDE : 2 * WIDE])
        D[rows, :] = total + nt(QKV[2, rows, :], WP[:, 2 * WIDE :])
        norm_rows_back(D, N1, I1, again, G, VS, 0, 1, range(4 * pairs[0], 4 * pairs[-1] + 4))
        E[rows, :] = G[rows, :].astype(BF)

    @pl.when(two)
    def _():
        for half in range(2):
            cross_back(half)
            if half == 0:
                for q in range(4, 8):
                    go(q, 1)
            self_back((half,))
            send_d[half].start()

    @pl.when(one)
    def _():
        self_back((0, 1))

    store_in.start()

    def late_sums():
        for j in range(4):
            VS[8 + j : 9 + j, :] = sum_columns(lambda k, r: SL[j, r, :], 1)
        VS[7:8, :] = sum_columns(lambda k, r: B1[r, :], 1)
        VS[2:3, :] = sum_columns(lambda k, r: QKV[0, r, :], 1)
        VS[3:4, :] = sum_columns(lambda k, r: QKV[2, r, :], 1)
        VS[4:5, :] = sum_columns(lambda k, r: HIN[r, :], 1)

        @pl.when(two)
        def _():
            VS[14:15, :] = sum_columns(lambda k, r: QC[r, :], 1)
            VS[16:17, :] = sum_columns(lambda k, r: B2[r, :], 1)
            VS[15:16, :] = sum_columns(
                lambda k, r: KV[k, :, pl.ds(r.start // 2, 16), WIDE:].reshape(32, WIDE), 4
            )

    def late_output():
        @pl.when(two)
        def _():
            H[...] = H[...] + rbias[...]
            for j in range(4):
                a = AT[4 * j : 4 * j + 4].reshape(WIDE, TOKENS)
                H[...] = H[...] + tn(a, GG[8 + j].reshape(WIDE, WIDE))
            M[...] = H[...].astype(BF)
            late_h.start()

    def turn_images():
        @pl.when(two)
        def _():
            for c in range(CAPS):
                AT[4 * c : 4 * c + 4] = IM[c].reshape(256, WIDE).T.reshape(4, 4, 48, TOKENS)

    def image_gradient():
        @pl.when(two)
        def _():
            for c in range(CAPS):
                part = nt(KV[c, :, :, :WIDE].reshape(256, WIDE), WC[1])
                part = part + nt(KV[c, :, :, WIDE:].reshape(256, WIDE), WC[2])
                IM[c] = part.astype(BF).reshape(2, 128, WIDE)
            send_i.start()
            images_out(IM.at[:, 1], "start")

    def image_pairs(j):
        for t in range(3):
            cols = pl.ds(WIDE * j + 256 * t, 256)
            part = sum(
                nn(AT[4 * c : 4 * c + 4].reshape(WIDE, TOKENS), KV[c, :, :, cols].reshape(256, 256))
                for c in range(CAPS)
            )
            GG[9 + j, :, :, :, :, :, pl.ds(256 * t, 256)] = part.astype(BF).reshape(LEAD + (48, 256))

    def self_chunk(i):
        if i < 3:
            weight_gradient(12 + i, ET1[...], lambda t: QKV[i, :, t])
        else:
            weight_gradient(15, MT[...], lambda t: HIN[:, t])

    def cross_chunk(i):
        if i == 0:
            weight_gradient(8, ET2[...], lambda t: QC[:, t])
        elif i < 3:
            image_pairs(i - 1)
        else:
            weight_gradient(11, CT[...], lambda t: B2[:, t])

    def compute(p):
        if p < 8:
            weight_gradient(p, ET3[...], lambda t: SL[p - 4, :, t])
        elif p < 12:
            pl.when(one)(lambda: self_chunk(p - 8))
            pl.when(two)(lambda: cross_chunk(p - 8))
        else:
            pl.when(two)(lambda: self_chunk(p - 12))

    def sums(k):
        if k > 0:
            sum_add(k - 1)
        else:
            sum_shards()
        if k < 4:
            sum_copy(k).start()
        else:
            pl.when(two)(lambda: across(sum_result(), VY, 5).start())

    def images_end():
        @pl.when(one)
        def _():
            images_b.wait_send()
            send_i.wait_recv()
            images_out(KV.at[:, 0, :, :WIDE], "start")

    def sums_end():
        pl.when(one)(lambda: across(sum_result(), VY, 5).wait_recv())
        crossed = lax.broadcasted_iota(jnp.int32, (24, 128), 0) >= 12
        final = jnp.where(crossed & one, VY[...], sum_result()[...])
        high = final.astype(BF)
        VB[0:24, 0:128] = high
        VB[24:48, 0:128] = (final - high.astype(F32)).astype(BF)
        store_v.start()

    def shards_end():
        @pl.when(one)
        def _():
            for i in range(4):
                for q in (16 + 2 * i, 17 + 2 * i):
                    across(shard(q), YS.at[(i, *half_of(q))], 11 + q - 16).wait_recv()
                shard_copies[i].start()

    store_v = pltpu.make_async_copy(VB, out_all.at[7 * TOKENS : 7 * TOKENS + 48], osem.at[6])
    shard_copies = [pltpu.make_async_copy(YS.at[i], shard_place(8 + i), lsem.at[24 + i]) for i in range(4)]
    work = {0: late_sums, 1: late_output, 2: image_gradient, 4: turn_images, 10: images_end, 11: sums_end, 12: shards_end}
    work.update({5 + k: functools.partial(sums, k) for k in range(5)})

    for q, k in EVENTS:
        if q == 32:
            work[k]()
            continue
        if k == 0 and q % 2 == 0:
            compute(q // 2)
        go(q, k)

    @pl.when(two)
    def _():
        across(sum_result(), VY, 5).wait_send()
        images_out(IM.at[:, 1], "wait")
        send_d[0].wait_send()
        send_d[1].wait_send()
        send_i.wait_send()
        late_h.wait()
        for q in range(16, 24):
            shard_across(q).wait_send()
        for q in range(24, 32):
            shard_out(q).wait()

    @pl.when(one)
    def _():
        for copy in shard_copies:
            copy.wait()
        images_out(KV.at[:, 0, :, :WIDE], "wait")

    store_in.wait()
    store_v.wait()
    for q in range(24):
        shard_out(q).wait()


def mega(args):
    (
        tokens, images, lengths, cotangent, again, ashift, proj, qb, vb, wo, ob, fg, fs, we, eb, wr, rb,
        cg, cs, cq, cqb, ck, cv, cvb, co, cob,
    ) = args
    operands = (
        lengths, tokens.reshape(TOKENS, WIDE), cotangent.reshape(TOKENS, WIDE), images,
        proj[0], wo[0], we.reshape(LEAD + (48, 4 * WIDE)), wr.reshape((4,) + LEAD + (48, WIDE)), cq, ck, cv, co,
        again, ashift, qb, vb, ob, fg, fs, rb, eb, cg, cs, cqb, cvb, cob,
    )
    hbm = pl.BlockSpec(memory_space=pl.ANY)
    dma = pltpu.SemaphoreType.DMA
    big = (TOKENS, WIDE)
    turned = (WIDE, TOKENS)
    b = lambda *shape: pltpu.VMEM(shape, BF)
    f = lambda *shape: pltpu.VMEM(shape, F32)
    return pl.pallas_call(
        mega_kernel,
        out_shape=jax.ShapeDtypeStruct((7 * TOKENS + 48, WIDE), BF),
        in_specs=[pl.BlockSpec(memory_space=pltpu.SMEM)] + [hbm] * (len(operands) - 1),
        out_specs=hbm,
        scratch_shapes=[
            b(16, *LEAD, 48, WIDE), b(WIDE, 3 * WIDE), b(WIDE, WIDE), b(4, WIDE, WIDE),
            b(8, 2, 2, 2, 48, WIDE), b(16, 2, 2, 48, WIDE), b(16, 2, 48, WIDE), b(16, 48, WIDE),
            f(*big), f(*big), f(*big), b(*big), b(*big), b(*big), f(TOKENS, 1), f(TOKENS, 1), f(TOKENS, 1),
            b(*big), b(*turned), b(*turned), b(*turned),
            b(3, *big), b(*big), b(*turned), b(*big), b(*turned), b(4, *big),
            b(16, 4, 48, TOKENS), b(12, 128, 256), b(24, 256, 128), b(CAPS, 2, 128, WIDE),
            b(CAPS, 2, 128, 2 * WIDE), b(*big), b(*big),
            b(*big), f(2, 128, 256), b(4, 48, WIDE), f(24, WIDE), f(*LEAD, 24, 128), f(2, 2, 2, 24, 128), f(2, 2, 24, 128),
            f(2, 24, 128), f(24, 128), f(24, 128), b(48, WIDE), f(24, WIDE),
            dma((17,)), dma((17,)), dma((32,)), dma((7,)), dma((19,)), dma((19,)),
            dma((32, 4)), dma((32, 4)), dma((4,)), dma((4,)), pltpu.SemaphoreType.REGULAR((16,)),
        ],
        compiler_params=pltpu.CompilerParams(
            collective_id=0, has_side_effects=True, vmem_limit_bytes=63 * 2**20
        ),
        name="layers",
    )(*operands)


def finish_kernel(every, *outs):
    (
        o_h, o_in, o_img, o_ag, o_as, o_proj, o_qb, o_vb, o_wo, o_ob, o_fg, o_fs, o_we, o_eb, o_wr, o_rb,
        o_cg, o_cs, o_cq, o_cqb, o_ck, o_cv, o_cvb, o_co, o_cob,
    ) = outs
    o_h[...] = every[0:TOKENS, :].reshape(o_h.shape)
    o_in[...] = every[TOKENS : 2 * TOKENS, :].astype(F32).reshape(o_in.shape)
    o_img[...] = every[2 * TOKENS : 4 * TOKENS, :].astype(F32).reshape(o_img.shape)
    shards = [every[4 * TOKENS + 48 * j : 4 * TOKENS + 48 * (j + 1), :].astype(F32) for j in range(16)]
    vec = every[7 * TOKENS : 7 * TOKENS + 48, 0:128].astype(F32)
    vec = vec[:24] + vec[24:]
    for j in range(3):
        o_proj[0, :, WIDE * j : WIDE * (j + 1)] = shards[12 + j]
    o_wo[0] = shards[15]
    for j in range(4):
        o_we[0, :, WIDE * j : WIDE * (j + 1)] = shards[4 + j]
        o_wr[0, 48 * j : 48 * (j + 1), :] = shards[j]
    for j, out in enumerate((o_cq, o_ck, o_cv, o_co)):
        out[...] = shards[8 + j]
    places = (
        (o_ag, 0), (o_as, 1), (o_qb, 2), (o_vb, 3), (o_ob, 4), (o_fg, 5), (o_fs, 6), (o_rb, 7),
        (o_cg, 12), (o_cs, 13), (o_cqb, 14), (o_cvb, 15), (o_cob, 16),
    )
    for out, i in places:
        out[...] = vec[i : i + 1, :48]
    for i in range(4):
        o_eb[:, 48 * i : 48 * (i + 1)] = vec[8 + i : 9 + i, :48]


def finish_outputs(every):
    vm = pl.BlockSpec(memory_space=pltpu.VMEM)
    small = (1, 48)
    shapes = [
        (1, CAPS, SLOT, WIDE), (1, CAPS, SLOT, WIDE), (CAPS, 128, WIDE),
        small, small, (1, 48, 3 * WIDE), small, small, (1, 48, WIDE), small, small, small,
        (1, 48, 4 * WIDE), (1, 192), (1, 192, WIDE), small,
        small, small, (48, WIDE), small, (48, WIDE), (48, WIDE), small, (48, WIDE), small,
    ]
    outs = pl.pallas_call(
        finish_kernel,
        out_shape=[jax.ShapeDtypeStruct(x, BF if i == 0 else F32) for i, x in enumerate(shapes)],
        in_specs=[vm],
        out_specs=[vm] * 25,
        compiler_params=pltpu.CompilerParams(vmem_limit_bytes=40 * 2**20),
        name="finish",
    )(every)
    outs = list(outs)
    for i in (16, 17, 19, 22, 24):
        outs[i] = outs[i].reshape(-1)
    return tuple(outs)


def body(
    tokens,
    images,
    lengths,
    cotangent,
    attend_gain,
    attend_shift,
    projections,
    query_bias,
    value_bias,
    output_weight,
    output_bias,
    feed_gain,
    feed_shift,
    expand_weight,
    expand_bias,
    reduce_weight,
    reduce_bias,
    cross_gain,
    cross_shift,
    cross_query,
    cross_query_bias,
    cross_key,
    cross_value,
    cross_value_bias,
    cross_out,
    cross_out_bias,
):
    layer = tuple(
        (
            weight[0]
            for weight in (
                attend_gain,
                attend_shift,
                projections,
                query_bias,
                value_bias,
                output_weight,
                output_bias,
                feed_gain,
                feed_shift,
                expand_weight,
                expand_bias,
                reduce_weight,
                reduce_bias,
            )
        )
    )
    cross = (
        cross_gain,
        cross_shift,
        cross_query,
        cross_query_bias,
        cross_key,
        cross_value,
        cross_value_bias,
        cross_out,
        cross_out_bias,
    )
    pair_weight = jnp.concatenate([cross_key, cross_value], 1)
    pair_bias = jnp.concatenate([jnp.zeros_like(cross_value_bias), cross_value_bias], 0)
    section_index = lax.axis_index("section")
    is_two = section_index == 1
    block = MB_CAPS
    half = images.shape[1]
    slots = tokens.shape[1]
    width = tokens.shape[2]
    positions = jnp.arange(slots, dtype=jnp.int32)
    causal = positions[None, :] <= positions[:, None]
    zero_cross = tuple((jnp.zeros(weight.shape, jnp.float32) for weight in cross))

    def image_project(image_rows):
        return (product(image_rows, pair_weight) + pair_bias).astype(jnp.bfloat16)

    def image_back(image_rows, dpairs):
        dimages = back_product(dpairs, pair_weight)
        pair_grad = weight_product(image_rows, dpairs)
        return (
            dimages,
            (pair_grad[:, :width], pair_grad[:, width:], column_sum(dpairs[..., width:])),
        )

    def cross_yes(hidden, image_data):
        pairs = image_project(image_data)
        after, saved = cross_forward(hidden, pairs, cross)
        return (after, saved, pairs)

    def cross_no(hidden, image_data):
        saved = (
            jnp.zeros((block, slots, width), jnp.float32),
            jnp.zeros((block, slots, 1), jnp.float32),
            jnp.zeros((block, slots, width), jnp.bfloat16),
            jnp.zeros((block, slots, width), jnp.bfloat16),
            jnp.zeros((block, slots, width), jnp.bfloat16),
            jnp.zeros((block, HEADS, slots, 1), jnp.float32),
        )
        return (hidden, saved, jnp.zeros((block, 2 * half, 2 * width), jnp.bfloat16))

    def back_yes(grad, saved, pairs, image_data):
        dgrad, parts, dpairs = cross_back(grad, saved, pairs, cross)
        dimages, image_terms = image_back(image_data, dpairs)
        return (dgrad, parts[:4] + image_terms + parts[4:], dimages)

    def back_no(grad, saved, pairs, image_data):
        return (grad, zero_cross, jnp.zeros((block, 2 * half, width), jnp.float32))

    received = jnp.zeros((block, slots, width), jnp.bfloat16)
    arriving = jnp.zeros((block, half, width), jnp.bfloat16)
    finished = jnp.zeros(tokens.shape, jnp.bfloat16)
    kept = []
    for tick in range(MICRO + 1):
        index = jnp.clip(tick - section_index, 0, MICRO - 1)
        start = index * block
        live = positions[None, :] < lax.dynamic_slice_in_dim(lengths, start, block, 0)[:, None]
        mask = live[:, None, :] & causal[None]
        own_tokens = lax.dynamic_slice_in_dim(tokens, start, block, 0)
        own_images = lax.dynamic_slice_in_dim(images, start, block, 0)
        hidden = jnp.where(is_two, received, own_tokens).astype(jnp.float32)
        after_self, self_saved = self_forward(hidden, layer, mask)
        image_data = jnp.concatenate([arriving, own_images], 1)
        after_cross, cross_saved, pairs = lax.cond(
            is_two, cross_yes, cross_no, after_self, image_data
        )
        final, feed_saved = feed_forward(after_cross, layer)
        result = final.astype(jnp.bfloat16)
        finished = lax.dynamic_update_slice_in_dim(finished, result, start, 0)
        kept.append((mask, live, self_saved, cross_saved, feed_saved, pairs, image_data))
        if tick < MICRO:
            received = shifted(result, "section", 1)
            arriving = shifted(own_images, "section", 1)
    layer_sums = tuple((jnp.zeros(weight.shape, jnp.float32) for weight in layer))
    cross_sums = zero_cross
    input_grads = jnp.zeros(tokens.shape, jnp.float32)
    image_grads = jnp.zeros(images.shape, jnp.float32)
    returning = jnp.zeros((block, slots, width), jnp.bfloat16)
    coming = jnp.zeros((block, half, width), jnp.float32)
    for turn in range(MICRO + 1):
        tick = MICRO - turn
        offset = tick - section_index
        index = jnp.clip(offset, 0, MICRO - 1)
        start = index * block
        valid = ((offset >= 0) & (offset < MICRO)).astype(jnp.float32)
        mask, live, self_saved, cross_saved, feed_saved, pairs, image_data = kept[tick]
        own_images = lax.dynamic_slice_in_dim(images, start, block, 0)
        seed_grad = lax.dynamic_slice_in_dim(cotangent[0], start, block, 0).astype(
            jnp.float32
        ) * live[..., None].astype(jnp.float32)
        grad = seed_grad + returning.astype(jnp.float32)
        grad, feed_grads = feed_back(grad, feed_saved, layer)
        grad, cross_grads, image_part = lax.cond(
            is_two, back_yes, back_no, grad, cross_saved, pairs, image_data
        )
        grad, self_grads = self_back(grad, self_saved, layer, mask)
        layer_sums = tuple(
            (total + valid * part for total, part in zip(layer_sums, self_grads + feed_grads))
        )
        cross_sums = tuple((total + valid * part for total, part in zip(cross_sums, cross_grads)))
        sent = grad.astype(jnp.bfloat16)
        stored = jnp.where(is_two, sent.astype(jnp.float32), grad)
        input_grads = jnp.where(
            valid > 0, lax.dynamic_update_slice_in_dim(input_grads, stored, start, 0), input_grads
        )
        own_dimages = jnp.where(is_two, image_part[:, half:], coming)
        image_grads = jnp.where(
            valid > 0,
            lax.dynamic_update_slice_in_dim(image_grads, own_dimages, start, 0),
            image_grads,
        )
        if turn < MICRO:
            returning = shifted(sent, "section", -1)
            coming = shifted(image_part[:, :half].astype(jnp.bfloat16), "section", -1).astype(
                jnp.float32
            )
    shared = lax.psum_scatter(
        tuple((total[None] for total in layer_sums)), "dp", scatter_dimension=1, tiled=True
    )
    scattered = lax.psum_scatter(cross_sums, "dp", scatter_dimension=0, tiled=True)
    crossed = jax.tree.map(
        lambda part: part.astype(jnp.float32), lax.psum(for_sending(tuple(scattered)), "section")
    )
    return (finished[None], input_grads[None], image_grads) + tuple(shared) + tuple(crossed)


def one_kernel(*args):
    return finish_outputs(mega(args))


def solution(mesh):
    placed = (
        P("dp", None, None),
        P("dp", "section", None),
        P("dp"),
        P("section", "dp", None, None),
        P("section", None),
        P("section", None),
        P("section", None, None),
        P("section", None),
        P("section", None),
        P("section", None, None),
        P("section", None),
        P("section", None),
        P("section", None),
        P("section", None, None),
        P("section", None),
        P("section", None, None),
        P("section", None),
        P(),
        P(),
        P(),
        P(),
        P(),
        P(),
        P(),
        P(),
        P(),
    )
    return jax.shard_map(
        one_kernel if mesh.shape["dp"] == 16 else body,
        mesh=mesh,
        in_specs=placed,
        out_specs=(
            P("section", "dp", None, None),
            P("section", "dp", None, None),
            P("dp", "section", None),
            P("section", "dp"),
            P("section", "dp"),
            P("section", "dp", None),
            P("section", "dp"),
            P("section", "dp"),
            P("section", "dp", None),
            P("section", "dp"),
            P("section", "dp"),
            P("section", "dp"),
            P("section", "dp", None),
            P("section", "dp"),
            P("section", "dp", None),
            P("section", "dp"),
            P("dp"),
            P("dp"),
            P("dp", None),
            P("dp"),
            P("dp", None),
            P("dp", None),
            P("dp"),
            P("dp", None),
            P("dp"),
        ),
        check_vma=False,
    )
```
